128 devices in a mesh: dp: 4 (over x_lo, core), seq: 32 (over y, x_hi, z).
Axes of the slice: x: 4 (x_hi: 2, x_lo: 2; x = x_hi * 2 + x_lo), y: 4, z: 4, core: 2. Of those that a mesh axis runs over, the one named last changes fastest.
Arguments:
- hist_x: bfloat16 [4, 4096, 1024], P('dp', 'seq'), may hold values from -6 to 6
- hist_cot: bfloat16 [4, 4096, 1024], P('dp', 'seq'), may hold values from -6 to 6
- cand_x: bfloat16 [32768, 1024], P(('dp', 'seq')), may hold values from -6 to 6
- cand_loop: int32 [32768, 1], P(('dp', 'seq')), may hold values from 0 to 3; in each aligned block of 256 rows (0 to 255, 256 to 511, ...) at most 128 rows name the same one
- hist_len: int32 [4], P('dp'), may hold values from 512 to 4096, as said below
- w_proj: bfloat16 [1024, 2048], replicated, may hold values from -0.1875 to 0.1875
- w_out: bfloat16 [512, 1024], replicated, may hold values from -0.25 to 0.25
Outputs:
- hist_out: bfloat16 [4, 4096, 1024], P('dp', 'seq')
- hist_grad: bfloat16 [4, 4096, 1024], P('dp', 'seq')
- cand_out: bfloat16 [32768, 1024], P(('dp', 'seq'))
The draws below stay inside these ranges and needn't reach their ends.
Inputs may be any that keep to these rules, and one draw needn't show every extreme that they name: `cand_loop`: among the 256 rows of one device (aligned blocks) no user is named more than 128 times, and some block names one user exactly 128 times. `hist_len`: one user's history fills all 4096 events.
All inputs are finite; a program needn't handle non-finite values.
Results may differ from the reference program's by a relative error of at most 0.022.
Values may be sent and summed in bfloat16 or wider, within the bound.
No kernel may reach another device: no remote copies, remote signals or barrier semaphores. Data moves between devices by JAX's collectives and lax.ppermute only.
A program may use at most 64 MiB of HBM per device.

```python
import math
import jax
import jax.numpy as jnp
import numpy as np
from jax import lax

D = 1024
HEADS = 4
HS = 128
CAND_DEV = 256
CAP = 128
HA = 512
SEQ = 4096
USERS = 4
CANDS = 32768
N_DP = 4


def draw_hist_len(key, part):
    key = jax.random.fold_in(key, 11)
    draw_key, pick_key = jax.random.split(key)
    lengths = jax.random.randint(draw_key, (USERS,), SEQ // 8, SEQ + 1)
    full_user = jax.random.randint(pick_key, (), 0, USERS)
    return jnp.where(jnp.arange(USERS) == full_user, SEQ, lengths).astype(jnp.int32)


def level_of(stream_key, dims, cuts, least, top_value):
    def one(position, blocks):
        draws = jax.random.uniform(jax.random.fold_in(jax.random.fold_in(stream_key, 6), position), (blocks,), jnp.float32, least / len(cuts), top_value / len(cuts))
        return jnp.repeat(jnp.exp(draws), dims[position] // blocks).reshape((-1,) + (1,) * (len(dims) - position - 1))

    loudness = one(*cuts[0])
    for cut in cuts[1:]:
        loudness = loudness * one(*cut)
    return loudness


def assign_block(key, own, number, rows, count, top, reach, lean):
    ranking = jax.random.permutation(key, count)
    packed, usual = load_shares(count, rows * top, reach, lean, True), load_shares(count, rows * top, reach, lean, False)
    places = jnp.arange(count)

    def named(sizes, turn):
        used = int((sizes > 0).sum())
        fixed = max(1, used // 4)
        moved = fixed + (places - fixed + turn * (used - fixed)) % max(1, count - fixed)
        return jnp.zeros((count,), jnp.int32).at[ranking[jnp.where(places < fixed, places, moved)]].set(jnp.asarray(sizes, jnp.int32))

    sizes = jnp.where(number % 4 == 0, named(packed, number // 4), named(usual, number - number // 4 - 1))
    mixed = jax.random.permutation(jax.random.fold_in(own, 3), count)
    giver, receiver = mixed[0:count // 2 * 2:2], mixed[1:count // 2 * 2:2]
    slack = jnp.minimum(sizes[giver] - 1, reach - sizes[receiver]) // 2
    slack = jnp.where((giver == ranking[0]) | (receiver == ranking[0]) | (sizes[receiver] == 0), 0, jnp.maximum(slack, 0))
    moved = jax.random.randint(jax.random.fold_in(own, 4), (count // 2,), 0, 1 << 20) % (slack + 1)
    sizes = sizes.at[giver].add(-moved).at[receiver].add(moved)
    members = jnp.searchsorted(jnp.cumsum(sizes), jnp.arange(rows * top), side="right").astype(jnp.int32)
    listing = members.reshape(top, rows).T
    listing = listing[jax.random.permutation(jax.random.fold_in(own, 1), rows)]
    turn = jax.random.randint(jax.random.fold_in(own, 2), (rows, 1), 0, top)
    return jnp.take_along_axis(listing, (jnp.arange(top)[None, :] + turn) % top, axis=1)


def load_shares(count, total, bound, skew, full):
    loads = [(1 << 20) // math.isqrt(grade ** skew) + 1 for grade in range(1, count + 1)]
    largest = bound if full else min(bound, max(-(-total // count), total * loads[0] // sum(loads)))
    least = 1 if total - largest >= count - 1 else 0
    holding, rest = [largest] + [least] * (count - 1), total - largest - least * (count - 1)
    while rest > 0:
        movable = [i for i in range(1, count) if holding[i] < largest] or [i for i in range(1, count) if holding[i] < bound]
        pool, left = sum([loads[i] for i in movable]), rest
        for i in movable:
            more = min(bound - holding[i], max(1, left * loads[i] // pool), rest)
            holding[i] = holding[i] + more
            rest = rest - more
    return np.array(holding)


def centred(own_key, extent, scale, bound, pieces=(), kind=jnp.bfloat16):
    array = jax.random.normal(own_key, extent, jnp.float32) * scale
    if len(pieces) > 0:
        array = level_of(own_key, extent, pieces, -0.22, 0.18) * array
    return jnp.clip(array, min=-bound, max=bound).astype(kind)


def setup_inputs(seed: int = 0) -> dict:
    seeds = jax.random.split(jax.random.key(seed), 8)
    hist_x = centred(seeds[0], (USERS, SEQ, D), 1.0, 6.0, ((0, 4), (1, 32)))
    hist_cot = centred(seeds[1], (USERS, SEQ, D), 1.0, 6.0, ((0, 4), (1, 32)))
    cand_x = centred(seeds[2], (CANDS, D), 1.0, 6.0, ((0, 128),))
    cand_loop_keys = jax.random.split(jax.random.fold_in(seeds[3], 1), CANDS // CAND_DEV)
    cand_loop_turns = jax.random.permutation(jax.random.fold_in(seeds[3], 3), CANDS // CAND_DEV)
    cand_loop = jax.vmap(lambda own, number: assign_block(jax.random.fold_in(seeds[3], 2), own, number, CAND_DEV, N_DP, 1, CAP, 2))(cand_loop_keys, cand_loop_turns).reshape((CANDS, 1))
    hist_len = draw_hist_len(jax.random.fold_in(seeds[7], 71), 0)
    w_proj = centred(seeds[5], (D, 4 * HA), D ** -0.5, 0.1875)
    w_out = centred(seeds[6], (HA, D), HA ** -0.5, 0.25)
    return {"hist_x": hist_x, "hist_cot": hist_cot, "cand_x": cand_x, "cand_loop": cand_loop, "hist_len": hist_len, "w_proj": w_proj, "w_out": w_out}


layer_eps = 1e-05

def normalize(values):
    center = values - lax.optimization_barrier(jnp.mean(values, axis=-1, keepdims=True))
    spread = lax.rsqrt(lax.optimization_barrier(jnp.mean(center * center, axis=-1, keepdims=True)) + layer_eps)
    return (center * spread, spread)

def norm_back(grad_in, normed, spread):
    return spread * (grad_in - lax.optimization_barrier(jnp.mean(grad_in, axis=-1, keepdims=True)) - normed * lax.optimization_barrier(jnp.mean(grad_in * normed, axis=-1, keepdims=True)))

def silu_slope(pre_act):
    sigmoid_gate = jax.nn.sigmoid(pre_act)
    return sigmoid_gate * (1.0 + pre_act * (1.0 - sigmoid_gate))

def rounded(values):
    return lax.optimization_barrier(values.astype(jnp.bfloat16)).astype(jnp.float32)

def attend(queries, key_block, value_block, weight):
    score_scale = HS ** (-0.5)
    scores = jnp.einsum('rhe,khe->hrk', queries.astype(jnp.float32), key_block.astype(jnp.float32)) * score_scale
    probabilities = rounded(scores * jax.nn.sigmoid(scores) * weight[None])
    return jnp.einsum('hrk,khe->rhe', probabilities, value_block.astype(jnp.float32))

def attend_grads(queries, grad_att, key_block, value_block, weight):
    score_scale = HS ** (-0.5)
    query_f = queries.astype(jnp.float32)
    grad_f = grad_att.astype(jnp.float32)
    key_f = key_block.astype(jnp.float32)
    value_f = value_block.astype(jnp.float32)
    scores = jnp.einsum('rhe,khe->hrk', query_f, key_f) * score_scale
    sigmoid_gate = jax.nn.sigmoid(scores)
    probabilities = rounded(scores * sigmoid_gate * weight[None])
    grad_probs = jnp.einsum('rhe,khe->hrk', grad_f, value_f)
    grad_scores = rounded(grad_probs * sigmoid_gate * (1.0 + scores * (1.0 - sigmoid_gate)) * weight[None])
    grad_q = jnp.einsum('hrk,khe->rhe', grad_scores, key_f) * score_scale
    grad_k = jnp.einsum('hrk,rhe->khe', grad_scores, query_f) * score_scale
    grad_v = jnp.einsum('hrk,rhe->khe', probabilities, grad_f)
    return (grad_q, grad_k, grad_v)

def reference(hist_x, hist_cot, cand_x, cand_loop, hist_len, w_proj, w_out):
    query_block = min(512, SEQ)
    cand_block = min(512, CANDS)
    cand_rows = cand_x.astype(jnp.float32)
    cand_normed, _ = normalize(cand_rows)
    cand_in = cand_normed.astype(jnp.bfloat16)
    cand_u_pre = jnp.dot(cand_in, w_proj[:, :HA], preferred_element_type=jnp.float32)
    cand_q_pre = jnp.dot(cand_in, w_proj[:, 2 * HA:3 * HA], preferred_element_type=jnp.float32)
    cand_gate = (cand_u_pre * jax.nn.sigmoid(cand_u_pre)).astype(jnp.bfloat16)
    cand_query = (cand_q_pre * jax.nn.sigmoid(cand_q_pre)).astype(jnp.bfloat16).reshape(CANDS, HEADS, HS)
    cand_att = jnp.zeros((CANDS, HEADS, HS), jnp.float32)
    key_pos = jnp.arange(SEQ, dtype=jnp.int32)
    out_list = []
    grad_list = []
    for user_index in range(USERS):
        x_rows = hist_x[user_index].astype(jnp.float32)
        x_normed, x_spread = normalize(x_rows)
        pre_act = jnp.dot(x_normed.astype(jnp.bfloat16), w_proj, preferred_element_type=jnp.float32)
        hidden = (pre_act * jax.nn.sigmoid(pre_act)).astype(jnp.bfloat16)
        gate_rows = hidden[:, :HA]
        value3 = hidden[:, HA:2 * HA].reshape(SEQ, HEADS, HS)
        query3 = hidden[:, 2 * HA:3 * HA].reshape(SEQ, HEADS, HS)
        key3 = hidden[:, 3 * HA:].reshape(SEQ, HEADS, HS)
        length = hist_len[user_index]
        inv_len = 1.0 / length.astype(jnp.float32)

        def block_weight(block_index):
            query_pos = block_index * query_block + jnp.arange(query_block, dtype=jnp.int32)
            return jnp.where((key_pos[None, :] <= query_pos[:, None]) & (key_pos[None, :] < length), inv_len, 0.0)

        def forward_block(block_index):
            block_q = lax.dynamic_slice_in_dim(query3, block_index * query_block, query_block, 0)
            return attend(block_q, key3, value3, block_weight(block_index))
        block_ids = jnp.arange(SEQ // query_block, dtype=jnp.int32)
        att_rows = lax.map(forward_block, block_ids).reshape(SEQ, HA)
        att_normed, att_spread = normalize(att_rows)
        gate_f = gate_rows.astype(jnp.float32)
        mixed_rows = (att_normed * gate_f).astype(jnp.bfloat16)
        out_list.append((x_rows + jnp.dot(mixed_rows, w_out, preferred_element_type=jnp.float32)).astype(jnp.bfloat16))
        cot_rows = hist_cot[user_index]
        grad_mixed = jnp.dot(cot_rows, w_out.T, preferred_element_type=jnp.float32)
        grad_gate = grad_mixed * att_normed
        grad_att = norm_back(grad_mixed * gate_f, att_normed, att_spread).astype(jnp.bfloat16).reshape(SEQ, HEADS, HS)

        def back_block(state_tuple, block_index):
            key_total, value_total = state_tuple
            start_row = block_index * query_block
            block_q = lax.dynamic_slice_in_dim(query3, start_row, query_block, 0)
            block_g = lax.dynamic_slice_in_dim(grad_att, start_row, query_block, 0)
            more_q, more_k, more_v = attend_grads(block_q, block_g, key3, value3, block_weight(block_index))
            return ((key_total + more_k, value_total + more_v), more_q)
        zero_rows = jnp.zeros((SEQ, HEADS, HS), jnp.float32)
        (key_grad, value_grad), query_grad = lax.scan(back_block, (zero_rows, zero_rows), block_ids)
        grad_hidden = jnp.concatenate([grad_gate, value_grad.reshape(SEQ, HA), query_grad.reshape(SEQ, HA), key_grad.reshape(SEQ, HA)], axis=1)
        grad_pre = (grad_hidden * silu_slope(pre_act)).astype(jnp.bfloat16)
        grad_in = jnp.dot(grad_pre, w_proj.T, preferred_element_type=jnp.float32)
        grad_list.append((cot_rows.astype(jnp.float32) + norm_back(grad_in, x_normed, x_spread)).astype(jnp.bfloat16))

        def cand_block_att(block_index):
            start_row = block_index * cand_block
            block_q = lax.dynamic_slice_in_dim(cand_query, start_row, cand_block, 0)
            block_loop = lax.dynamic_slice_in_dim(cand_loop[:, 0], start_row, cand_block, 0)
            weight = jnp.broadcast_to(jnp.where(key_pos < length, inv_len, 0.0)[None, :], (cand_block, SEQ))
            partial_value = attend(block_q, key3, value3, weight)
            return jnp.where((block_loop == user_index)[:, None, None], partial_value, 0.0)
        cand_ids = jnp.arange(CANDS // cand_block, dtype=jnp.int32)
        cand_att = cand_att + lax.map(cand_block_att, cand_ids).reshape(CANDS, HEADS, HS)
    cand_att_normed, _ = normalize(cand_att.reshape(CANDS, HA))
    cand_mixed = (cand_att_normed * cand_gate.astype(jnp.float32)).astype(jnp.bfloat16)
    cand_out = (cand_rows + jnp.dot(cand_mixed, w_out, preferred_element_type=jnp.float32)).astype(jnp.bfloat16)
    return (jnp.stack(out_list), jnp.stack(grad_list), cand_out)
```

```python
import functools

import jax
import jax.numpy as jnp
from jax import lax
from jax.experimental import pallas as pl
from jax.experimental.pallas import tpu as pltpu
from jax.sharding import Mesh, PartitionSpec as P

HS = 128
CAP = 128
HEADS = 4
EPS = 1e-05
SCALE = HS ** (-0.5)
BF = jnp.bfloat16
F32 = jnp.float32

NN = (((1,), (0,)), ((), ()))
NT = (((1,), (1,)), ((), ()))
SMEM = pl.BlockSpec(memory_space=pltpu.SMEM)


def dot(a, b, dims=NN):
    return lax.dot_general(a, b, dims, preferred_element_type=F32)


def whole(shape):
    return pl.BlockSpec(shape, lambda *i: (0,) * len(shape))


def call(body, name, grid, in_specs, outs, out_specs, scratch, flops):
    return pl.pallas_call(
        body,
        out_shape=outs,
        grid=grid,
        in_specs=in_specs,
        out_specs=out_specs,
        scratch_shapes=scratch,
        compiler_params=pltpu.CompilerParams(vmem_limit_bytes=48 * 1024 * 1024),
        cost_estimate=pl.CostEstimate(flops=flops, transcendentals=0, bytes_accessed=1 << 20),
        name=name,
    )


def shaped(shape, dtype=BF):
    return jax.ShapeDtypeStruct(shape, dtype)


def normalize(values):
    center = values - jnp.mean(values, axis=-1, keepdims=True)
    spread = lax.rsqrt(jnp.mean(center * center, axis=-1, keepdims=True) + EPS)
    return center * spread, spread


def silu_parts(pre):
    half = 0.5 * pre
    sig = 0.5 + 0.5 * jnp.tanh(half)
    act = pre * sig
    return act, sig + act * (1.0 - sig)


def project_kv(info, x_ref, w_ref, k0, k1, k2, k3, slope_ref, xn_ref, act_ref):
    outs = (k0, k1, k2, k3)
    step = pl.program_id(0)

    @pl.when(step == 0)
    def _():
        normed, _ = normalize(x_ref[...].astype(F32))
        xn_ref[...] = normed.astype(BF)

    act, slope = silu_parts(dot(xn_ref[...], w_ref[...]))
    slope_ref[0] = slope.astype(BF)
    length = info[0]
    rows = info[1] + lax.broadcasted_iota(jnp.int32, (128, 1), 0)
    len_f = jnp.full((128, 1), length, jnp.int32).astype(F32)
    factor = jnp.where(rows < length, jnp.where(step == 0, 1.0, 1.0 / len_f), 0.0)
    act_ref[...] = (act * factor).astype(BF)
    for k in range(4):
        head = (info[2] + k) & 3
        part = act_ref[:, pl.ds(pl.multiple_of(head * HS, HS), HS)]

        @pl.when(step == 0)
        def _():
            outs[k][:, :HS] = part

        @pl.when(step == 1)
        def _():
            outs[k][:, HS:] = part


def project_qg(info, xn_ref, cot_ref, wo_ref, w_ref, k0, k1, k2, k3, slope_ref, act_ref):
    outs = (k0, k1, k2, k3)
    step = pl.program_id(0)
    act, slope = silu_parts(dot(xn_ref[...], w_ref[...]))
    slope_ref[0] = slope.astype(BF)
    act_ref[...] = jnp.where(step == 0, act * (0.5 * SCALE), act).astype(BF)

    def put(lane):
        for k in range(4):
            head = (info[2] + k) & 3
            outs[k][:, lane : lane + HS] = act_ref[:, pl.ds(pl.multiple_of(head * HS, HS), HS)]

    @pl.when(step == 0)
    def _():
        put(0)

    @pl.when(step == 1)
    def _():
        put(HS)
        act_ref[...] = dot(cot_ref[...], wo_ref[...], NT).astype(BF)
        put(2 * HS)


def slot_ids(ids_ref):
    col = ids_ref[...]
    first = lax.broadcasted_iota(jnp.int32, (256, 256), 0)
    second = lax.broadcasted_iota(jnp.int32, (256, 256), 1)
    row = jnp.sum(jnp.where(first == second, col, 0), axis=0, keepdims=True)
    return col, row, first, second


def project_cand(ids_ref, x_ref, w_ref, sent_ref, gate_ref, xn_ref):
    step = pl.program_id(0)

    @pl.when(step == 0)
    def _():
        normed, _ = normalize(x_ref[...].astype(F32))
        xn_ref[...] = normed.astype(BF)

    act, _ = silu_parts(dot(xn_ref[...], w_ref[...]))

    @pl.when(step == 0)
    def _():
        col, row, first, second = slot_ids(ids_ref)
        rank = jnp.sum(jnp.where((col == row) & (first < second), 1, 0), axis=0, keepdims=True)
        slot = row * CAP + rank
        hits = (lax.broadcasted_iota(jnp.int32, (4 * CAP, 256), 0) == slot).astype(F32).astype(BF)
        placed = dot(hits, (act * (0.5 * SCALE)).astype(BF)).astype(BF)
        for u in range(4):
            for h in range(HEADS):
                sent_ref[u * HEADS + h] = placed[u * CAP : (u + 1) * CAP, h * HS : (h + 1) * HS]

    @pl.when(step == 1)
    def _():
        gate_ref[...] = act.astype(BF)


def arrange(info, a0, a1, a2, a3, out_ref):
    for k, a in enumerate((a0, a1, a2, a3)):
        out_ref[(info[2] - k) & 3] = a[...]


def cand_attend(q_ref, *refs):
    kvs, out_ref = refs[:8], refs[8]
    q = q_ref[...].reshape(2 * CAP, HS)
    total = None
    for kv in kvs:
        block = kv[...].reshape(512, 2 * HS)
        half = dot(q, block[:, :HS], NT).astype(BF)
        probs = half + half * jnp.tanh(half)
        more = dot(probs, block[:, HS:])
        total = more if total is None else total + more
    out_ref[...] = total.astype(BF).reshape(2, CAP, HS)


def group_of(info, j):
    core = info[3] if j < 4 else 1 - info[3]
    return core * 4 + ((info[4] - (j & 3)) & 3)


def hist_forward(info, p0, p1, p2, p3, *refs):
    kvs, (att_ref, stat_ref, q_ref, g_ref) = refs[:8], refs[8:]
    for k, part in enumerate((p0, p1, p2, p3)):
        y = (info[2] - k) & 3
        rows = pl.ds(pl.multiple_of(y * 128, 128), 128)
        q_ref[rows, :] = part[:, :HS]
        g_ref[rows, :] = part[:, HS : 2 * HS].astype(F32) * part[:, 2 * HS :].astype(F32)
    mine = group_of(info, 0)
    first = lax.broadcasted_iota(jnp.int32, (128, 128), 0)
    second = lax.broadcasted_iota(jnp.int32, (128, 128), 1)
    masks = []
    for j in range(8):
        lead = jnp.where(group_of(info, j) < mine, 128, jnp.where(group_of(info, j) == mine, 0, -128))
        masks.append((second <= first + lead).astype(F32).astype(BF))
    for y in range(4):
        q = q_ref[y * 128 : (y + 1) * 128, :]
        total = None
        for j, kv in enumerate(kvs):
            block = kv[...].reshape(512, 2 * HS)[: 128 * (y + 1)]
            half = dot(q, block[:, :HS], NT).astype(BF)
            probs = half + half * jnp.tanh(half)
            last = probs[:, 128 * y :] * masks[j]
            probs = last if y == 0 else jnp.concatenate([probs[:, : 128 * y], last], axis=1)
            more = dot(probs, block[:, HS:])
            total = more if total is None else total + more
        att_ref[y * 128 : (y + 1) * 128, :] = total
    att = att_ref[...]
    g = g_ref[...]
    mean = jnp.mean(att, axis=1, keepdims=True)
    center = att - mean
    lane = lax.broadcasted_iota(jnp.int32, (512, 128), 1)
    stats = jnp.where(lane == 0, mean, 0.0)
    stats = jnp.where(lane == 1, jnp.sum(center * center, axis=1, keepdims=True), stats)
    stats = jnp.where(lane == 2, jnp.sum(g, axis=1, keepdims=True), stats)
    stats = jnp.where(lane == 3, jnp.sum(g * center, axis=1, keepdims=True), stats)
    stat_ref[...] = jnp.transpose(stats)[:8]


def normed_grads(info, p0, p1, p2, p3, att_ref, s0, s1, s2, s3, ga_ref, b0, b1, b2, b3, gate_ref, gm_ref):
    for k, part in enumerate((p0, p1, p2, p3)):
        y = (info[2] - k) & 3
        rows = pl.ds(pl.multiple_of(y * 128, 128), 128)
        gate_ref[rows, :] = part[:, HS : 2 * HS].astype(F32)
        gm_ref[rows, :] = part[:, 2 * HS :].astype(F32)
    stats = [s[...] for s in (s0, s1, s2, s3)]
    mean = sum(s[0:1] for s in stats) * 0.25
    squares = sum(s[1:2] + HS * (s[0:1] - mean) * (s[0:1] - mean) for s in stats)
    spread = lax.rsqrt(squares * (1.0 / (HEADS * HS)) + EPS)
    g_mean = sum(s[2:3] for s in stats) * (1.0 / (HEADS * HS))
    ga_sum = sum(s[3:4] + s[2:3] * (s[0:1] - mean) for s in stats)
    ga_mean = ga_sum * spread * (1.0 / (HEADS * HS))
    line = lax.broadcasted_iota(jnp.int32, (128, 512), 0)
    packed = jnp.where(line == 0, mean, 0.0)
    packed = jnp.where(line == 1, spread, packed)
    packed = jnp.where(line == 2, g_mean, packed)
    packed = jnp.where(line == 3, ga_mean, packed)
    cols = jnp.transpose(packed)
    spread_c = cols[:, 1:2]
    normed = (att_ref[...] - cols[:, 0:1]) * spread_c
    gate = gate_ref[...]
    gm = gm_ref[...]
    ga_ref[...] = (spread_c * (gate * gm - cols[:, 2:3] - normed * cols[:, 3:4])).astype(BF)
    gate_ref[...] = normed * gate
    gm_ref[...] = normed * gm
    for k, out in enumerate((b0, b1, b2, b3)):
        y = (info[2] + k) & 3
        rows = pl.ds(pl.multiple_of(y * 128, 128), 128)
        out[:, :HS] = gate_ref[rows, :].astype(BF)
        out[:, HS:] = gm_ref[rows, :].astype(BF)


def slope_times(half, grads):
    t = jnp.tanh(half)
    probs = half + half * t
    slope = (1.0 + t + probs * (1.0 - t)).astype(BF)
    return probs, grads * slope


def hist_dq(info, q_in, ga_ref, *refs):
    kvs, dq_ref = refs[:8], refs[8]
    mine = group_of(info, 0)
    first = lax.broadcasted_iota(jnp.int32, (128, 128), 0)
    second = lax.broadcasted_iota(jnp.int32, (128, 128), 1)
    masks = []
    for j in range(8):
        lead = jnp.where(group_of(info, j) < mine, 128, jnp.where(group_of(info, j) == mine, 0, -128))
        masks.append((second <= first + lead).astype(F32).astype(BF))
    for y in range(4):
        q = q_in[y * 128 : (y + 1) * 128, :]
        ga = ga_ref[y * 128 : (y + 1) * 128, :]
        total = None
        for j, kv in enumerate(kvs):
            block = kv[...].reshape(512, 2 * HS)[: 128 * (y + 1)]
            half = dot(q, block[:, :HS], NT).astype(BF)
            _, ds = slope_times(half, dot(ga, block[:, HS:], NT).astype(BF))
            last = ds[:, 128 * y :] * masks[j]
            ds = last if y == 0 else jnp.concatenate([ds[:, : 128 * y], last], axis=1)
            more = dot(ds, block[:, :HS])
            total = more if total is None else total + more
        dq_ref[y * 128 : (y + 1) * 128, :] = (total * (0.5 * SCALE)).astype(BF)


def hist_dkv(info, dq_ref, kv_ref, *refs):
    qs, gas, outs, all_ref = refs[:8], refs[8:16], refs[16:20], refs[20]
    mine = group_of(info, 0)
    first = lax.broadcasted_iota(jnp.int32, (128, 128), 0)
    second = lax.broadcasted_iota(jnp.int32, (128, 128), 1)
    masks = []
    for j in range(8):
        lead = jnp.where(group_of(info, j) > mine, 128, jnp.where(group_of(info, j) == mine, 0, -128))
        masks.append((first <= second + lead).astype(F32).astype(BF))
    for y in range(4):
        key = kv_ref[y, :, :HS]
        value = kv_ref[y, :, HS:]
        dk = dv = None
        for j in range(8):
            q = qs[j][128 * y :, :]
            ga = gas[j][128 * y :, :]
            half = dot(key, q, NT).astype(BF)
            probs, ds = slope_times(half, dot(value, ga, NT).astype(BF))
            p_first = probs[:, :128] * masks[j]
            d_first = ds[:, :128] * masks[j]
            if y < 3:
                probs = jnp.concatenate([p_first, probs[:, 128:]], axis=1)
                ds = jnp.concatenate([d_first, ds[:, 128:]], axis=1)
            else:
                probs, ds = p_first, d_first
            more_k = dot(ds, q)
            more_v = dot(probs, ga)
            dk = more_k if dk is None else dk + more_k
            dv = more_v if dv is None else dv + more_v
        all_ref[y, :, :HS] = dq_ref[y * 128 : (y + 1) * 128, :]
        all_ref[y, :, HS : 2 * HS] = dk.astype(BF)
        all_ref[y, :, 2 * HS :] = dv.astype(BF)
    for k in range(4):
        outs[k][...] = all_ref[(info[2] + k) & 3]


def hist_close(info, x_ref, wo_ref, b0, b1, b2, b3, out_ref, mixed_ref):
    for k, b in enumerate((b0, b1, b2, b3)):
        head = (info[2] - k) & 3
        mixed_ref[:, pl.ds(pl.multiple_of(head * HS, HS), HS)] = b[:, :HS]
    out_ref[0] = (x_ref[...].astype(F32) + dot(mixed_ref[...], wo_ref[...])).astype(BF)


def grad_close(info, x_ref, cot_ref, skv_ref, sqg_ref, w_ref, *refs):
    ones, twos, out_ref, hid_ref, e_ref = refs[:4], refs[4:8], refs[8], refs[9], refs[10]
    step = pl.program_id(0)

    @pl.when(step == 0)
    def _():
        len_f = jnp.full((128, 1), info[0], jnp.int32).astype(F32)
        for k in range(4):
            head = (info[2] - k) & 3
            cols = pl.ds(pl.multiple_of(head * HS, HS), HS)
            hid_ref[0, :, cols] = ones[k][:, HS:]
            hid_ref[1, :, cols] = (twos[k][:, 2 * HS :].astype(F32) / len_f).astype(BF)
            hid_ref[2, :, cols] = twos[k][:, :HS]
            hid_ref[3, :, cols] = twos[k][:, HS : 2 * HS]
        hid_ref[0] = (hid_ref[0].astype(F32) * sqg_ref[1].astype(F32)).astype(BF)
        hid_ref[1] = (hid_ref[1].astype(F32) * skv_ref[1].astype(F32)).astype(BF)
        hid_ref[2] = (hid_ref[2].astype(F32) * sqg_ref[0].astype(F32)).astype(BF)
        hid_ref[3] = (hid_ref[3].astype(F32) * skv_ref[0].astype(F32)).astype(BF)
        e_ref[...] = jnp.zeros_like(e_ref)

    e_ref[...] += dot(hid_ref[step], w_ref[...], NT)

    @pl.when(step == 3)
    def _():
        normed, spread = normalize(x_ref[...].astype(F32))
        e = e_ref[...]
        back = spread * (
            e
            - jnp.mean(e, axis=-1, keepdims=True)
            - normed * jnp.mean(e * normed, axis=-1, keepdims=True)
        )
        out_ref[0] = (cot_ref[...].astype(F32) + back).astype(BF)


def cand_close(ids_ref, x_ref, gate_ref, wo_ref, ret_ref, out_ref):
    col, row, first, second = slot_ids(ids_ref)
    rank = jnp.sum(jnp.where((col == row) & (second < first), 1, 0), axis=1, keepdims=True)
    slot = col * CAP + rank
    hits = (lax.broadcasted_iota(jnp.int32, (256, 4 * CAP), 1) == slot).astype(F32).astype(BF)
    heads = []
    for h in range(HEADS):
        rows = jnp.concatenate([ret_ref[u * HEADS + h] for u in range(4)], axis=0)
        heads.append(dot(hits, rows))
    normed, _ = normalize(jnp.concatenate(heads, axis=1))
    mixed = (normed * gate_ref[...].astype(F32)).astype(BF)
    out_ref[...] = (x_ref[...].astype(F32) + dot(mixed, wo_ref[...])).astype(BF)


def turned(value, axis, size, steps):
    return lax.ppermute(value, axis, [(i, (i + steps) % size) for i in range(size)])


def crossed(value, steps):
    pairs = []
    for c in range(2):
        for y in range(4):
            for xh in range(2):
                pairs.append(((c * 4 + y) * 2 + xh, (xh * 4 + (y + steps) % 4) * 2 + c))
    return lax.ppermute(value, ("c", "y", "xh"), pairs)


def gathered(value):
    mine = [value] + [turned(value, "z", 4, k) for k in (1, 2, 3)]
    return mine + [turned(v, "c", 2, 1) for v in mine]


def per_device(hist_x, hist_cot, cand_x, cand_loop, hist_len, w_proj, w_out):
    y, xh, z = lax.axis_index("y"), lax.axis_index("xh"), lax.axis_index("z")
    info = jnp.stack(
        [hist_len[0], (y * 8 + xh * 4 + z) * 128, y, lax.axis_index("c"), z]
    ).astype(jnp.int32)
    x_rows = hist_x.reshape(128, 1024)
    cot = hist_cot.reshape(128, 1024)
    row_part = whole((128, 1024))

    def pieces(width):
        return [shaped((128, width))] * 4

    def piece_specs(width):
        return [whole((128, width))] * 4

    def wcol(pick):
        return pl.BlockSpec((1024, 512), lambda i: (0, pick(i)))

    slope = pl.BlockSpec((1, 128, 512), lambda i: (i, 0, 0))
    *kv_out, slope_kv, xn = call(
        project_kv, "project_kv", (2,),
        [SMEM, row_part, wcol(lambda i: 3 - 2 * i)],
        pieces(256) + [shaped((2, 128, 512)), shaped((128, 1024))],
        piece_specs(256) + [slope, row_part],
        [pltpu.VMEM((128, 512), BF)], 270_000_000,
    )(info, x_rows, w_proj)
    kv_in = [crossed(v, k) for k, v in enumerate(kv_out)]

    *qg_out, slope_qg = call(
        project_qg, "project_qg", (2,),
        [SMEM, row_part, row_part, whole((512, 1024)), wcol(lambda i: 2 - 2 * i)],
        pieces(384) + [shaped((2, 128, 512))],
        piece_specs(384) + [slope],
        [pltpu.VMEM((128, 512), BF)], 400_000_000,
    )(info, xn, cot, w_out, w_proj)
    qg_in = [crossed(v, k) for k, v in enumerate(qg_out)]

    sent, cand_gate = call(
        project_cand, "project_cand", (2,),
        [whole((256, 1)), whole((256, 1024)), wcol(lambda i: 2 - 2 * i)],
        [shaped((16, 128, 128)), shaped((256, 512))],
        [whole((16, 128, 128)), whole((256, 512))],
        [pltpu.VMEM((256, 1024), BF)], 700_000_000,
    )(cand_loop, cand_x, w_proj)
    arrived = lax.all_to_all(sent, ("xl", "xh", "y"), 0, 0, tiled=True)

    def arranged(parts, width):
        return call(
            arrange, "arrange", (1,), [SMEM] + piece_specs(width),
            shaped((4, 128, width)), whole((4, 128, width)), [], 1_000_000,
        )(info, *parts)

    kv_mine = arranged(kv_in, 256)
    kvs = gathered(kv_mine)
    q_mine = arranged([v[:, :HS] for v in qg_in], HS).reshape(512, HS)
    qs = gathered(q_mine)
    kv_specs = [whole((4, 128, 256))] * 8
    flat = whole((512, 128))

    att, stats = call(
        hist_forward, "hist_forward", (1,), [SMEM] + piece_specs(384) + kv_specs,
        [shaped((512, 128), F32), shaped((8, 512), F32)], [flat, whole((8, 512))],
        [pltpu.VMEM((512, 128), BF), pltpu.VMEM((512, 128), F32)], 1_400_000_000,
    )(info, *qg_in, *kvs)

    halves = []
    for part in range(2):
        halves.append(
            call(
                cand_attend, "cand_attend", (4,),
                [pl.BlockSpec((2, 128, 128), functools.partial(lambda p, i: (i + 4 * p, 0, 0), part))] + kv_specs,
                shaped((8, 128, 128)), pl.BlockSpec((2, 128, 128), lambda i: (i, 0, 0)),
                [], 4_300_000_000,
            )(arrived, *kvs)
        )
    returned = lax.all_to_all(
        jnp.concatenate(halves, axis=0), ("xl", "xh", "y"), 0, 0, tiled=True
    )

    all_stats = [stats] + [turned(stats, "y", 4, k) for k in (1, 2, 3)]
    ga, *back_one = call(
        normed_grads, "normed_grads", (1,),
        [SMEM] + piece_specs(384) + [flat] + [whole((8, 512))] * 4,
        [shaped((512, 128))] + pieces(256), [flat] + piece_specs(256),
        [pltpu.VMEM((512, 128), F32)] * 2, 1_000_000,
    )(info, *qg_in, att, *all_stats)
    gas = gathered(ga)
    one_in = [crossed(v, k) for k, v in enumerate(back_one)]

    dq = call(
        hist_dq, "hist_dq", (1,), [SMEM, flat, flat] + kv_specs,
        shaped((512, 128)), flat, [], 2_000_000_000,
    )(info, q_mine, ga, *kvs)
    back_two = call(
        hist_dkv, "hist_dkv", (1,), [SMEM, flat, whole((4, 128, 256))] + [flat] * 16,
        pieces(384), piece_specs(384), [pltpu.VMEM((4, 128, 384), BF)], 2_800_000_000,
    )(info, dq, kv_mine, *qs, *gas)
    two_in = [crossed(v, k) for k, v in enumerate(back_two)]

    cand_out = call(
        cand_close, "cand_close", (1,),
        [whole((256, 1)), whole((256, 1024)), whole((256, 512)), whole((512, 1024)), whole((16, 128, 128))],
        shaped((256, 1024)), whole((256, 1024)), [], 400_000_000,
    )(cand_loop, cand_x, cand_gate, w_out, returned)

    out_spec = whole((1, 128, 1024))
    hist_out = call(
        hist_close, "hist_close", (1,),
        [SMEM, row_part, whole((512, 1024))] + piece_specs(256),
        shaped((1, 128, 1024)), out_spec, [pltpu.VMEM((128, 512), BF)], 140_000_000,
    )(info, x_rows, w_out, *one_in)

    hist_grad = call(
        grad_close, "grad_close", (4,),
        [SMEM, row_part, row_part, whole((2, 128, 512)), whole((2, 128, 512)), wcol(lambda i: i)]
        + piece_specs(256) + piece_specs(384),
        shaped((1, 128, 1024)), out_spec,
        [pltpu.VMEM((4, 128, 512), BF), pltpu.VMEM((128, 1024), F32)], 550_000_000,
    )(info, x_rows, cot, slope_kv, slope_qg, w_proj, *one_in, *two_in)
    return hist_out, hist_grad, cand_out


def solution(mesh):
    split = Mesh(mesh.devices.reshape(2, 2, 4, 2, 4), ("xl", "c", "y", "xh", "z"))
    users, rows = ("xl", "c"), ("y", "xh", "z")
    hist = P(users, rows, None)
    cand = P(users + rows, None)
    return jax.shard_map(
        per_device,
        mesh=split,
        in_specs=(hist, hist, cand, cand, P(users), P(), P()),
        out_specs=(hist, hist, cand),
        check_vma=False,
    )
```

```python
import functools

import jax
import jax.numpy as jnp
from jax import lax
from jax.experimental import pallas as pl
from jax.experimental.pallas import tpu as pltpu
from jax.sharding import Mesh, PartitionSpec as P

HS = 128
CAP = 128
HEADS = 4
EPS = 1e-05
SCALE = HS ** (-0.5)
BF = jnp.bfloat16
F32 = jnp.float32

NN = (((1,), (0,)), ((), ()))
NT = (((1,), (1,)), ((), ()))
SMEM = pl.BlockSpec(memory_space=pltpu.SMEM)


def dot(a, b, dims=NN):
    return lax.dot_general(a, b, dims, preferred_element_type=F32)


def whole(shape):
    return pl.BlockSpec(memory_space=pltpu.VMEM)


def call(body, name, grid, in_specs, outs, out_specs, scratch, flops, after=(), limit=12):
    count = len(in_specs)

    def without(*refs):
        return body(*refs[:count], *refs[count + len(after) :])

    made = pl.pallas_call(
        without if after else body,
        out_shape=outs,
        grid=grid,
        in_specs=list(in_specs) + [pl.BlockSpec(memory_space=pl.ANY)] * len(after),
        out_specs=out_specs,
        scratch_shapes=scratch,
        compiler_params=pltpu.CompilerParams(vmem_limit_bytes=limit * 1024 * 1024),
        cost_estimate=pl.CostEstimate(flops=flops, transcendentals=0, bytes_accessed=1 << 20),
        name=name,
    )
    def run(*args):
        pinned = []
        for arg, spec in zip(args, in_specs):
            if spec is not SMEM:
                space = spec.memory_space or pltpu.VMEM
                arg = pltpu.with_memory_space_constraint(arg, space)
            pinned.append(arg)
        return made(*pinned, *[pltpu.with_memory_space_constraint(t, pltpu.VMEM) for t in after])

    return run


def shaped(shape, dtype=BF):
    return pltpu.VMEM(shape, dtype)


def normalize(values):
    center = values - jnp.mean(values, axis=-1, keepdims=True)
    spread = lax.rsqrt(jnp.mean(center * center, axis=-1, keepdims=True) + EPS)
    return center * spread, spread


def silu_parts(pre):
    half = 0.5 * pre
    sig = 0.5 + 0.5 * jnp.tanh(half)
    act = pre * sig
    return act, sig + act * (1.0 - sig)


def columns(w_ref, buf, sems, picks):
    copies = []
    for slot, pick in enumerate(picks):
        copy = pltpu.make_async_copy(w_ref.at[:, pl.ds(512 * pick, 512)], buf.at[slot], sems.at[slot])
        copy.start()
        copies.append(copy)
    return copies


def slot_ids(ids_ref):
    col = ids_ref[...]
    first = lax.broadcasted_iota(jnp.int32, (256, 256), 0)
    second = lax.broadcasted_iota(jnp.int32, (256, 256), 1)
    row = jnp.sum(jnp.where(first == second, col, 0), axis=0, keepdims=True)
    return col, row, first, second


def project_all(info, x_ref, cot_ref, wo_ref, w_ref, k0, k1, k2, k3, slope_ref, xn_ref, act_ref, buf, sems):
    copies = columns(w_ref, buf, sems, (3, 1, 2, 0))
    normed, _ = normalize(x_ref[...].astype(F32))
    xn_ref[...] = normed.astype(BF)
    rows = info[1] + lax.broadcasted_iota(jnp.int32, (128, 1), 0)
    inside = jnp.where(rows < info[0], 1.0, 0.0)
    length = jnp.full((128, 1), info[0], jnp.int32).astype(F32)

    def put(values, part):
        act_ref[...] = values.astype(BF)
        for k, out in enumerate((k0, k1, k2, k3)):
            lane = pl.multiple_of(((info[2] + k) & 3) * HS, HS)
            out[:, part * HS : (part + 1) * HS] = act_ref[:, pl.ds(lane, HS)]

    put(dot(cot_ref[...], wo_ref[...], NT), 4)
    for part in range(4):
        copies[part].wait()
        act, slope = silu_parts(dot(xn_ref[...], buf[part]))
        slope_ref[part] = slope.astype(BF)
        put(act * (inside, inside / length, 0.5 * SCALE, 1.0)[part], part)


def arrange(info, a0, a1, a2, a3, out_ref):
    for k, a in enumerate((a0, a1, a2, a3)):
        out_ref[(info[2] - k) & 3] = a[:, : 3 * HS]


def project_cand(ids_ref, x_ref, w_ref, sent_ref, gate_ref, xn_ref, buf, sems):
    copies = columns(w_ref, buf, sems, (2, 0))
    xn_ref[...] = normalize(x_ref[...].astype(F32))[0].astype(BF)
    col, row, first, second = slot_ids(ids_ref)
    rank = jnp.sum(jnp.where((col == row) & (first < second), 1, 0), axis=0, keepdims=True)
    slot = row * CAP + rank
    hits = (lax.broadcasted_iota(jnp.int32, (4 * CAP, 256), 0) == slot).astype(F32).astype(BF)
    copies[0].wait()
    act, _ = silu_parts(dot(xn_ref[...], buf[0]))
    placed = dot(hits, (act * (0.5 * SCALE)).astype(BF)).astype(BF)
    for u in range(4):
        for h in range(HEADS):
            sent_ref[u * HEADS + h] = placed[u * CAP : (u + 1) * CAP, h * HS : (h + 1) * HS]
    copies[1].wait()
    act, _ = silu_parts(dot(xn_ref[...], buf[1]))
    gate_ref[...] = act.astype(BF)


def pack(one_ref, two_ref, out_ref):
    out_ref[0] = one_ref[...]
    out_ref[1] = two_ref[...]


def unpack(pair_ref, out_ref):
    out_ref[...] = pair_ref[0]


def blocks_of(refs):
    pair, first, second, third, fourth = refs
    out = [pair.at[0], pair.at[1], first.at[0], first.at[1], second.at[0], second.at[1], third, fourth]
    return out


def order_of(info):
    c, z = info[3], info[4]
    o = 1 - c
    side = 1 - 2 * c
    near, far = (z - side) & 3, (z + side) & 3
    across = (z + 2) & 3
    spots = [(c, z), (o, z), (c, near), (o, near), (o, far), (c, far), (c, across), (o, across)]
    return [4 * core + spot for core, spot in spots]


def corner_masks(info, backward):
    order = order_of(info)
    first = lax.broadcasted_iota(jnp.int32, (128, 128), 0)
    second = lax.broadcasted_iota(jnp.int32, (128, 128), 1)
    masks = []
    for o in order:
        ahead = o > order[0] if backward else o < order[0]
        lead = jnp.where(ahead, 128, jnp.where(o == order[0], 0, -128))
        keep = first <= second + lead if backward else second <= first + lead
        masks.append(keep.astype(F32).astype(BF))
    return masks


def cand_attend(count, begin, end, *refs):
    q_ref, kvs, rest = refs[0], refs[1 : 1 + count], refs[1 + count :]
    q = q_ref[...].reshape(4 * CAP, HS)
    total = None if begin else rest[0][...]
    for kv in kvs:
        pieces = [kv] if len(kv.shape) == 2 else [kv.at[0], kv.at[1]]
        for block in pieces:
            half = dot(q, block[:, :HS], NT).astype(BF)
            probs = half + half * jnp.tanh(half)
            more = dot(probs, block[:, HS : 2 * HS])
            total = more if total is None else total + more
    if end:
        rest[-1][...] = total.astype(BF).reshape(4, CAP, HS)
    else:
        rest[-1][...] = total


def hist_forward(info, p0, p1, p2, p3, *refs):
    blocks, (att_ref, stat_ref, g_ref) = blocks_of(refs[:5]), refs[5:]
    masks = corner_masks(info, False)
    for k, part in enumerate((p0, p1, p2, p3)):
        rows = pl.ds(pl.multiple_of(((info[2] - k) & 3) * 128, 128), 128)
        g_ref[rows, :] = part[:, 3 * HS : 4 * HS].astype(F32) * part[:, 4 * HS :].astype(F32)
    for y in range(4):
        q = blocks[0][y * 128 : (y + 1) * 128, 2 * HS :]
        total = None
        for block, mask in zip(blocks, masks):
            half = dot(q, block[: 128 * (y + 1), :HS], NT).astype(BF)
            probs = half + half * jnp.tanh(half)
            last = probs[:, 128 * y :] * mask
            probs = last if y == 0 else jnp.concatenate([probs[:, : 128 * y], last], axis=1)
            more = dot(probs, block[: 128 * (y + 1), HS : 2 * HS])
            total = more if total is None else total + more
        att_ref[y * 128 : (y + 1) * 128, :] = total
    att = att_ref[...]
    g = g_ref[...]
    mean = jnp.mean(att, axis=1, keepdims=True)
    center = att - mean
    lane = lax.broadcasted_iota(jnp.int32, (512, 128), 1)
    stats = jnp.where(lane == 0, mean, 0.0)
    stats = jnp.where(lane == 1, jnp.sum(center * center, axis=1, keepdims=True), stats)
    stats = jnp.where(lane == 2, jnp.sum(g, axis=1, keepdims=True), stats)
    stats = jnp.where(lane == 3, jnp.sum(g * center, axis=1, keepdims=True), stats)
    stat_ref[...] = jnp.transpose(stats)[:8]


def normed_grads(info, p0, p1, p2, p3, att_ref, s0, s1, s2, s3, ga_ref, mg_ref, gate_ref, gm_ref):
    for k, part in enumerate((p0, p1, p2, p3)):
        y = (info[2] - k) & 3
        rows = pl.ds(pl.multiple_of(y * 128, 128), 128)
        gate_ref[rows, :] = part[:, 3 * HS : 4 * HS].astype(F32)
        gm_ref[rows, :] = part[:, 4 * HS :].astype(F32)
    stats = [s[...] for s in (s0, s1, s2, s3)]
    mean = sum(s[0:1] for s in stats) * 0.25
    squares = sum(s[1:2] + HS * (s[0:1] - mean) * (s[0:1] - mean) for s in stats)
    spread = lax.rsqrt(squares * (1.0 / (HEADS * HS)) + EPS)
    g_mean = sum(s[2:3] for s in stats) * (1.0 / (HEADS * HS))
    ga_sum = sum(s[3:4] + s[2:3] * (s[0:1] - mean) for s in stats)
    ga_mean = ga_sum * spread * (1.0 / (HEADS * HS))
    line = lax.broadcasted_iota(jnp.int32, (128, 512), 0)
    packed = jnp.where(line == 0, mean, 0.0)
    packed = jnp.where(line == 1, spread, packed)
    packed = jnp.where(line == 2, g_mean, packed)
    packed = jnp.where(line == 3, ga_mean, packed)
    cols = jnp.transpose(packed)
    spread_c = cols[:, 1:2]
    normed = (att_ref[...] - cols[:, 0:1]) * spread_c
    gate = gate_ref[...]
    gm = gm_ref[...]
    ga_ref[...] = (spread_c * (gate * gm - cols[:, 2:3] - normed * cols[:, 3:4])).astype(BF)
    mg_ref[:, :HS] = (normed * gate).astype(BF)
    mg_ref[:, HS:] = (normed * gm).astype(BF)


def slope_times(half, grads):
    t = jnp.tanh(half)
    probs = half + half * t
    slope = (1.0 + t + probs * (1.0 - t)).astype(BF)
    return probs, grads * slope


def hist_dq(info, ga_ref, *refs):
    blocks, dq_ref = blocks_of(refs[:5]), refs[5]
    masks = corner_masks(info, False)
    for y in range(4):
        q = blocks[0][y * 128 : (y + 1) * 128, 2 * HS :]
        ga = ga_ref[y * 128 : (y + 1) * 128, :]
        total = None
        for block, mask in zip(blocks, masks):
            key = block[: 128 * (y + 1), :HS]
            half = dot(q, key, NT).astype(BF)
            _, ds = slope_times(half, dot(ga, block[: 128 * (y + 1), HS : 2 * HS], NT).astype(BF))
            last = ds[:, 128 * y :] * mask
            ds = last if y == 0 else jnp.concatenate([ds[:, : 128 * y], last], axis=1)
            more = dot(ds, key)
            total = more if total is None else total + more
        dq_ref[y] = (total * (0.5 * SCALE)).astype(BF)


def hist_dkv(info, dq_ref, mg_ref, *refs):
    blocks, gas, outs, all_ref = blocks_of(refs[:5]), blocks_of(refs[5:10]), refs[10:14], refs[14]
    masks = corner_masks(info, True)
    for y in range(4):
        key = blocks[0][y * 128 : (y + 1) * 128, :HS]
        value = blocks[0][y * 128 : (y + 1) * 128, HS : 2 * HS]
        dk = dv = None
        for block, ga_block, mask in zip(blocks, gas, masks):
            q = block[128 * y :, 2 * HS :]
            ga = ga_block[128 * y :, :]
            half = dot(key, q, NT).astype(BF)
            probs, ds = slope_times(half, dot(value, ga, NT).astype(BF))
            p_first = probs[:, :128] * mask
            d_first = ds[:, :128] * mask
            if y < 3:
                probs = jnp.concatenate([p_first, probs[:, 128:]], axis=1)
                ds = jnp.concatenate([d_first, ds[:, 128:]], axis=1)
            else:
                probs, ds = p_first, d_first
            more_k = dot(ds, q)
            more_v = dot(probs, ga)
            dk = more_k if dk is None else dk + more_k
            dv = more_v if dv is None else dv + more_v
        all_ref[y, :, HS : 2 * HS] = dk.astype(BF)
        all_ref[y, :, 2 * HS : 3 * HS] = dv.astype(BF)
        all_ref[y, :, :HS] = dq_ref[y]
        all_ref[y, :, 3 * HS :] = mg_ref[y * 128 : (y + 1) * 128, :]
    for k in range(4):
        outs[k][...] = all_ref[(info[2] + k) & 3]


def hist_close(info, x_ref, wo_ref, b0, b1, b2, b3, out_ref, mixed_ref):
    for k, b in enumerate((b0, b1, b2, b3)):
        lane = pl.multiple_of(((info[2] - k) & 3) * HS, HS)
        mixed_ref[:, pl.ds(lane, HS)] = b[:, 3 * HS : 4 * HS]
    out_ref[0] = (x_ref[...].astype(F32) + dot(mixed_ref[...], wo_ref[...])).astype(BF)


def grad_close(info, x_ref, cot_ref, slope_ref, w_ref, b0, b1, b2, b3, out_ref, hid_ref, buf, sems):
    copies = columns(w_ref, buf, sems, (0, 1, 2, 3))
    length = jnp.full((128, 1), info[0], jnp.int32).astype(F32)
    for k, b in enumerate((b0, b1, b2, b3)):
        lanes = pl.ds(pl.multiple_of(((info[2] - k) & 3) * HS, HS), HS)

        def put(part, grads, which):
            hid_ref[part, :, lanes] = (grads * slope_ref[which, :, lanes].astype(F32)).astype(BF)

        put(0, b[:, 4 * HS :].astype(F32), 3)
        put(1, b[:, 2 * HS : 3 * HS].astype(F32) / length, 1)
        put(2, b[:, :HS].astype(F32), 2)
        put(3, b[:, HS : 2 * HS].astype(F32), 0)
    e = None
    for part in range(4):
        copies[part].wait()
        more = dot(hid_ref[part], buf[part], NT)
        e = more if e is None else e + more
    normed, spread = normalize(x_ref[...].astype(F32))
    back = spread * (
        e - jnp.mean(e, axis=-1, keepdims=True) - normed * jnp.mean(e * normed, axis=-1, keepdims=True)
    )
    out_ref[0] = (cot_ref[...].astype(F32) + back).astype(BF)


def relay(value_ref, out_ref):
    out_ref[...] = value_ref[...]


def cand_close(ids_ref, x_ref, gate_ref, wo_ref, ret_ref, out_ref):
    col, row, first, second = slot_ids(ids_ref)
    rank = jnp.sum(jnp.where((col == row) & (second < first), 1, 0), axis=1, keepdims=True)
    slot = col * CAP + rank
    hits = (lax.broadcasted_iota(jnp.int32, (256, 4 * CAP), 1) == slot).astype(F32).astype(BF)
    heads = []
    for h in range(HEADS):
        rows = jnp.concatenate([ret_ref[u * HEADS + h] for u in range(4)], axis=0)
        heads.append(dot(hits, rows))
    normed, _ = normalize(jnp.concatenate(heads, axis=1))
    mixed = (normed * gate_ref[...].astype(F32)).astype(BF)
    out_ref[...] = (x_ref[...].astype(F32) + dot(mixed, wo_ref[...])).astype(BF)


def turned(value, axis, size, steps):
    return lax.ppermute(value, axis, [(i, (i + steps) % size) for i in range(size)])


def crossed(value, steps):
    pairs = []
    for c in range(2):
        for y in range(4):
            for xh in range(2):
                pairs.append(((c * 4 + y) * 2 + xh, (xh * 4 + (y + steps) % 4) * 2 + c))
    return lax.ppermute(value, ("c", "y", "xh"), pairs)


def across(value):
    return lax.ppermute(value, "c", [(0, 1), (1, 0)])


def along(value):
    pairs = []
    for z in range(4):
        pairs.append((z, (z + 1) % 4))
        pairs.append((4 + z, 4 + (z + 3) % 4))
    return lax.ppermute(value, ("c", "z"), pairs)


def per_device(hist_x, hist_cot, cand_x, cand_loop, hist_len, w_proj, w_out):
    y, xh, z, c = (lax.axis_index(n) for n in ("y", "xh", "z", "c"))
    x_rows = hist_x.reshape(128, 1024)
    cot = hist_cot.reshape(128, 1024)
    info = jnp.stack([hist_len[0], (y * 8 + xh * 4 + z) * 128, y, c, z]).astype(jnp.int32)
    held = pl.BlockSpec(memory_space=pltpu.VMEM)
    far = pl.BlockSpec(memory_space=pltpu.HBM)

    def weights(count):
        return [pltpu.VMEM((count, 1024, 512), BF), pltpu.SemaphoreType.DMA((count,))]

    def packed(one, two, after=()):
        return call(
            pack, "pack", (1,), [held] * 2, shaped((2,) + one.shape), held, [], 1_000_000, after
        )(one, two)

    def unpacked(pair, after=()):
        return call(unpack, "unpack", (1,), [held], shaped(pair.shape[1:]), held, [], 1_000_000, after)(pair)

    *sent, slope = call(
        project_all, "project_all", (1,), [SMEM, held, held, held, far],
        [shaped((128, 640))] * 4 + [shaped((4, 128, 512))], [held] * 5,
        [pltpu.VMEM((128, 1024), BF), pltpu.VMEM((128, 512), BF)] + weights(4), 700_000_000,
    )(info, x_rows, cot, w_out, w_proj)
    parts = [crossed(v, k) for k, v in enumerate(sent)]

    sent_cand, cand_gate = call(
        project_cand, "project_cand", (1,), [held, held, far],
        [shaped((16, 128, 128)), shaped((256, 512))], [held] * 2,
        [pltpu.VMEM((256, 1024), BF)] + weights(2), 700_000_000, (slope,),
    )(cand_loop, cand_x, w_proj)

    own = call(
        arrange, "arrange", (1,), [SMEM] + [held] * 4, shaped((4, 128, 384)), held, [], 1_000_000,
        (cand_gate,),
    )(info, *parts).reshape(512, 384)
    pair = packed(own, across(own))
    near = along(pair)
    arrived = lax.all_to_all(sent_cand, ("xl", "xh", "y"), 0, 0, tiled=True)
    passing = unpacked(near, (arrived,))
    third = along(passing)
    kvq = [pair, near, across(near), third, across(third)]

    q_spec = pl.BlockSpec((4, 128, 128), lambda i: (i, 0, 0))
    acc_spec = pl.BlockSpec((512, 128), lambda i: (i, 0))

    def cand_part(kvs, total, end, after):
        begin = total is None
        return call(
            functools.partial(cand_attend, len(kvs), begin, end), "cand_attend", (4,),
            [q_spec] + [held] * len(kvs) + ([] if begin else [acc_spec]),
            shaped((16, 128, 128)) if end else shaped((2048, 128), F32),
            q_spec if end else acc_spec, [], 1_000_000_000 * len(kvs), after,
        )(arrived, *kvs, *([] if begin else [total]))

    total = cand_part(kvq[:1], None, False, (passing,))
    att, stats = call(
        hist_forward, "hist_forward", (1,), [SMEM] + [held] * 9,
        [shaped((512, 128), F32), shaped((8, 512), F32)], [held] * 2,
        [pltpu.VMEM((512, 128), F32)], 1_400_000_000, (total,),
    )(info, *parts, *kvq)
    all_stats = [stats] + [turned(stats, "y", 4, k) for k in (1, 2, 3)]
    total = cand_part(kvq[1:3], total, False, (stats,))
    ga, mg = call(
        normed_grads, "normed_grads", (1,), [SMEM] + [held] * 9,
        [shaped((512, 128)), shaped((512, 256))], [held] * 2,
        [pltpu.VMEM((512, 128), F32)] * 2, 1_000_000, (total,),
    )(info, *parts, att, *all_stats)

    ga_pair = packed(ga, across(ga))
    ga_near = along(ga_pair)
    dq = call(
        hist_dq, "hist_dq", (1,), [SMEM] + [held] * 6,
        shaped((4, 128, 128)), held, [], 2_000_000_000, (ga_pair,),
    )(info, ga, *kvq)
    ga_passing = unpacked(ga_near, (dq,))
    ga_third = along(ga_passing)
    gas = [ga_pair, ga_near, across(ga_near), ga_third, across(ga_third)]
    weighed = cand_part(kvq[3:], total, True, (ga_passing,))

    grads = call(
        hist_dkv, "hist_dkv", (1,), [SMEM] + [held] * 12,
        [shaped((128, 640))] * 4, [held] * 4, [pltpu.VMEM((4, 128, 640), BF)], 2_800_000_000,
        (weighed,),
    )(info, dq, mg, *kvq, *gas)
    back = [crossed(v, k) for k, v in enumerate(grads)]

    leaving = call(
        relay, "relay", (1,), [held], shaped((16, 128, 128)), held, [], 1_000_000, tuple(grads[:1])
    )(weighed)
    returned = lax.all_to_all(leaving, ("xl", "xh", "y"), 0, 0, tiled=True)

    hist_grad = call(
        grad_close, "grad_close", (1,), [SMEM] + [held] * 3 + [far] + [held] * 4,
        shaped((1, 128, 1024)), held, [pltpu.VMEM((4, 128, 512), BF)] + weights(4), 550_000_000,
        (leaving,),
    )(info, x_rows, cot, slope, w_proj, *back)
    hist_out = call(
        hist_close, "hist_close", (1,), [SMEM] + [held] * 6,
        shaped((1, 128, 1024)), held, [pltpu.VMEM((128, 512), BF)], 140_000_000, (hist_grad,),
    )(info, x_rows, w_out, *back)
    cand_out = call(
        cand_close, "cand_close", (1,), [held] * 5,
        shaped((256, 1024)), held, [], 400_000_000, (hist_out,),
    )(cand_loop, cand_x, cand_gate, w_out, returned)
    return hist_out, hist_grad, cand_out


def solution(mesh):
    split = Mesh(mesh.devices.reshape(2, 2, 4, 2, 4), ("xl", "c", "y", "xh", "z"))
    users, rows = ("xl", "c"), ("y", "xh", "z")
    hist = P(users, rows, None)
    cand = P(users + rows, None)
    return jax.shard_map(
        per_device,
        mesh=split,
        in_specs=(hist, hist, cand, cand, P(users), P(), P()),
        out_specs=(hist, hist, cand),
        check_vma=False,
    )
```

```python
import functools

import jax
import jax.numpy as jnp
from jax import lax
from jax.experimental import pallas as pl
from jax.experimental.pallas import tpu as pltpu
from jax.sharding import Mesh, PartitionSpec as P

HS = 128
CAP = 128
HEADS = 4
EPS = 1e-05
SCALE = HS ** (-0.5)
BF = jnp.bfloat16
F32 = jnp.float32

NN = (((1,), (0,)), ((), ()))
NT = (((1,), (1,)), ((), ()))
SMEM = pl.BlockSpec(memory_space=pltpu.SMEM)


def dot(a, b, dims=NN):
    return lax.dot_general(a, b, dims, preferred_element_type=F32)


def whole(shape):
    return pl.BlockSpec(memory_space=pltpu.VMEM)


def call(body, name, grid, in_specs, outs, out_specs, scratch, flops, after=(), limit=12, carry=()):
    count, extra = len(in_specs), len(after) + len(carry)
    single = not isinstance(outs, (list, tuple))
    outs = [outs] if single else list(outs)
    out_specs = [out_specs] if single else list(out_specs)
    kept = len(outs)
    anywhere = pl.BlockSpec(memory_space=pl.ANY)

    def without(*refs):
        first = count + extra
        return body(*refs[:count], *refs[first : first + kept], *refs[first + kept + len(carry) :])

    made = pl.pallas_call(
        without,
        out_shape=outs + [jax.ShapeDtypeStruct(v.shape, v.dtype) for v in carry],
        grid=grid,
        in_specs=list(in_specs) + [anywhere] * extra,
        out_specs=out_specs + [anywhere] * len(carry),
        input_output_aliases={count + len(after) + n: kept + n for n in range(len(carry))},
        scratch_shapes=scratch,
        compiler_params=pltpu.CompilerParams(vmem_limit_bytes=limit * 1024 * 1024),
        cost_estimate=pl.CostEstimate(flops=flops, transcendentals=0, bytes_accessed=1 << 20),
        name=name,
    )

    def run(*args):
        pinned = []
        for arg, spec in zip(args, in_specs):
            if spec is not SMEM:
                space = spec.memory_space or pltpu.VMEM
                arg = pltpu.with_memory_space_constraint(arg, space)
            pinned.append(arg)
        got = made(*pinned, *after, *carry)
        return got[0] if len(got) == 1 and single else got

    return run


def shaped(shape, dtype=BF):
    return pltpu.VMEM(shape, dtype)


def normalize(values):
    center = values - jnp.mean(values, axis=-1, keepdims=True)
    spread = lax.rsqrt(jnp.mean(center * center, axis=-1, keepdims=True) + EPS)
    return center * spread, spread


def silu_parts(pre):
    half = 0.5 * pre
    sig = 0.5 + 0.5 * jnp.tanh(half)
    act = pre * sig
    return act, sig + act * (1.0 - sig)


def columns(w_ref, buf, sems, picks):
    copies = []
    for slot, pick in enumerate(picks):
        copy = pltpu.make_async_copy(w_ref.at[:, pl.ds(512 * pick, 512)], buf.at[slot], sems.at[slot])
        copy.start()
        copies.append(copy)
    return copies


def slot_ids(ids_ref):
    col = ids_ref[...]
    first = lax.broadcasted_iota(jnp.int32, (256, 256), 0)
    second = lax.broadcasted_iota(jnp.int32, (256, 256), 1)
    row = jnp.sum(jnp.where(first == second, col, 0), axis=0, keepdims=True)
    return col, row, first, second


def fetched(pairs, sems):
    copies = []
    for slot, (source, target) in enumerate(pairs):
        copy = pltpu.make_async_copy(source, target, sems.at[slot])
        copy.start()
        copies.append(copy)
    return copies


def project_all(
    info, x_far, cot_far, wo_far, w_ref, k0, k1, k2, k3, slope_ref,
    xn_ref, act_ref, x_ref, cot_ref, wo_ref, few, buf, sems,
):
    (got_x,) = fetched([(x_far, x_ref)], few)
    copies = columns(w_ref, buf, sems, (3, 1, 2, 0))
    rest = fetched([(cot_far, cot_ref), (wo_far, wo_ref)], few.at[pl.ds(1, 2)])
    got_x.wait()
    normed, _ = normalize(x_ref[...].astype(F32))
    xn_ref[...] = normed.astype(BF)
    rows = info[1] + lax.broadcasted_iota(jnp.int32, (128, 1), 0)
    inside = jnp.where(rows < info[0], 1.0, 0.0)
    length = jnp.full((128, 1), info[0], jnp.int32).astype(F32)

    def put(values, part):
        act_ref[...] = values.astype(BF)
        for k, out in enumerate((k0, k1, k2, k3)):
            lane = pl.multiple_of(((info[2] + k) & 3) * HS, HS)
            out[:, part * HS : (part + 1) * HS] = act_ref[:, pl.ds(lane, HS)]

    for part in range(4):
        copies[part].wait()
        act, slope = silu_parts(dot(xn_ref[...], buf[part]))
        slope_ref[part] = slope.astype(BF)
        put(act * (inside, inside / length, 0.5 * SCALE, 1.0)[part], part)
    for copy in rest:
        copy.wait()
    put(dot(cot_ref[...], wo_ref[...], NT), 4)


def arrange(info, a0, a1, a2, a3, out_ref):
    for k, a in enumerate((a0, a1, a2, a3)):
        out_ref[(info[2] - k) & 3] = a[:, : 3 * HS]


def project_cand(ids_ref, x_ref, w_ref, sent_ref, gate_ref, xn_ref, buf, sems):
    copies = columns(w_ref, buf, sems, (2, 0))
    xn_ref[...] = normalize(x_ref[...].astype(F32))[0].astype(BF)
    col, row, first, second = slot_ids(ids_ref)
    rank = jnp.sum(jnp.where((col == row) & (first < second), 1, 0), axis=0, keepdims=True)
    slot = row * CAP + rank
    hits = (lax.broadcasted_iota(jnp.int32, (4 * CAP, 256), 0) == slot).astype(F32).astype(BF)
    copies[0].wait()
    act, _ = silu_parts(dot(xn_ref[...], buf[0]))
    placed = dot(hits, (act * (0.5 * SCALE)).astype(BF)).astype(BF)
    for u in range(4):
        for h in range(HEADS):
            sent_ref[u * HEADS + h] = placed[u * CAP : (u + 1) * CAP, h * HS : (h + 1) * HS]
    copies[1].wait()
    act, _ = silu_parts(dot(xn_ref[...], buf[1]))
    gate_ref[...] = act.astype(BF)


def nothing(*refs):
    del refs


def order_of(info):
    c, z = info[3], info[4]
    o = 1 - c
    side = 1 - 2 * c
    near, far = (z - side) & 3, (z + side) & 3
    across = (z + 2) & 3
    spots = [(c, z), (o, z), (c, near), (o, far), (c, far), (o, near), (c, across), (o, across)]
    return [4 * core + spot for core, spot in spots]


def corner_masks(info, backward):
    order = order_of(info)
    first = lax.broadcasted_iota(jnp.int32, (128, 128), 0)
    second = lax.broadcasted_iota(jnp.int32, (128, 128), 1)
    masks = []
    for o in order:
        ahead = o > order[0] if backward else o < order[0]
        lead = jnp.where(ahead, 128, jnp.where(o == order[0], 0, -128))
        keep = first <= second + lead if backward else second <= first + lead
        masks.append(keep.astype(F32).astype(BF))
    return masks


def cand_attend(count, begin, end, *refs):
    q_ref, kvs, rest = refs[0], refs[1 : 1 + count], refs[1 + count :]
    q = q_ref[...].reshape(4 * CAP, HS)
    total = None if begin else rest[0][...]
    for block in kvs:
        half = dot(q, block[:, :HS], NT).astype(BF)
        probs = half + half * jnp.tanh(half)
        more = dot(probs, block[:, HS : 2 * HS])
        total = more if total is None else total + more
    if end:
        rest[-1][...] = total.astype(BF).reshape(4, CAP, HS)
    else:
        rest[-1][...] = total


def attend_rows(q_ref, blocks, masks, old_ref, att_ref):
    for y in range(4):
        rows = slice(y * 128, (y + 1) * 128)
        q = q_ref[rows, 2 * HS :]
        total = None if old_ref is None else old_ref[rows, :]
        for block, mask in zip(blocks, masks):
            half = dot(q, block[: 128 * (y + 1), :HS], NT).astype(BF)
            probs = half + half * jnp.tanh(half)
            last = probs[:, 128 * y :] * mask
            probs = last if y == 0 else jnp.concatenate([probs[:, : 128 * y], last], axis=1)
            more = dot(probs, block[: 128 * (y + 1), HS : 2 * HS])
            total = more if total is None else total + more
        att_ref[rows, :] = total


def hist_begin(info, *refs):
    attend_rows(refs[0], refs[:6], corner_masks(info, False)[:6], None, refs[6])


def hist_end(info, p0, p1, p2, p3, own_ref, b0, b1, old_ref, att_ref, stat_ref, g_ref):
    for k, part in enumerate((p0, p1, p2, p3)):
        rows = pl.ds(pl.multiple_of(((info[2] - k) & 3) * 128, 128), 128)
        g_ref[rows, :] = part[:, 3 * HS : 4 * HS].astype(F32) * part[:, 4 * HS :].astype(F32)
    attend_rows(own_ref, (b0, b1), corner_masks(info, False)[6:], old_ref, att_ref)
    att = att_ref[...]
    g = g_ref[...]
    mean = jnp.mean(att, axis=1, keepdims=True)
    center = att - mean
    lane = lax.broadcasted_iota(jnp.int32, (512, 128), 1)
    stats = jnp.where(lane == 0, mean, 0.0)
    stats = jnp.where(lane == 1, jnp.sum(center * center, axis=1, keepdims=True), stats)
    stats = jnp.where(lane == 2, jnp.sum(g, axis=1, keepdims=True), stats)
    stats = jnp.where(lane == 3, jnp.sum(g * center, axis=1, keepdims=True), stats)
    stat_ref[...] = jnp.transpose(stats)[:8]


def normed_grads(info, p0, p1, p2, p3, att_ref, s0, s1, s2, s3, ga_ref, mg_ref, gate_ref, gm_ref):
    for k, part in enumerate((p0, p1, p2, p3)):
        y = (info[2] - k) & 3
        rows = pl.ds(pl.multiple_of(y * 128, 128), 128)
        gate_ref[rows, :] = part[:, 3 * HS : 4 * HS].astype(F32)
        gm_ref[rows, :] = part[:, 4 * HS :].astype(F32)
    stats = [s[...] for s in (s0, s1, s2, s3)]
    mean = sum(s[0:1] for s in stats) * 0.25
    squares = sum(s[1:2] + HS * (s[0:1] - mean) * (s[0:1] - mean) for s in stats)
    spread = lax.rsqrt(squares * (1.0 / (HEADS * HS)) + EPS)
    g_mean = sum(s[2:3] for s in stats) * (1.0 / (HEADS * HS))
    ga_sum = sum(s[3:4] + s[2:3] * (s[0:1] - mean) for s in stats)
    ga_mean = ga_sum * spread * (1.0 / (HEADS * HS))
    line = lax.broadcasted_iota(jnp.int32, (128, 512), 0)
    packed = jnp.where(line == 0, mean, 0.0)
    packed = jnp.where(line == 1, spread, packed)
    packed = jnp.where(line == 2, g_mean, packed)
    packed = jnp.where(line == 3, ga_mean, packed)
    cols = jnp.transpose(packed)
    spread_c = cols[:, 1:2]
    normed = (att_ref[...] - cols[:, 0:1]) * spread_c
    gate = gate_ref[...]
    gm = gm_ref[...]
    ga_ref[...] = (spread_c * (gate * gm - cols[:, 2:3] - normed * cols[:, 3:4])).astype(BF)
    mg_ref[:, :HS] = (normed * gate).astype(BF)
    mg_ref[:, HS:] = (normed * gm).astype(BF)


def slope_times(half, grads):
    t = jnp.tanh(half)
    probs = half + half * t
    slope = (1.0 + t + probs * (1.0 - t)).astype(BF)
    return probs, grads * slope


def hist_dq(info, ga_ref, *refs):
    blocks, dq_ref = refs[:8], refs[8]
    masks = corner_masks(info, False)
    for y in range(4):
        q = blocks[0][y * 128 : (y + 1) * 128, 2 * HS :]
        ga = ga_ref[y * 128 : (y + 1) * 128, :]
        total = None
        for block, mask in zip(blocks, masks):
            key = block[: 128 * (y + 1), :HS]
            half = dot(q, key, NT).astype(BF)
            _, ds = slope_times(half, dot(ga, block[: 128 * (y + 1), HS : 2 * HS], NT).astype(BF))
            last = ds[:, 128 * y :] * mask
            ds = last if y == 0 else jnp.concatenate([ds[:, : 128 * y], last], axis=1)
            more = dot(ds, key)
            total = more if total is None else total + more
        dq_ref[y] = (total * (0.5 * SCALE)).astype(BF)


def key_grads(own_ref, blocks, gas, masks, y, dk, dv):
    key = own_ref[y * 128 : (y + 1) * 128, :HS]
    value = own_ref[y * 128 : (y + 1) * 128, HS : 2 * HS]
    for block, ga_block, mask in zip(blocks, gas, masks):
        q = block[128 * y :, 2 * HS :]
        ga = ga_block[128 * y :, :]
        half = dot(key, q, NT).astype(BF)
        probs, ds = slope_times(half, dot(value, ga, NT).astype(BF))
        p_first = probs[:, :128] * mask
        d_first = ds[:, :128] * mask
        if y < 3:
            probs = jnp.concatenate([p_first, probs[:, 128:]], axis=1)
            ds = jnp.concatenate([d_first, ds[:, 128:]], axis=1)
        else:
            probs, ds = p_first, d_first
        more_k = dot(ds, q)
        more_v = dot(probs, ga)
        dk = more_k if dk is None else dk + more_k
        dv = more_v if dv is None else dv + more_v
    return dk, dv


def hist_dkv_begin(info, *refs):
    masks = corner_masks(info, True)[:6]
    for y in range(4):
        dk, dv = key_grads(refs[0], refs[:6], refs[6:12], masks, y, None, None)
        refs[12][y, :, :HS] = dk
        refs[12][y, :, HS:] = dv


def hist_dkv_end(info, dq_ref, mg_ref, own_ref, b0, b1, g0, g1, old_ref, k0, k1, k2, k3, all_ref):
    masks = corner_masks(info, True)[6:]
    for y in range(4):
        dk, dv = key_grads(own_ref, (b0, b1), (g0, g1), masks, y, old_ref[y, :, :HS], old_ref[y, :, HS:])
        all_ref[y, :, :HS] = dq_ref[y]
        all_ref[y, :, HS : 2 * HS] = dk.astype(BF)
        all_ref[y, :, 2 * HS : 3 * HS] = dv.astype(BF)
        all_ref[y, :, 3 * HS :] = mg_ref[y * 128 : (y + 1) * 128, :]
    for k, out in enumerate((k0, k1, k2, k3)):
        out[...] = all_ref[(info[2] + k) & 3]


def hist_close(
    info, x_far, cot_far, slope_far, wo_far, w_ref, b0, b1, b2, b3, out_far, grad_far,
    mixed_ref, hid_ref, out_ref, grad_ref, x_ref, cot_ref, slope_ref, wo_ref, most, few, buf, sems,
):
    got = fetched([(slope_far, slope_ref), (wo_far, wo_ref), (x_far, x_ref)], most)
    copies = columns(w_ref, buf, sems, (0, 1, 2, 3))
    got += fetched([(cot_far, cot_ref)], most.at[pl.ds(3, 1)])
    length = jnp.full((128, 1), info[0], jnp.int32).astype(F32)
    got[0].wait()
    for k, b in enumerate((b0, b1, b2, b3)):
        lanes = pl.ds(pl.multiple_of(((info[2] - k) & 3) * HS, HS), HS)

        def put(part, grads, which):
            hid_ref[part, :, lanes] = (grads * slope_ref[which, :, lanes].astype(F32)).astype(BF)

        put(0, b[:, 4 * HS :].astype(F32), 3)
        put(1, b[:, 2 * HS : 3 * HS].astype(F32) / length, 1)
        put(2, b[:, :HS].astype(F32), 2)
        put(3, b[:, HS : 2 * HS].astype(F32), 0)
        mixed_ref[:, lanes] = b[:, 3 * HS : 4 * HS]
    got[1].wait()
    got[2].wait()
    x = x_ref[...].astype(F32)
    out_ref[...] = (x + dot(mixed_ref[...], wo_ref[...])).astype(BF)
    done = fetched([(out_ref, out_far.at[0])], few)
    e = None
    for part in range(4):
        copies[part].wait()
        more = dot(hid_ref[part], buf[part], NT)
        e = more if e is None else e + more
    normed, spread = normalize(x)
    back = spread * (
        e - jnp.mean(e, axis=-1, keepdims=True) - normed * jnp.mean(e * normed, axis=-1, keepdims=True)
    )
    got[3].wait()
    grad_ref[...] = (cot_ref[...].astype(F32) + back).astype(BF)
    done += fetched([(grad_ref, grad_far.at[0])], few.at[pl.ds(1, 1)])
    for copy in done:
        copy.wait()


def cand_close(ids_ref, gate_far, ret_ref, x_far, wo_far, out_ref, gate_ref, x_ref, wo_ref, few):
    copies = fetched([(gate_far, gate_ref), (wo_far, wo_ref), (x_far, x_ref)], few)
    col, row, first, second = slot_ids(ids_ref)
    rank = jnp.sum(jnp.where((col == row) & (second < first), 1, 0), axis=1, keepdims=True)
    slot = col * CAP + rank
    hits = (lax.broadcasted_iota(jnp.int32, (256, 4 * CAP), 1) == slot).astype(F32).astype(BF)
    heads = []
    for h in range(HEADS):
        rows = jnp.concatenate([ret_ref[u * HEADS + h] for u in range(4)], axis=0)
        heads.append(dot(hits, rows))
    normed, _ = normalize(jnp.concatenate(heads, axis=1))
    copies[0].wait()
    mixed = (normed * gate_ref[...].astype(F32)).astype(BF)
    copies[1].wait()
    more = dot(mixed, wo_ref[...])
    copies[2].wait()
    out_ref[...] = (x_ref[...].astype(F32) + more).astype(BF)


def turned(value, axis, size, steps):
    return lax.ppermute(value, axis, [(i, (i + steps) % size) for i in range(size)])


def crossed(value, steps):
    pairs = []
    for c in range(2):
        for y in range(4):
            for xh in range(2):
                pairs.append(((c * 4 + y) * 2 + xh, (xh * 4 + (y + steps) % 4) * 2 + c))
    return lax.ppermute(value, ("c", "y", "xh"), pairs)


def across(value):
    return lax.ppermute(value, "c", [(0, 1), (1, 0)])


def along(value, way, cross):
    pairs = []
    for c in range(2):
        step = way if c == 0 else -way
        for z in range(4):
            pairs.append((4 * c + z, 4 * (c ^ cross) + (z + step) % 4))
    return lax.ppermute(value, ("c", "z"), pairs)


def per_device(hist_x, hist_cot, cand_x, cand_loop, hist_len, w_proj, w_out):
    y, xh, z, c = (lax.axis_index(n) for n in ("y", "xh", "z", "c"))
    x_rows = hist_x.reshape(128, 1024)
    cot = hist_cot.reshape(128, 1024)
    info = jnp.stack([hist_len[0], (y * 8 + xh * 4 + z) * 128, y, c, z]).astype(jnp.int32)
    held = pl.BlockSpec(memory_space=pltpu.VMEM)
    far = pl.BlockSpec(memory_space=pltpu.HBM)

    def weights(count):
        return [pltpu.VMEM((count, 1024, 512), BF), pltpu.SemaphoreType.DMA((count,))]

    def relayed(values, after):
        return call(nothing, "relay", (1,), [], [], [], [], 1_000, after, carry=values)()

    *sent, slope = call(
        project_all, "project_all", (1,), [SMEM, far, far, far, far],
        [shaped((128, 640))] * 4 + [shaped((4, 128, 512))], [held] * 5,
        [
            pltpu.VMEM((128, 1024), BF), pltpu.VMEM((128, 512), BF), pltpu.VMEM((128, 1024), BF),
            pltpu.VMEM((128, 1024), BF), pltpu.VMEM((512, 1024), BF), pltpu.SemaphoreType.DMA((3,)),
        ] + weights(4), 700_000_000, (), 16,
    )(info, x_rows, cot, w_out, w_proj)
    parts = [crossed(v, k) for k, v in enumerate(sent)]

    sent_cand, cand_gate = call(
        project_cand, "project_cand", (1,), [held, held, far],
        [shaped((16, 128, 128)), shaped((256, 512))], [held] * 2,
        [pltpu.VMEM((256, 1024), BF)] + weights(2), 700_000_000, (slope,),
    )(cand_loop, cand_x, w_proj)

    own, sent_cand = call(
        arrange, "arrange", (1,), [SMEM] + [held] * 4, shaped((4, 128, 384)), held, [], 1_000_000,
        (cand_gate,), carry=(sent_cand,),
    )(info, *parts)
    own = own.reshape(512, 384)
    own_pair = across(own)
    plus, minus = along(own, 1, 0), along(own, -1, 0)
    arrived = lax.all_to_all(sent_cand, ("xl", "xh", "y"), 0, 0, tiled=True)
    last = [along(plus, 1, 0), along(plus, 1, 1)]
    kvq = [own, own_pair, plus, across(plus), minus, across(minus)]

    q_spec = pl.BlockSpec((4, 128, 128), lambda i: (i, 0, 0))
    acc_spec = pl.BlockSpec((512, 128), lambda i: (i, 0))

    def cand_part(kvs, total, end, after):
        begin = total is None
        return call(
            functools.partial(cand_attend, len(kvs), begin, end), "cand_attend", (4,),
            [q_spec] + [held] * len(kvs) + ([] if begin else [acc_spec]),
            shaped((16, 128, 128)) if end else shaped((2048, 128), F32),
            q_spec if end else acc_spec, [], 600_000_000 * len(kvs), after,
        )(arrived, *kvs, *([] if begin else [total]))

    total = cand_part(kvq, None, False, ())
    att = call(
        hist_begin, "hist_begin", (1,), [SMEM] + [held] * 6,
        shaped((512, 128), F32), held, [], 1_400_000_000, (total,),
    )(info, *kvq)
    att, stats = call(
        hist_end, "hist_end", (1,), [SMEM] + [held] * 8,
        [shaped((512, 128), F32), shaped((8, 512), F32)], [held] * 2,
        [pltpu.VMEM((512, 128), F32)], 400_000_000,
    )(info, *parts, own, *last, att)
    all_stats = [stats] + [turned(stats, "y", 4, k) for k in (1, 2, 3)]
    weighed = cand_part(last, total, True, (stats,))
    ga, mg = call(
        normed_grads, "normed_grads", (1,), [SMEM] + [held] * 9,
        [shaped((512, 128)), shaped((512, 256))], [held] * 2,
        [pltpu.VMEM((512, 128), F32)] * 2, 1_000_000, (weighed,),
    )(info, *parts, att, *all_stats)

    ga_plus, ga_minus = along(ga, 1, 0), along(ga, -1, 0)
    dq = call(
        hist_dq, "hist_dq", (1,), [SMEM] + [held] * 9,
        shaped((4, 128, 128)), held, [], 2_000_000_000,
    )(info, ga, *kvq, *last)
    ga_plus, ga_minus = relayed([ga_plus, ga_minus], (dq,))
    ga_last = [along(ga_plus, 1, 0), along(ga_plus, 1, 1)]
    gas = [ga, across(ga), ga_plus, across(ga_plus), ga_minus, across(ga_minus)]
    key_sums = call(
        hist_dkv_begin, "hist_dkv_begin", (1,), [SMEM] + [held] * 12,
        shaped((4, 128, 256), F32), held, [], 2_000_000_000,
    )(info, *kvq, *gas)
    (leaving,) = relayed([weighed], (key_sums,))
    returned = lax.all_to_all(leaving, ("xl", "xh", "y"), 0, 0, tiled=True)
    grads = call(
        hist_dkv_end, "hist_dkv_end", (1,), [SMEM] + [held] * 8,
        [shaped((128, 640))] * 4, [held] * 4, [pltpu.VMEM((4, 128, 640), BF)], 800_000_000,
    )(info, dq, mg, own, *last, *ga_last, key_sums)
    back = [crossed(v, k) for k, v in enumerate(grads)]

    cand_out = call(
        cand_close, "cand_close", (1,), [held, far, held, far, far],
        pltpu.HBM((256, 1024), BF), pl.BlockSpec((256, 1024), lambda i: (0, 0)),
        [
            pltpu.VMEM((256, 512), BF), pltpu.VMEM((256, 1024), BF), pltpu.VMEM((512, 1024), BF),
            pltpu.SemaphoreType.DMA((3,)),
        ], 400_000_000, (grads[0],),
    )(cand_loop, cand_gate, returned, cand_x, w_out)
    final = pltpu.HBM((1, 128, 1024), BF)
    hist_out, hist_grad = call(
        hist_close, "hist_close", (1,), [SMEM] + [far] * 5 + [held] * 4,
        [final] * 2, [far] * 2,
        [
            pltpu.VMEM((128, 512), BF), pltpu.VMEM((4, 128, 512), BF), pltpu.VMEM((128, 1024), BF),
            pltpu.VMEM((128, 1024), BF), pltpu.VMEM((128, 1024), BF), pltpu.VMEM((128, 1024), BF),
            pltpu.VMEM((4, 128, 512), BF), pltpu.VMEM((512, 1024), BF), pltpu.SemaphoreType.DMA((4,)),
            pltpu.SemaphoreType.DMA((2,)),
        ] + weights(4), 700_000_000, (pltpu.with_memory_space_constraint(cand_out, pltpu.HBM),), 16,
    )(info, x_rows, cot, slope, w_out, w_proj, *back)
    return hist_out, hist_grad, cand_out


def solution(mesh):
    split = Mesh(mesh.devices.reshape(2, 2, 4, 2, 4), ("xl", "c", "y", "xh", "z"))
    users, rows = ("xl", "c"), ("y", "xh", "z")
    hist = P(users, rows, None)
    cand = P(users + rows, None)
    return jax.shard_map(
        per_device,
        mesh=split,
        in_specs=(hist, hist, cand, cand, P(users), P(), P()),
        out_specs=(hist, hist, cand),
        check_vma=False,
    )
```

```python
import functools

import jax
import jax.numpy as jnp
from jax import lax
from jax.experimental import pallas as pl
from jax.experimental.pallas import tpu as pltpu
from jax.sharding import Mesh, PartitionSpec as P

HS = 128
CAP = 128
HEADS = 4
EPS = 1e-05
SCALE = HS ** (-0.5)
BF = jnp.bfloat16
F32 = jnp.float32

NN = (((1,), (0,)), ((), ()))
NT = (((1,), (1,)), ((), ()))
SMEM = pl.BlockSpec(memory_space=pltpu.SMEM)


def dot(a, b, dims=NN):
    return lax.dot_general(a, b, dims, preferred_element_type=F32)


def whole(shape):
    return pl.BlockSpec(memory_space=pltpu.VMEM)


def call(body, name, grid, in_specs, outs, out_specs, scratch, flops, after=(), limit=12, carry=()):
    count, extra = len(in_specs), len(after) + len(carry)
    single = not isinstance(outs, (list, tuple))
    outs = [outs] if single else list(outs)
    out_specs = [out_specs] if single else list(out_specs)
    kept = len(outs)
    anywhere = pl.BlockSpec(memory_space=pl.ANY)

    def without(*refs):
        first = count + extra
        return body(*refs[:count], *refs[first : first + kept], *refs[first + kept + len(carry) :])

    made = pl.pallas_call(
        without,
        out_shape=outs + [jax.ShapeDtypeStruct(v.shape, v.dtype) for v in carry],
        grid=grid,
        in_specs=list(in_specs) + [anywhere] * extra,
        out_specs=out_specs + [anywhere] * len(carry),
        input_output_aliases={count + len(after) + n: kept + n for n in range(len(carry))},
        scratch_shapes=scratch,
        compiler_params=pltpu.CompilerParams(vmem_limit_bytes=limit * 1024 * 1024),
        cost_estimate=pl.CostEstimate(flops=flops, transcendentals=0, bytes_accessed=(1 << 20) if flops > 1000 else 1000),
        name=name,
    )

    def run(*args):
        pinned = []
        for arg, spec in zip(args, in_specs):
            if spec is not SMEM:
                space = spec.memory_space or pltpu.VMEM
                arg = pltpu.with_memory_space_constraint(arg, space)
            pinned.append(arg)
        got = made(*pinned, *after, *carry)
        return got[0] if len(got) == 1 and single else got

    return run


def shaped(shape, dtype=BF):
    return pltpu.VMEM(shape, dtype)


def normalize(values):
    center = values - jnp.mean(values, axis=-1, keepdims=True)
    spread = lax.rsqrt(jnp.mean(center * center, axis=-1, keepdims=True) + EPS)
    return center * spread, spread


def silu_parts(pre):
    half = 0.5 * pre
    sig = 0.5 + 0.5 * jnp.tanh(half)
    act = pre * sig
    return act, sig + act * (1.0 - sig)


def columns(w_ref, buf, sems, picks):
    copies = []
    for slot, pick in enumerate(picks):
        copy = pltpu.make_async_copy(w_ref.at[:, pl.ds(512 * pick, 512)], buf.at[slot], sems.at[slot])
        copy.start()
        copies.append(copy)
    return copies


def slot_ids(ids_ref):
    col = ids_ref[...]
    first = lax.broadcasted_iota(jnp.int32, (256, 256), 0)
    second = lax.broadcasted_iota(jnp.int32, (256, 256), 1)
    row = jnp.sum(jnp.where(first == second, col, 0), axis=0, keepdims=True)
    return col, row, first, second


def fetched(pairs, sems):
    copies = []
    for slot, (source, target) in enumerate(pairs):
        copy = pltpu.make_async_copy(source, target, sems.at[slot])
        copy.start()
        copies.append(copy)
    return copies


def project_all(
    info, x_far, cot_far, wo_far, w_ref, k0, k1, k2, k3, slope_ref, gate_ref, gm_ref,
    xn_ref, act_ref, x_ref, cot_ref, wo_ref, few, buf, sems,
):
    (got_x,) = fetched([(x_far, x_ref)], few)
    copies = columns(w_ref, buf, sems, (3, 1, 2, 0))
    rest = fetched([(cot_far, cot_ref), (wo_far, wo_ref)], few.at[pl.ds(1, 2)])
    got_x.wait()
    normed, _ = normalize(x_ref[...].astype(F32))
    xn_ref[...] = normed.astype(BF)
    rows = info[1] + lax.broadcasted_iota(jnp.int32, (128, 1), 0)
    inside = jnp.where(rows < info[0], 1.0, 0.0)
    length = jnp.full((128, 1), info[0], jnp.int32).astype(F32)

    def put(values, part):
        act_ref[...] = values.astype(BF)
        for k, out in enumerate((k0, k1, k2, k3)):
            lane = pl.multiple_of(((info[2] + k) & 3) * HS, HS)
            out[:, part * HS : (part + 1) * HS] = act_ref[:, pl.ds(lane, HS)]

    for part in range(4):
        copies[part].wait()
        act, slope = silu_parts(dot(xn_ref[...], buf[part]))
        slope_ref[part] = slope.astype(BF)
        if part < 3:
            put(act * (inside, inside / length, 0.5 * SCALE)[part], part)
    gate_ref[...] = act.astype(BF)
    for copy in rest:
        copy.wait()
    gm = dot(cot_ref[...], wo_ref[...], NT)
    gm_ref[...] = gm.astype(BF)
    put(gm * gate_ref[...].astype(F32), 3)


def arrange(info, a0, a1, a2, a3, out_ref):
    for k, a in enumerate((a0, a1, a2, a3)):
        out_ref[(info[2] - k) & 3] = a[:, : 3 * HS]


def project_cand(ids_ref, x_ref, w_ref, sent_ref, gate_ref, xn_ref, buf, sems):
    copies = columns(w_ref, buf, sems, (2, 0))
    xn_ref[...] = normalize(x_ref[...].astype(F32))[0].astype(BF)
    col, row, first, second = slot_ids(ids_ref)
    rank = jnp.sum(jnp.where((col == row) & (first < second), 1, 0), axis=0, keepdims=True)
    slot = row * CAP + rank
    hits = (lax.broadcasted_iota(jnp.int32, (4 * CAP, 256), 0) == slot).astype(F32).astype(BF)
    copies[0].wait()
    act, _ = silu_parts(dot(xn_ref[...], buf[0]))
    placed = dot(hits, (act * (0.5 * SCALE)).astype(BF)).astype(BF)
    for u in range(4):
        for h in range(HEADS):
            sent_ref[u * HEADS + h] = placed[u * CAP : (u + 1) * CAP, h * HS : (h + 1) * HS]
    copies[1].wait()
    act, _ = silu_parts(dot(xn_ref[...], buf[1]))
    gate_ref[...] = act.astype(BF)


def nothing(*refs):
    del refs


def order_of(info):
    c, z = info[3], info[4]
    o = 1 - c
    side = 1 - 2 * c
    near, far = (z - side) & 3, (z + side) & 3
    across = (z + 2) & 3
    spots = [(c, z), (o, z), (c, near), (o, far), (c, far), (o, near), (c, across), (o, across)]
    return [4 * core + spot for core, spot in spots]


def corner_masks(info, backward):
    order = order_of(info)
    first = lax.broadcasted_iota(jnp.int32, (128, 128), 0)
    second = lax.broadcasted_iota(jnp.int32, (128, 128), 1)
    masks = []
    for o in order:
        ahead = o > order[0] if backward else o < order[0]
        lead = jnp.where(ahead, 128, jnp.where(o == order[0], 0, -128))
        keep = first <= second + lead if backward else second <= first + lead
        masks.append(keep.astype(F32).astype(BF))
    return masks


def cand_attend(count, begin, end, *refs):
    q_ref, kvs, rest = refs[0], refs[1 : 1 + count], refs[1 + count :]
    q = q_ref[...].reshape(4 * CAP, HS)
    total = None if begin else rest[0][...]
    for block in kvs:
        half = dot(q, block[:, :HS], NT).astype(BF)
        probs = half + half * jnp.tanh(half)
        more = dot(probs, block[:, HS : 2 * HS])
        total = more if total is None else total + more
    if end:
        rest[-1][...] = total.astype(BF).reshape(4, CAP, HS)
    else:
        rest[-1][...] = total


def attend_rows(q_ref, blocks, masks, old_ref, att_ref):
    for y in range(4):
        rows = slice(y * 128, (y + 1) * 128)
        q = q_ref[rows, 2 * HS :]
        total = None if old_ref is None else old_ref[rows, :]
        for block, mask in zip(blocks, masks):
            half = dot(q, block[: 128 * (y + 1), :HS], NT).astype(BF)
            probs = half + half * jnp.tanh(half)
            last = probs[:, 128 * y :] * mask
            probs = last if y == 0 else jnp.concatenate([probs[:, : 128 * y], last], axis=1)
            more = dot(probs, block[: 128 * (y + 1), HS : 2 * HS])
            total = more if total is None else total + more
        att_ref[rows, :] = total


def hist_begin(info, *refs):
    attend_rows(refs[0], refs[:6], corner_masks(info, False)[:6], None, refs[6])


def hist_end(info, p0, p1, p2, p3, own_ref, b0, b1, old_ref, att_ref, stat_ref, g_ref):
    for k, part in enumerate((p0, p1, p2, p3)):
        rows = pl.ds(pl.multiple_of(((info[2] - k) & 3) * 128, 128), 128)
        g_ref[rows, :] = part[:, 3 * HS :].astype(F32)
    attend_rows(own_ref, (b0, b1), corner_masks(info, False)[6:], old_ref, att_ref)
    att = att_ref[...]
    g = g_ref[...]
    mean = jnp.mean(att, axis=1, keepdims=True)
    center = att - mean
    lane = lax.broadcasted_iota(jnp.int32, (512, 128), 1)
    stats = jnp.where(lane == 0, mean, 0.0)
    stats = jnp.where(lane == 1, jnp.sum(center * center, axis=1, keepdims=True), stats)
    stats = jnp.where(lane == 2, jnp.sum(g, axis=1, keepdims=True), stats)
    stats = jnp.where(lane == 3, jnp.sum(g * center, axis=1, keepdims=True), stats)
    stat_ref[...] = jnp.transpose(stats)[:8]


def normed_grads(info, p0, p1, p2, p3, att_ref, s0, s1, s2, s3, ga_ref, normed_ref, g_ref):
    for k, part in enumerate((p0, p1, p2, p3)):
        y = (info[2] - k) & 3
        rows = pl.ds(pl.multiple_of(y * 128, 128), 128)
        g_ref[rows, :] = part[:, 3 * HS :].astype(F32)
    stats = [s[...] for s in (s0, s1, s2, s3)]
    mean = sum(s[0:1] for s in stats) * 0.25
    squares = sum(s[1:2] + HS * (s[0:1] - mean) * (s[0:1] - mean) for s in stats)
    spread = lax.rsqrt(squares * (1.0 / (HEADS * HS)) + EPS)
    g_mean = sum(s[2:3] for s in stats) * (1.0 / (HEADS * HS))
    ga_sum = sum(s[3:4] + s[2:3] * (s[0:1] - mean) for s in stats)
    ga_mean = ga_sum * spread * (1.0 / (HEADS * HS))
    line = lax.broadcasted_iota(jnp.int32, (128, 512), 0)
    packed = jnp.where(line == 0, mean, 0.0)
    packed = jnp.where(line == 1, spread, packed)
    packed = jnp.where(line == 2, g_mean, packed)
    packed = jnp.where(line == 3, ga_mean, packed)
    cols = jnp.transpose(packed)
    spread_c = cols[:, 1:2]
    normed = (att_ref[...] - cols[:, 0:1]) * spread_c
    ga_ref[...] = (spread_c * (g_ref[...] - cols[:, 2:3] - normed * cols[:, 3:4])).astype(BF)
    normed_ref[...] = normed.astype(BF)


def slope_times(half, grads):
    t = jnp.tanh(half)
    probs = half + half * t
    slope = (1.0 + t + probs * (1.0 - t)).astype(BF)
    return probs, grads * slope


def hist_dq(info, ga_ref, *refs):
    blocks, dq_ref = refs[:8], refs[8]
    masks = corner_masks(info, False)
    for y in range(4):
        q = blocks[0][y * 128 : (y + 1) * 128, 2 * HS :]
        ga = ga_ref[y * 128 : (y + 1) * 128, :]
        total = None
        for block, mask in zip(blocks, masks):
            key = block[: 128 * (y + 1), :HS]
            half = dot(q, key, NT).astype(BF)
            _, ds = slope_times(half, dot(ga, block[: 128 * (y + 1), HS : 2 * HS], NT).astype(BF))
            last = ds[:, 128 * y :] * mask
            ds = last if y == 0 else jnp.concatenate([ds[:, : 128 * y], last], axis=1)
            more = dot(ds, key)
            total = more if total is None else total + more
        dq_ref[y] = (total * (0.5 * SCALE)).astype(BF)


def key_grads(own_ref, blocks, gas, masks, y, dk, dv):
    key = own_ref[y * 128 : (y + 1) * 128, :HS]
    value = own_ref[y * 128 : (y + 1) * 128, HS : 2 * HS]
    for block, ga_block, mask in zip(blocks, gas, masks):
        q = block[128 * y :, 2 * HS :]
        ga = ga_block[128 * y :, :]
        half = dot(key, q, NT).astype(BF)
        probs, ds = slope_times(half, dot(value, ga, NT).astype(BF))
        p_first = probs[:, :128] * mask
        d_first = ds[:, :128] * mask
        if y < 3:
            probs = jnp.concatenate([p_first, probs[:, 128:]], axis=1)
            ds = jnp.concatenate([d_first, ds[:, 128:]], axis=1)
        else:
            probs, ds = p_first, d_first
        more_k = dot(ds, q)
        more_v = dot(probs, ga)
        dk = more_k if dk is None else dk + more_k
        dv = more_v if dv is None else dv + more_v
    return dk, dv


def hist_dkv_begin(info, *refs):
    masks = corner_masks(info, True)[:6]
    for y in range(4):
        dk, dv = key_grads(refs[0], refs[:6], refs[6:12], masks, y, None, None)
        refs[12][y, :, :HS] = dk
        refs[12][y, :, HS:] = dv


def hist_dkv_end(info, dq_ref, normed_ref, own_ref, b0, b1, g0, g1, old_ref, k0, k1, k2, k3, all_ref):
    masks = corner_masks(info, True)[6:]
    for y in range(4):
        dk, dv = key_grads(own_ref, (b0, b1), (g0, g1), masks, y, old_ref[y, :, :HS], old_ref[y, :, HS:])
        all_ref[y, :, :HS] = dq_ref[y]
        all_ref[y, :, HS : 2 * HS] = dk.astype(BF)
        all_ref[y, :, 2 * HS : 3 * HS] = dv.astype(BF)
        all_ref[y, :, 3 * HS :] = normed_ref[y * 128 : (y + 1) * 128, :]
    for k, out in enumerate((k0, k1, k2, k3)):
        out[...] = all_ref[(info[2] + k) & 3]


def hist_close(
    info, x_ref, cot_ref, slope_ref, wo_ref, buf, gate_ref, gm_ref, b0, b1, b2, b3, out_far, grad_far,
    mixed_ref, hid_ref, out_ref, grad_ref, few,
):
    length = jnp.full((128, 1), info[0], jnp.int32).astype(F32)
    for k, b in enumerate((b0, b1, b2, b3)):
        lanes = pl.ds(pl.multiple_of(((info[2] - k) & 3) * HS, HS), HS)

        def put(part, grads, which):
            hid_ref[part, :, lanes] = (grads * slope_ref[which, :, lanes].astype(F32)).astype(BF)

        normed = b[:, 3 * HS :].astype(F32)
        put(0, normed * gm_ref[:, lanes].astype(F32), 3)
        put(1, b[:, 2 * HS : 3 * HS].astype(F32) / length, 1)
        put(2, b[:, :HS].astype(F32), 2)
        put(3, b[:, HS : 2 * HS].astype(F32), 0)
        mixed_ref[:, lanes] = (normed * gate_ref[:, lanes].astype(F32)).astype(BF)
    x = x_ref[...].astype(F32)
    out_ref[...] = (x + dot(mixed_ref[...], wo_ref[...])).astype(BF)
    done = fetched([(out_ref, out_far.at[0])], few)
    e = None
    for part in range(4):
        more = dot(hid_ref[part], buf[part], NT)
        e = more if e is None else e + more
    normed, spread = normalize(x)
    back = spread * (
        e - jnp.mean(e, axis=-1, keepdims=True) - normed * jnp.mean(e * normed, axis=-1, keepdims=True)
    )
    grad_ref[...] = (cot_ref[...].astype(F32) + back).astype(BF)
    done += fetched([(grad_ref, grad_far.at[0])], few.at[pl.ds(1, 1)])
    for copy in done:
        copy.wait()


def cand_close(
    ids_ref, gate_far, ret_ref, x_far, wo_far, w_far, hx_far, cot_far, out_ref, wo_ref, buf, hx_ref, cot_ref,
    gate_ref, x_ref, few, sems,
):
    copies = fetched([(gate_far, gate_ref), (wo_far, wo_ref), (x_far, x_ref)], few)
    later = columns(w_far, buf, sems, (0, 1, 2, 3))
    later += fetched([(hx_far, hx_ref), (cot_far, cot_ref)], few.at[pl.ds(3, 2)])
    col, row, first, second = slot_ids(ids_ref)
    rank = jnp.sum(jnp.where((col == row) & (second < first), 1, 0), axis=1, keepdims=True)
    slot = col * CAP + rank
    hits = (lax.broadcasted_iota(jnp.int32, (256, 4 * CAP), 1) == slot).astype(F32).astype(BF)
    heads = []
    for h in range(HEADS):
        rows = jnp.concatenate([ret_ref[u * HEADS + h] for u in range(4)], axis=0)
        heads.append(dot(hits, rows))
    normed, _ = normalize(jnp.concatenate(heads, axis=1))
    copies[0].wait()
    mixed = (normed * gate_ref[...].astype(F32)).astype(BF)
    copies[1].wait()
    more = dot(mixed, wo_ref[...])
    copies[2].wait()
    out_ref[...] = (x_ref[...].astype(F32) + more).astype(BF)
    for copy in later:
        copy.wait()


def turned(value, axis, size, steps):
    return lax.ppermute(value, axis, [(i, (i + steps) % size) for i in range(size)])


def crossed(value, steps):
    pairs = []
    for c in range(2):
        for y in range(4):
            for xh in range(2):
                pairs.append(((c * 4 + y) * 2 + xh, (xh * 4 + (y + steps) % 4) * 2 + c))
    return lax.ppermute(value, ("c", "y", "xh"), pairs)


def across(value):
    return lax.ppermute(value, "c", [(0, 1), (1, 0)])


def along(value, way, cross):
    pairs = []
    for c in range(2):
        step = way if c == 0 else -way
        for z in range(4):
            pairs.append((4 * c + z, 4 * (c ^ cross) + (z + step) % 4))
    return lax.ppermute(value, ("c", "z"), pairs)


def per_device(hist_x, hist_cot, cand_x, cand_loop, hist_len, w_proj, w_out):
    y, xh, z, c = (lax.axis_index(n) for n in ("y", "xh", "z", "c"))
    x_rows = hist_x.reshape(128, 1024)
    cot = hist_cot.reshape(128, 1024)
    info = jnp.stack([hist_len[0], (y * 8 + xh * 4 + z) * 128, y, c, z]).astype(jnp.int32)
    held = pl.BlockSpec(memory_space=pltpu.VMEM)
    far = pl.BlockSpec(memory_space=pltpu.HBM)

    def weights(count):
        return [pltpu.VMEM((count, 1024, 512), BF), pltpu.SemaphoreType.DMA((count,))]

    def relayed(values, after):
        return call(nothing, "relay", (1,), [], [], [], [], 1_000, after, carry=values)()

    *sent, slope, gate, gm = call(
        project_all, "project_all", (1,), [SMEM, far, far, far, far],
        [shaped((128, 512))] * 4 + [shaped((4, 128, 512))] + [shaped((128, 512))] * 2, [held] * 7,
        [
            pltpu.VMEM((128, 1024), BF), pltpu.VMEM((128, 512), BF), pltpu.VMEM((128, 1024), BF),
            pltpu.VMEM((128, 1024), BF), pltpu.VMEM((512, 1024), BF), pltpu.SemaphoreType.DMA((3,)),
        ] + weights(4), 700_000_000, (), 16,
    )(info, x_rows, cot, w_out, w_proj)
    parts = [crossed(v, k) for k, v in enumerate(sent)]

    sent_cand, cand_gate = call(
        project_cand, "project_cand", (1,), [held, held, far],
        [shaped((16, 128, 128)), shaped((256, 512))], [held] * 2,
        [pltpu.VMEM((256, 1024), BF)] + weights(2), 700_000_000, (slope,),
    )(cand_loop, cand_x, w_proj)

    own, sent_cand = call(
        arrange, "arrange", (1,), [SMEM] + [held] * 4, shaped((4, 128, 384)), held, [], 1_000_000,
        (cand_gate,), carry=(sent_cand,),
    )(info, *parts)
    own = own.reshape(512, 384)
    own_pair = across(own)
    plus, minus = along(own, 1, 0), along(own, -1, 0)
    arrived = lax.all_to_all(sent_cand, ("xl", "xh", "y"), 0, 0, tiled=True)
    last = [along(plus, 1, 0), along(plus, 1, 1)]
    kvq = [own, own_pair, plus, across(plus), minus, across(minus)]

    q_spec = pl.BlockSpec((4, 128, 128), lambda i: (i, 0, 0))
    acc_spec = pl.BlockSpec((512, 128), lambda i: (i, 0))

    def cand_part(kvs, total, end, after):
        begin = total is None
        return call(
            functools.partial(cand_attend, len(kvs), begin, end), "cand_attend", (4,),
            [q_spec] + [held] * len(kvs) + ([] if begin else [acc_spec]),
            shaped((16, 128, 128)) if end else shaped((2048, 128), F32),
            q_spec if end else acc_spec, [], 600_000_000 * len(kvs), after,
        )(arrived, *kvs, *([] if begin else [total]))

    att = call(
        hist_begin, "hist_begin", (1,), [SMEM] + [held] * 6,
        shaped((512, 128), F32), held, [], 1_000,
    )(info, *kvq)
    total = cand_part(kvq, None, False, (att,))
    att, stats = call(
        hist_end, "hist_end", (1,), [SMEM] + [held] * 8,
        [shaped((512, 128), F32), shaped((8, 512), F32)], [held] * 2,
        [pltpu.VMEM((512, 128), F32)], 400_000_000, (total,),
    )(info, *parts, own, *last, att)
    all_stats = [stats] + [turned(stats, "y", 4, k) for k in (1, 2, 3)]
    weighed = cand_part(last, total, True, (stats,))
    ga, normed = call(
        normed_grads, "normed_grads", (1,), [SMEM] + [held] * 9,
        [shaped((512, 128))] * 2, [held] * 2,
        [pltpu.VMEM((512, 128), F32)], 1_000_000, (weighed,),
    )(info, *parts, att, *all_stats)

    ga_plus, ga_minus = along(ga, 1, 0), along(ga, -1, 0)
    dq = call(
        hist_dq, "hist_dq", (1,), [SMEM] + [held] * 9,
        shaped((4, 128, 128)), held, [], 2_000_000_000,
    )(info, ga, *kvq, *last)
    ga_plus, ga_minus = relayed([ga_plus, ga_minus], (dq,))
    ga_last = [along(ga_plus, 1, 0), along(ga_plus, 1, 1)]
    gas = [ga, across(ga), ga_plus, across(ga_plus), ga_minus, across(ga_minus)]
    key_sums = call(
        hist_dkv_begin, "hist_dkv_begin", (1,), [SMEM] + [held] * 12,
        shaped((4, 128, 256), F32), held, [], 2_000_000_000,
    )(info, *kvq, *gas)
    (leaving,) = relayed([weighed], (key_sums, *ga_last))
    returned = lax.all_to_all(leaving, ("xl", "xh", "y"), 0, 0, tiled=True)
    grads = call(
        hist_dkv_end, "hist_dkv_end", (1,), [SMEM] + [held] * 8,
        [shaped((128, 512))] * 4, [held] * 4, [pltpu.VMEM((4, 128, 512), BF)], 800_000_000,
    )(info, dq, normed, own, *last, *ga_last, key_sums)
    back = [crossed(v, k) for k, v in enumerate(grads)]

    cand_out, wo_near, w_near, x_near, cot_near = call(
        cand_close, "cand_close", (1,), [held, far, held] + [far] * 5,
        [pltpu.HBM((256, 1024), BF), shaped((512, 1024)), shaped((4, 1024, 512))] + [shaped((128, 1024))] * 2,
        [pl.BlockSpec((256, 1024), lambda i: (0, 0))] + [held] * 4,
        [
            pltpu.VMEM((256, 512), BF), pltpu.VMEM((256, 1024), BF),
            pltpu.SemaphoreType.DMA((5,)), pltpu.SemaphoreType.DMA((4,)),
        ], 400_000_000, (grads[0],),
    )(cand_loop, cand_gate, returned, cand_x, w_out, w_proj, x_rows, cot)
    final = pltpu.HBM((1, 128, 1024), BF)
    hist_out, hist_grad = call(
        hist_close, "hist_close", (1,), [SMEM] + [held] * 11,
        [final] * 2, [far] * 2,
        [
            pltpu.VMEM((128, 512), BF), pltpu.VMEM((4, 128, 512), BF), pltpu.VMEM((128, 1024), BF),
            pltpu.VMEM((128, 1024), BF), pltpu.SemaphoreType.DMA((2,)),
        ], 700_000_000,
    )(info, x_near, cot_near, slope, wo_near, w_near, gate, gm, *back)
    return hist_out, hist_grad, cand_out


def solution(mesh):
    split = Mesh(mesh.devices.reshape(2, 2, 4, 2, 4), ("xl", "c", "y", "xh", "z"))
    users, rows = ("xl", "c"), ("y", "xh", "z")
    hist = P(users, rows, None)
    cand = P(users + rows, None)
    return jax.shard_map(
        per_device,
        mesh=split,
        in_specs=(hist, hist, cand, cand, P(users), P(), P()),
        out_specs=(hist, hist, cand),
        check_vma=False,
    )
```

```python
import functools

import jax
import jax.numpy as jnp
from jax import lax
from jax.experimental import pallas as pl
from jax.experimental.pallas import tpu as pltpu
from jax.sharding import Mesh, PartitionSpec as P

HS = 128
CAP = 128
HEADS = 4
EPS = 1e-05
SCALE = HS ** (-0.5)
BF = jnp.bfloat16
F32 = jnp.float32

NN = (((1,), (0,)), ((), ()))
NT = (((1,), (1,)), ((), ()))
SMEM = pl.BlockSpec(memory_space=pltpu.SMEM)


def dot(a, b, dims=NN):
    return lax.dot_general(a, b, dims, preferred_element_type=F32)


def whole(shape):
    return pl.BlockSpec(memory_space=pltpu.VMEM)


def call(body, name, grid, in_specs, outs, out_specs, scratch, flops, after=(), limit=12, carry=()):
    count, extra = len(in_specs), len(after) + len(carry)
    single = not isinstance(outs, (list, tuple))
    outs = [outs] if single else list(outs)
    out_specs = [out_specs] if single else list(out_specs)
    kept = len(outs)
    anywhere = pl.BlockSpec(memory_space=pl.ANY)

    def without(*refs):
        first = count + extra
        return body(*refs[:count], *refs[first : first + kept], *refs[first + kept + len(carry) :])

    made = pl.pallas_call(
        without,
        out_shape=outs + [jax.ShapeDtypeStruct(v.shape, v.dtype) for v in carry],
        grid=grid,
        in_specs=list(in_specs) + [anywhere] * extra,
        out_specs=out_specs + [anywhere] * len(carry),
        input_output_aliases={count + len(after) + n: kept + n for n in range(len(carry))},
        scratch_shapes=scratch,
        compiler_params=pltpu.CompilerParams(vmem_limit_bytes=limit * 1024 * 1024),
        cost_estimate=pl.CostEstimate(flops=flops, transcendentals=0, bytes_accessed=(1 << 20) if flops > 1000 else 1000),
        name=name,
    )

    def run(*args):
        pinned = []
        for arg, spec in zip(args, in_specs):
            if spec is not SMEM:
                space = spec.memory_space or pltpu.VMEM
                arg = pltpu.with_memory_space_constraint(arg, space)
            pinned.append(arg)
        got = made(*pinned, *after, *carry)
        return got[0] if len(got) == 1 and single else got

    return run


def shaped(shape, dtype=BF):
    return pltpu.VMEM(shape, dtype)


def normalize(values):
    center = values - jnp.mean(values, axis=-1, keepdims=True)
    spread = lax.rsqrt(jnp.mean(center * center, axis=-1, keepdims=True) + EPS)
    return center * spread, spread


def silu_parts(pre):
    half = 0.5 * pre
    sig = 0.5 + 0.5 * jnp.tanh(half)
    act = pre * sig
    return act, sig + act * (1.0 - sig)


def columns(w_ref, buf, sems, picks):
    copies = []
    for slot, pick in enumerate(picks):
        copy = pltpu.make_async_copy(w_ref.at[:, pl.ds(512 * pick, 512)], buf.at[slot], sems.at[slot])
        copy.start()
        copies.append(copy)
    return copies


def slot_ids(ids_ref):
    col = ids_ref[...]
    first = lax.broadcasted_iota(jnp.int32, (256, 256), 0)
    second = lax.broadcasted_iota(jnp.int32, (256, 256), 1)
    row = jnp.sum(jnp.where(first == second, col, 0), axis=0, keepdims=True)
    return col, row, first, second


def fetched(pairs, sems):
    copies = []
    for slot, (source, target) in enumerate(pairs):
        copy = pltpu.make_async_copy(source, target, sems.at[slot])
        copy.start()
        copies.append(copy)
    return copies


def project_all(
    info, x_far, cot_far, wo_far, w_ref, k0, k1, k2, k3, slope_ref, gate_ref, gm_ref,
    xn_ref, act_ref, x_ref, cot_ref, wo_ref, few, buf, sems,
):
    (got_x,) = fetched([(x_far, x_ref)], few)
    copies = columns(w_ref, buf, sems, (3, 1, 2, 0))
    rest = fetched([(cot_far, cot_ref), (wo_far, wo_ref)], few.at[pl.ds(1, 2)])
    got_x.wait()
    normed, _ = normalize(x_ref[...].astype(F32))
    xn_ref[...] = normed.astype(BF)
    rows = info[1] + lax.broadcasted_iota(jnp.int32, (128, 1), 0)
    inside = jnp.where(rows < info[0], 1.0, 0.0)
    length = jnp.full((128, 1), info[0], jnp.int32).astype(F32)

    def put(values, part):
        act_ref[...] = values.astype(BF)
        for k, out in enumerate((k0, k1, k2, k3)):
            lane = pl.multiple_of(((info[2] + k) & 3) * HS, HS)
            out[:, part * HS : (part + 1) * HS] = act_ref[:, pl.ds(lane, HS)]

    for part in range(4):
        copies[part].wait()
        act, slope = silu_parts(dot(xn_ref[...], buf[part]))
        slope_ref[part] = slope.astype(BF)
        if part < 3:
            put(act * (inside, inside / length, 0.5 * SCALE)[part], part)
    gate_ref[...] = act.astype(BF)
    for copy in rest:
        copy.wait()
    gm = dot(cot_ref[...], wo_ref[...], NT)
    gm_ref[...] = gm.astype(BF)
    put(gm * gate_ref[...].astype(F32), 3)


def arrange(info, a0, a1, a2, a3, out_ref):
    for k, a in enumerate((a0, a1, a2, a3)):
        out_ref[(info[2] - k) & 3] = a[:, : 3 * HS]


def project_cand(ids_ref, x_ref, w_ref, sent_ref, gate_ref, xn_ref, buf, sems):
    copies = columns(w_ref, buf, sems, (2, 0))
    xn_ref[...] = normalize(x_ref[...].astype(F32))[0].astype(BF)
    col, row, first, second = slot_ids(ids_ref)
    rank = jnp.sum(jnp.where((col == row) & (first < second), 1, 0), axis=0, keepdims=True)
    slot = row * CAP + rank
    hits = (lax.broadcasted_iota(jnp.int32, (4 * CAP, 256), 0) == slot).astype(F32).astype(BF)
    copies[0].wait()
    act, _ = silu_parts(dot(xn_ref[...], buf[0]))
    placed = dot(hits, (act * (0.5 * SCALE)).astype(BF)).astype(BF)
    for u in range(4):
        for h in range(HEADS):
            sent_ref[u * HEADS + h] = placed[u * CAP : (u + 1) * CAP, h * HS : (h + 1) * HS]
    copies[1].wait()
    act, _ = silu_parts(dot(xn_ref[...], buf[1]))
    gate_ref[...] = act.astype(BF)


def nothing(*refs):
    del refs


def order_of(info):
    c, z = info[3], info[4]
    o = 1 - c
    side = 1 - 2 * c
    near, far = (z - side) & 3, (z + side) & 3
    across = (z + 2) & 3
    spots = [(c, z), (o, z), (c, near), (o, far), (c, far), (o, near), (c, across), (o, across)]
    return [4 * core + spot for core, spot in spots]


def corner_masks(info, backward):
    order = order_of(info)
    first = lax.broadcasted_iota(jnp.int32, (256, 256), 0)
    second = lax.broadcasted_iota(jnp.int32, (256, 256), 1)
    early, late = (first, second) if backward else (second, first)
    below = (early >> 7) < (late >> 7)
    gap = jnp.where((early >> 7) == (late >> 7), early - late, 512)
    gap = jnp.where(below, -512, gap)
    masks = []
    for o in order:
        ahead = o > order[0] if backward else o < order[0]
        lead = jnp.where(ahead, 128, jnp.where(o == order[0], 0, -128))
        masks.append((gap <= lead).astype(F32).astype(BF))
    return masks


def cand_attend(count, begin, end, *refs):
    q_ref, kvs, rest = refs[0], refs[1 : 1 + count], refs[1 + count :]
    q = q_ref[...].reshape(8 * CAP, HS)
    total = None if begin else rest[0][...]
    for block in kvs:
        half = dot(q, block[:, :HS], NT).astype(BF)
        probs = half + half * jnp.tanh(half)
        more = dot(probs, block[:, HS : 2 * HS])
        total = more if total is None else total + more
    if end:
        rest[-1][...] = total.astype(BF).reshape(8, CAP, HS)
    else:
        rest[-1][...] = total


def attend_rows(q_ref, blocks, masks, old_ref, att_ref):
    for y in range(2):
        rows = slice(y * 256, (y + 1) * 256)
        q = q_ref[rows, 2 * HS :]
        total = None if old_ref is None else old_ref[rows, :]
        for block, mask in zip(blocks, masks):
            half = dot(q, block[: 256 * (y + 1), :HS], NT).astype(BF)
            probs = half + half * jnp.tanh(half)
            last = probs[:, 256 * y :] * mask
            probs = last if y == 0 else jnp.concatenate([probs[:, : 256 * y], last], axis=1)
            more = dot(probs, block[: 256 * (y + 1), HS : 2 * HS])
            total = more if total is None else total + more
        att_ref[rows, :] = total


def hist_begin(info, *refs):
    attend_rows(refs[0], refs[:6], corner_masks(info, False)[:6], None, refs[6])


def hist_end(info, p0, p1, p2, p3, own_ref, b0, b1, old_ref, att_ref, stat_ref, g_ref):
    for k, part in enumerate((p0, p1, p2, p3)):
        rows = pl.ds(pl.multiple_of(((info[2] - k) & 3) * 128, 128), 128)
        g_ref[rows, :] = part[:, 3 * HS :].astype(F32)
    attend_rows(own_ref, (b0, b1), corner_masks(info, False)[6:], old_ref, att_ref)
    att = att_ref[...]
    g = g_ref[...]
    mean = jnp.mean(att, axis=1, keepdims=True)
    center = att - mean
    lane = lax.broadcasted_iota(jnp.int32, (512, 128), 1)
    stats = jnp.where(lane == 0, mean, 0.0)
    stats = jnp.where(lane == 1, jnp.sum(center * center, axis=1, keepdims=True), stats)
    stats = jnp.where(lane == 2, jnp.sum(g, axis=1, keepdims=True), stats)
    stats = jnp.where(lane == 3, jnp.sum(g * center, axis=1, keepdims=True), stats)
    stat_ref[...] = jnp.transpose(stats)[:8]


def normed_grads(info, p0, p1, p2, p3, att_ref, s0, s1, s2, s3, ga_ref, normed_ref, g_ref):
    for k, part in enumerate((p0, p1, p2, p3)):
        y = (info[2] - k) & 3
        rows = pl.ds(pl.multiple_of(y * 128, 128), 128)
        g_ref[rows, :] = part[:, 3 * HS :].astype(F32)
    stats = [s[...] for s in (s0, s1, s2, s3)]
    mean = sum(s[0:1] for s in stats) * 0.25
    squares = sum(s[1:2] + HS * (s[0:1] - mean) * (s[0:1] - mean) for s in stats)
    spread = lax.rsqrt(squares * (1.0 / (HEADS * HS)) + EPS)
    g_mean = sum(s[2:3] for s in stats) * (1.0 / (HEADS * HS))
    ga_sum = sum(s[3:4] + s[2:3] * (s[0:1] - mean) for s in stats)
    ga_mean = ga_sum * spread * (1.0 / (HEADS * HS))
    line = lax.broadcasted_iota(jnp.int32, (128, 512), 0)
    packed = jnp.where(line == 0, mean, 0.0)
    packed = jnp.where(line == 1, spread, packed)
    packed = jnp.where(line == 2, g_mean, packed)
    packed = jnp.where(line == 3, ga_mean, packed)
    cols = jnp.transpose(packed)
    spread_c = cols[:, 1:2]
    normed = (att_ref[...] - cols[:, 0:1]) * spread_c
    ga_ref[...] = (spread_c * (g_ref[...] - cols[:, 2:3] - normed * cols[:, 3:4])).astype(BF)
    normed_ref[...] = normed.astype(BF)


def slope_times(half, grads):
    t = jnp.tanh(half)
    probs = half + half * t
    slope = (1.0 + t + probs * (1.0 - t)).astype(BF)
    return probs, grads * slope


def hist_dq(info, ga_ref, *refs):
    blocks, dq_ref = refs[:8], refs[8]
    masks = corner_masks(info, False)
    for y in range(2):
        q = blocks[0][y * 256 : (y + 1) * 256, 2 * HS :]
        ga = ga_ref[y * 256 : (y + 1) * 256, :]
        total = None
        for block, mask in zip(blocks, masks):
            key = block[: 256 * (y + 1), :HS]
            half = dot(q, key, NT).astype(BF)
            _, ds = slope_times(half, dot(ga, block[: 256 * (y + 1), HS : 2 * HS], NT).astype(BF))
            last = ds[:, 256 * y :] * mask
            ds = last if y == 0 else jnp.concatenate([ds[:, : 256 * y], last], axis=1)
            more = dot(ds, key)
            total = more if total is None else total + more
        dq_ref[2 * y : 2 * y + 2] = (total * (0.5 * SCALE)).astype(BF).reshape(2, 128, HS)


def key_grads(own_ref, blocks, gas, masks, y, dk, dv):
    key = own_ref[y * 256 : (y + 1) * 256, :HS]
    value = own_ref[y * 256 : (y + 1) * 256, HS : 2 * HS]
    for block, ga_block, mask in zip(blocks, gas, masks):
        q = block[256 * y :, 2 * HS :]
        ga = ga_block[256 * y :, :]
        half = dot(key, q, NT).astype(BF)
        probs, ds = slope_times(half, dot(value, ga, NT).astype(BF))
        p_first = probs[:, :256] * mask
        d_first = ds[:, :256] * mask
        if y < 1:
            probs = jnp.concatenate([p_first, probs[:, 256:]], axis=1)
            ds = jnp.concatenate([d_first, ds[:, 256:]], axis=1)
        else:
            probs, ds = p_first, d_first
        more_k = dot(ds, q)
        more_v = dot(probs, ga)
        dk = more_k if dk is None else dk + more_k
        dv = more_v if dv is None else dv + more_v
    return dk, dv


def hist_dkv_begin(info, *refs):
    masks = corner_masks(info, True)[:6]
    for y in range(2):
        dk, dv = key_grads(refs[0], refs[:6], refs[6:12], masks, y, None, None)
        refs[12][y, :, :HS] = dk
        refs[12][y, :, HS:] = dv


def hist_dkv_end(info, dq_ref, normed_ref, own_ref, b0, b1, g0, g1, old_ref, k0, k1, k2, k3, all_ref):
    masks = corner_masks(info, True)[6:]
    for y in range(2):
        dk, dv = key_grads(own_ref, (b0, b1), (g0, g1), masks, y, old_ref[y, :, :HS], old_ref[y, :, HS:])
        all_ref[2 * y : 2 * y + 2, :, HS : 2 * HS] = dk.astype(BF).reshape(2, 128, HS)
        all_ref[2 * y : 2 * y + 2, :, 2 * HS : 3 * HS] = dv.astype(BF).reshape(2, 128, HS)
    for y in range(4):
        all_ref[y, :, :HS] = dq_ref[y]
        all_ref[y, :, 3 * HS :] = normed_ref[y * 128 : (y + 1) * 128, :]
    for k, out in enumerate((k0, k1, k2, k3)):
        out[...] = all_ref[(info[2] + k) & 3]


def hist_close(
    info, x_ref, cot_ref, slope_ref, wo_ref, buf, gate_ref, gm_ref, b0, b1, b2, b3, out_far, grad_far,
    mixed_ref, hid_ref, out_ref, grad_ref, few,
):
    length = jnp.full((128, 1), info[0], jnp.int32).astype(F32)
    for k, b in enumerate((b0, b1, b2, b3)):
        lanes = pl.ds(pl.multiple_of(((info[2] - k) & 3) * HS, HS), HS)

        def put(part, grads, which):
            hid_ref[part, :, lanes] = (grads * slope_ref[which, :, lanes].astype(F32)).astype(BF)

        normed = b[:, 3 * HS :].astype(F32)
        put(0, normed * gm_ref[:, lanes].astype(F32), 3)
        put(1, b[:, 2 * HS : 3 * HS].astype(F32) / length, 1)
        put(2, b[:, :HS].astype(F32), 2)
        put(3, b[:, HS : 2 * HS].astype(F32), 0)
        mixed_ref[:, lanes] = (normed * gate_ref[:, lanes].astype(F32)).astype(BF)
    x = x_ref[...].astype(F32)
    out_ref[...] = (x + dot(mixed_ref[...], wo_ref[...])).astype(BF)
    done = fetched([(out_ref, out_far.at[0])], few)
    e = None
    for part in range(4):
        more = dot(hid_ref[part], buf[part], NT)
        e = more if e is None else e + more
    normed, spread = normalize(x)
    back = spread * (
        e - jnp.mean(e, axis=-1, keepdims=True) - normed * jnp.mean(e * normed, axis=-1, keepdims=True)
    )
    grad_ref[...] = (cot_ref[...].astype(F32) + back).astype(BF)
    done += fetched([(grad_ref, grad_far.at[0])], few.at[pl.ds(1, 1)])
    for copy in done:
        copy.wait()


def cand_close(
    ids_ref, gate_far, ret_ref, x_far, wo_far, w_far, hx_far, cot_far, out_ref, wo_ref, buf, hx_ref, cot_ref,
    gate_ref, x_ref, few, sems,
):
    copies = fetched([(gate_far, gate_ref), (wo_far, wo_ref), (x_far, x_ref)], few)
    later = columns(w_far, buf, sems, (0, 1, 2, 3))
    later += fetched([(hx_far, hx_ref), (cot_far, cot_ref)], few.at[pl.ds(3, 2)])
    col, row, first, second = slot_ids(ids_ref)
    rank = jnp.sum(jnp.where((col == row) & (second < first), 1, 0), axis=1, keepdims=True)
    slot = col * CAP + rank
    hits = (lax.broadcasted_iota(jnp.int32, (256, 4 * CAP), 1) == slot).astype(F32).astype(BF)
    heads = []
    for h in range(HEADS):
        rows = jnp.concatenate([ret_ref[u * HEADS + h] for u in range(4)], axis=0)
        heads.append(dot(hits, rows))
    normed, _ = normalize(jnp.concatenate(heads, axis=1))
    copies[0].wait()
    mixed = (normed * gate_ref[...].astype(F32)).astype(BF)
    copies[1].wait()
    more = dot(mixed, wo_ref[...])
    copies[2].wait()
    out_ref[...] = (x_ref[...].astype(F32) + more).astype(BF)
    for copy in later:
        copy.wait()


def turned(value, axis, size, steps):
    return lax.ppermute(value, axis, [(i, (i + steps) % size) for i in range(size)])


def crossed(value, steps):
    pairs = []
    for c in range(2):
        for y in range(4):
            for xh in range(2):
                pairs.append(((c * 4 + y) * 2 + xh, (xh * 4 + (y + steps) % 4) * 2 + c))
    return lax.ppermute(value, ("c", "y", "xh"), pairs)


def across(value):
    return lax.ppermute(value, "c", [(0, 1), (1, 0)])


def along(value, way, cross):
    pairs = []
    for c in range(2):
        step = way if c == 0 else -way
        for z in range(4):
            pairs.append((4 * c + z, 4 * (c ^ cross) + (z + step) % 4))
    return lax.ppermute(value, ("c", "z"), pairs)


def per_device(hist_x, hist_cot, cand_x, cand_loop, hist_len, w_proj, w_out):
    y, xh, z, c = (lax.axis_index(n) for n in ("y", "xh", "z", "c"))
    x_rows = hist_x.reshape(128, 1024)
    cot = hist_cot.reshape(128, 1024)
    info = jnp.stack([hist_len[0], (y * 8 + xh * 4 + z) * 128, y, c, z]).astype(jnp.int32)
    held = pl.BlockSpec(memory_space=pltpu.VMEM)
    far = pl.BlockSpec(memory_space=pltpu.HBM)

    def weights(count):
        return [pltpu.VMEM((count, 1024, 512), BF), pltpu.SemaphoreType.DMA((count,))]

    def relayed(values, after):
        return call(nothing, "relay", (1,), [], [], [], [], 1_000, after, carry=values)()

    *sent, slope, gate, gm = call(
        project_all, "project_all", (1,), [SMEM, far, far, far, far],
        [shaped((128, 512))] * 4 + [shaped((4, 128, 512))] + [pltpu.HBM((128, 512), BF)] * 2,
        [held] * 5 + [pl.BlockSpec((128, 512), lambda i: (0, 0))] * 2,
        [
            pltpu.VMEM((128, 1024), BF), pltpu.VMEM((128, 512), BF), pltpu.VMEM((128, 1024), BF),
            pltpu.VMEM((128, 1024), BF), pltpu.VMEM((512, 1024), BF), pltpu.SemaphoreType.DMA((3,)),
        ] + weights(4), 700_000_000, (), 16,
    )(info, x_rows, cot, w_out, w_proj)
    parts = [crossed(v, k) for k, v in enumerate(sent)]

    sent_cand, cand_gate = call(
        project_cand, "project_cand", (1,), [held, held, far],
        [shaped((16, 128, 128)), shaped((256, 512))], [held] * 2,
        [pltpu.VMEM((256, 1024), BF)] + weights(2), 700_000_000, (slope,),
    )(cand_loop, cand_x, w_proj)

    own, sent_cand = call(
        arrange, "arrange", (1,), [SMEM] + [held] * 4, shaped((4, 128, 384)), held, [], 1_000_000,
        (cand_gate,), carry=(sent_cand,),
    )(info, *parts)
    own = own.reshape(512, 384)
    own_pair = across(own)
    plus, minus = along(own, 1, 0), along(own, -1, 0)
    arrived = lax.all_to_all(sent_cand, ("xl", "xh", "y"), 0, 0, tiled=True)
    last = [along(plus, 1, 0), along(plus, 1, 1)]
    kvq = [own, own_pair, plus, across(plus), minus, across(minus)]

    q_spec = pl.BlockSpec((8, 128, 128), lambda i: (i, 0, 0))
    acc_spec = pl.BlockSpec((1024, 128), lambda i: (i, 0))

    def cand_part(kvs, total, end, after):
        begin = total is None
        return call(
            functools.partial(cand_attend, len(kvs), begin, end), "cand_attend", (2,),
            [q_spec] + [held] * len(kvs) + ([] if begin else [acc_spec]),
            shaped((16, 128, 128)) if end else shaped((2048, 128), F32),
            q_spec if end else acc_spec, [], 600_000_000 * len(kvs), after,
        )(arrived, *kvs, *([] if begin else [total]))

    att = call(
        hist_begin, "hist_begin", (1,), [SMEM] + [held] * 6,
        shaped((512, 128), F32), held, [], 1_000,
    )(info, *kvq)
    total = cand_part(kvq, None, False, (att,))
    att, stats = call(
        hist_end, "hist_end", (1,), [SMEM] + [held] * 8,
        [shaped((512, 128), F32), shaped((8, 512), F32)], [held] * 2,
        [pltpu.VMEM((512, 128), F32)], 400_000_000, (total,),
    )(info, *parts, own, *last, att)
    all_stats = [stats] + [turned(stats, "y", 4, k) for k in (1, 2, 3)]
    weighed = cand_part(last, total, True, (stats,))
    ga, normed = call(
        normed_grads, "normed_grads", (1,), [SMEM] + [held] * 9,
        [shaped((512, 128))] * 2, [held] * 2,
        [pltpu.VMEM((512, 128), F32)], 1_000_000, (weighed,),
    )(info, *parts, att, *all_stats)

    ga_plus, ga_minus = along(ga, 1, 0), along(ga, -1, 0)
    dq = call(
        hist_dq, "hist_dq", (1,), [SMEM] + [held] * 9,
        shaped((4, 128, 128)), held, [], 2_000_000_000,
    )(info, ga, *kvq, *last)
    ga_plus, ga_minus = relayed([ga_plus, ga_minus], (dq,))
    ga_last = [along(ga_plus, 1, 0), along(ga_plus, 1, 1)]
    gas = [ga, across(ga), ga_plus, across(ga_plus), ga_minus, across(ga_minus)]
    key_sums = call(
        hist_dkv_begin, "hist_dkv_begin", (1,), [SMEM] + [held] * 12,
        shaped((2, 256, 256), F32), held, [], 2_000_000_000,
    )(info, *kvq, *gas)
    (leaving,) = relayed([weighed], (key_sums, *ga_last))
    returned = lax.all_to_all(leaving, ("xl", "xh", "y"), 0, 0, tiled=True)
    grads = call(
        hist_dkv_end, "hist_dkv_end", (1,), [SMEM] + [held] * 8,
        [shaped((128, 512))] * 4, [held] * 4, [pltpu.VMEM((4, 128, 512), BF)], 800_000_000,
    )(info, dq, normed, own, *last, *ga_last, key_sums)
    back = [crossed(v, k) for k, v in enumerate(grads)]

    cand_out, wo_near, w_near, x_near, cot_near = call(
        cand_close, "cand_close", (1,), [held, far, held] + [far] * 5,
        [pltpu.HBM((256, 1024), BF), shaped((512, 1024)), shaped((4, 1024, 512))] + [shaped((128, 1024))] * 2,
        [pl.BlockSpec((256, 1024), lambda i: (0, 0))] + [held] * 4,
        [
            pltpu.VMEM((256, 512), BF), pltpu.VMEM((256, 1024), BF),
            pltpu.SemaphoreType.DMA((5,)), pltpu.SemaphoreType.DMA((4,)),
        ], 400_000_000, (grads[0],),
    )(cand_loop, cand_gate, returned, cand_x, w_out, w_proj, x_rows, cot)
    final = pltpu.HBM((1, 128, 1024), BF)
    hist_out, hist_grad = call(
        hist_close, "hist_close", (1,), [SMEM] + [held] * 11,
        [final] * 2, [far] * 2,
        [
            pltpu.VMEM((128, 512), BF), pltpu.VMEM((4, 128, 512), BF), pltpu.VMEM((128, 1024), BF),
            pltpu.VMEM((128, 1024), BF), pltpu.SemaphoreType.DMA((2,)),
        ], 700_000_000,
    )(info, x_near, cot_near, slope, wo_near, w_near, gate, gm, *back)
    return hist_out, hist_grad, cand_out


def solution(mesh):
    split = Mesh(mesh.devices.reshape(2, 2, 4, 2, 4), ("xl", "c", "y", "xh", "z"))
    users, rows = ("xl", "c"), ("y", "xh", "z")
    hist = P(users, rows, None)
    cand = P(users + rows, None)
    return jax.shard_map(
        per_device,
        mesh=split,
        in_specs=(hist, hist, cand, cand, P(users), P(), P()),
        out_specs=(hist, hist, cand),
        check_vma=False,
    )
```

```python
import functools

import jax
import jax.numpy as jnp
from jax import lax
from jax.experimental import pallas as pl
from jax.experimental.pallas import tpu as pltpu
from jax.sharding import Mesh, PartitionSpec as P

HS = 128
CAP = 128
HEADS = 4
EPS = 1e-05
SCALE = HS ** (-0.5)
BF = jnp.bfloat16
F32 = jnp.float32

NN = (((1,), (0,)), ((), ()))
NT = (((1,), (1,)), ((), ()))
SMEM = pl.BlockSpec(memory_space=pltpu.SMEM)


def dot(a, b, dims=NN):
    return lax.dot_general(a, b, dims, preferred_element_type=F32)


def whole(shape):
    return pl.BlockSpec(memory_space=pltpu.VMEM)


def call(body, name, grid, in_specs, outs, out_specs, scratch, flops, after=(), limit=12, carry=()):
    count, extra = len(in_specs), len(after) + len(carry)
    single = not isinstance(outs, (list, tuple))
    outs = [outs] if single else list(outs)
    out_specs = [out_specs] if single else list(out_specs)
    kept = len(outs)
    anywhere = pl.BlockSpec(memory_space=pl.ANY)

    def without(*refs):
        first = count + extra
        return body(*refs[:count], *refs[first : first + kept], *refs[first + kept + len(carry) :])

    made = pl.pallas_call(
        without,
        out_shape=outs + [jax.ShapeDtypeStruct(v.shape, v.dtype) for v in carry],
        grid=grid,
        in_specs=list(in_specs) + [anywhere] * extra,
        out_specs=out_specs + [anywhere] * len(carry),
        input_output_aliases={count + len(after) + n: kept + n for n in range(len(carry))},
        scratch_shapes=scratch,
        compiler_params=pltpu.CompilerParams(vmem_limit_bytes=limit * 1024 * 1024),
        cost_estimate=pl.CostEstimate(flops=flops, transcendentals=0, bytes_accessed=(1 << 20) if flops > 1000 else 1000),
        name=name,
    )

    def run(*args):
        pinned = []
        for arg, spec in zip(args, in_specs):
            if spec is not SMEM:
                space = spec.memory_space or pltpu.VMEM
                arg = pltpu.with_memory_space_constraint(arg, space)
            pinned.append(arg)
        got = made(*pinned, *after, *carry)
        return got[0] if len(got) == 1 and single else got

    return run


def shaped(shape, dtype=BF):
    return pltpu.VMEM(shape, dtype)


def normalize(values):
    center = values - jnp.mean(values, axis=-1, keepdims=True)
    spread = lax.rsqrt(jnp.mean(center * center, axis=-1, keepdims=True) + EPS)
    return center * spread, spread


def silu_parts(pre):
    half = 0.5 * pre
    sig = 0.5 + 0.5 * jnp.tanh(half)
    act = pre * sig
    return act, sig + act * (1.0 - sig)


def columns(w_ref, buf, sems, picks):
    copies = []
    for slot, pick in enumerate(picks):
        copy = pltpu.make_async_copy(w_ref.at[:, pl.ds(512 * pick, 512)], buf.at[slot], sems.at[slot])
        copy.start()
        copies.append(copy)
    return copies


def slot_ids(ids_ref):
    col = ids_ref[...]
    first = lax.broadcasted_iota(jnp.int32, (256, 256), 0)
    second = lax.broadcasted_iota(jnp.int32, (256, 256), 1)
    row = jnp.sum(jnp.where(first == second, col, 0), axis=0, keepdims=True)
    return col, row, first, second


def fetched(pairs, sems):
    copies = []
    for slot, (source, target) in enumerate(pairs):
        copy = pltpu.make_async_copy(source, target, sems.at[slot])
        copy.start()
        copies.append(copy)
    return copies


def project_all(
    info, x_far, cot_far, wo_far, w_ref, k0, k1, k2, k3, slope_ref, gate_ref, gm_ref,
    xn_ref, act_ref, x_ref, cot_ref, wo_ref, few, buf, sems,
):
    (got_x,) = fetched([(x_far, x_ref)], few)
    copies = columns(w_ref, buf, sems, (3, 1, 2, 0))
    rest = fetched([(cot_far, cot_ref), (wo_far, wo_ref)], few.at[pl.ds(1, 2)])
    got_x.wait()
    normed, _ = normalize(x_ref[...].astype(F32))
    xn_ref[...] = normed.astype(BF)
    rows = info[1] + lax.broadcasted_iota(jnp.int32, (128, 1), 0)
    inside = jnp.where(rows < info[0], 1.0, 0.0)
    length = jnp.full((128, 1), info[0], jnp.int32).astype(F32)

    def put(values, part):
        act_ref[...] = values.astype(BF)
        for k, out in enumerate((k0, k1, k2, k3)):
            lane = pl.multiple_of(((info[2] + k) & 3) * HS, HS)
            out[:, part * HS : (part + 1) * HS] = act_ref[:, pl.ds(lane, HS)]

    for part in range(4):
        copies[part].wait()
        act, slope = silu_parts(dot(xn_ref[...], buf[part]))
        slope_ref[part] = slope.astype(BF)
        if part < 3:
            put(act * (inside, inside / length, 0.5 * SCALE)[part], part)
    gate_ref[...] = act.astype(BF)
    for copy in rest:
        copy.wait()
    gm = dot(cot_ref[...], wo_ref[...], NT)
    gm_ref[...] = gm.astype(BF)
    put(gm * gate_ref[...].astype(F32), 3)


def arrange(info, a0, a1, a2, a3, out_ref):
    for k, a in enumerate((a0, a1, a2, a3)):
        out_ref[(info[2] - k) & 3] = a[:, : 3 * HS]


def project_cand(ids_ref, x_ref, w_ref, sent_ref, gate_ref, xn_ref, buf, sems):
    copies = columns(w_ref, buf, sems, (2, 0))
    xn_ref[...] = normalize(x_ref[...].astype(F32))[0].astype(BF)
    col, row, first, second = slot_ids(ids_ref)
    rank = jnp.sum(jnp.where((col == row) & (first < second), 1, 0), axis=0, keepdims=True)
    slot = row * CAP + rank
    hits = (lax.broadcasted_iota(jnp.int32, (4 * CAP, 256), 0) == slot).astype(F32).astype(BF)
    copies[0].wait()
    act, _ = silu_parts(dot(xn_ref[...], buf[0]))
    placed = dot(hits, (act * (0.5 * SCALE)).astype(BF)).astype(BF)
    for u in range(4):
        for h in range(HEADS):
            sent_ref[u * HEADS + h] = placed[u * CAP : (u + 1) * CAP, h * HS : (h + 1) * HS]
    copies[1].wait()
    act, _ = silu_parts(dot(xn_ref[...], buf[1]))
    gate_ref[...] = act.astype(BF)


def nothing(*refs):
    del refs


def order_of(info):
    c, z = info[3], info[4]
    o = 1 - c
    side = 1 - 2 * c
    near, far = (z - side) & 3, (z + side) & 3
    across = (z + 2) & 3
    spots = [(c, z), (o, z), (c, near), (o, far), (c, far), (o, near), (c, across), (o, across)]
    return [4 * core + spot for core, spot in spots]


def corner_masks(info, backward):
    order = order_of(info)
    first = lax.broadcasted_iota(jnp.int32, (256, 256), 0)
    second = lax.broadcasted_iota(jnp.int32, (256, 256), 1)
    early, late = (first, second) if backward else (second, first)
    below = (early >> 7) < (late >> 7)
    gap = jnp.where((early >> 7) == (late >> 7), early - late, 512)
    gap = jnp.where(below, -512, gap)
    masks = []
    for o in order:
        ahead = o > order[0] if backward else o < order[0]
        lead = jnp.where(ahead, 128, jnp.where(o == order[0], 0, -128))
        masks.append((gap <= lead).astype(F32).astype(BF))
    return masks


def cand_attend(count, begin, end, *refs):
    q_ref, kvs, rest = refs[0], refs[1 : 1 + count], refs[1 + count :]
    q = q_ref[...].reshape(16 * CAP, HS)
    total = None if begin else rest[0][...]
    for block in kvs:
        half = dot(q, block[:, :HS], NT).astype(BF)
        probs = half + half * jnp.tanh(half)
        more = dot(probs, block[:, HS : 2 * HS])
        total = more if total is None else total + more
    if end:
        rest[-1][...] = total.astype(BF).reshape(16, CAP, HS)
    else:
        rest[-1][...] = total


def attend_rows(q_ref, blocks, masks, old_ref, att_ref):
    for y in range(2):
        rows = slice(y * 256, (y + 1) * 256)
        q = q_ref[rows, 2 * HS :]
        total = None if old_ref is None else old_ref[rows, :]
        for block, mask in zip(blocks, masks):
            half = dot(q, block[: 256 * (y + 1), :HS], NT).astype(BF)
            probs = half + half * jnp.tanh(half)
            last = probs[:, 256 * y :] * mask
            probs = last if y == 0 else jnp.concatenate([probs[:, : 256 * y], last], axis=1)
            more = dot(probs, block[: 256 * (y + 1), HS : 2 * HS])
            total = more if total is None else total + more
        att_ref[rows, :] = total


def hist_begin(info, *refs):
    attend_rows(refs[0], refs[:6], corner_masks(info, False)[:6], None, refs[6])


def hist_end(info, p0, p1, p2, p3, own_ref, b0, b1, old_ref, att_ref, stat_ref, g_ref):
    for k, part in enumerate((p0, p1, p2, p3)):
        rows = pl.ds(pl.multiple_of(((info[2] - k) & 3) * 128, 128), 128)
        g_ref[rows, :] = part[:, 3 * HS :].astype(F32)
    attend_rows(own_ref, (b0, b1), corner_masks(info, False)[6:], old_ref, att_ref)
    att = att_ref[...]
    g = g_ref[...]
    mean = jnp.mean(att, axis=1, keepdims=True)
    center = att - mean
    lane = lax.broadcasted_iota(jnp.int32, (512, 128), 1)
    stats = jnp.where(lane == 0, mean, 0.0)
    stats = jnp.where(lane == 1, jnp.sum(center * center, axis=1, keepdims=True), stats)
    stats = jnp.where(lane == 2, jnp.sum(g, axis=1, keepdims=True), stats)
    stats = jnp.where(lane == 3, jnp.sum(g * center, axis=1, keepdims=True), stats)
    stat_ref[...] = jnp.transpose(stats)[:8]


def normed_grads(info, p0, p1, p2, p3, att_ref, s0, s1, s2, s3, ga_ref, normed_ref, g_ref):
    for k, part in enumerate((p0, p1, p2, p3)):
        y = (info[2] - k) & 3
        rows = pl.ds(pl.multiple_of(y * 128, 128), 128)
        g_ref[rows, :] = part[:, 3 * HS :].astype(F32)
    stats = [s[...] for s in (s0, s1, s2, s3)]
    mean = sum(s[0:1] for s in stats) * 0.25
    squares = sum(s[1:2] + HS * (s[0:1] - mean) * (s[0:1] - mean) for s in stats)
    spread = lax.rsqrt(squares * (1.0 / (HEADS * HS)) + EPS)
    g_mean = sum(s[2:3] for s in stats) * (1.0 / (HEADS * HS))
    ga_sum = sum(s[3:4] + s[2:3] * (s[0:1] - mean) for s in stats)
    ga_mean = ga_sum * spread * (1.0 / (HEADS * HS))
    line = lax.broadcasted_iota(jnp.int32, (128, 512), 0)
    packed = jnp.where(line == 0, mean, 0.0)
    packed = jnp.where(line == 1, spread, packed)
    packed = jnp.where(line == 2, g_mean, packed)
    packed = jnp.where(line == 3, ga_mean, packed)
    cols = jnp.transpose(packed)
    spread_c = cols[:, 1:2]
    normed = (att_ref[...] - cols[:, 0:1]) * spread_c
    ga_ref[...] = (spread_c * (g_ref[...] - cols[:, 2:3] - normed * cols[:, 3:4])).astype(BF)
    normed_ref[...] = normed.astype(BF)


def slope_times(half, grads):
    t = jnp.tanh(half)
    probs = half + half * t
    slope = (1.0 + t + probs * (1.0 - t)).astype(BF)
    return probs, grads * slope


def hist_dq(info, ga_ref, *refs):
    blocks, dq_ref = refs[:8], refs[8]
    masks = corner_masks(info, False)
    for y in range(2):
        q = blocks[0][y * 256 : (y + 1) * 256, 2 * HS :]
        ga = ga_ref[y * 256 : (y + 1) * 256, :]
        total = None
        for block, mask in zip(blocks, masks):
            key = block[: 256 * (y + 1), :HS]
            half = dot(q, key, NT).astype(BF)
            _, ds = slope_times(half, dot(ga, block[: 256 * (y + 1), HS : 2 * HS], NT).astype(BF))
            last = ds[:, 256 * y :] * mask
            ds = last if y == 0 else jnp.concatenate([ds[:, : 256 * y], last], axis=1)
            more = dot(ds, key)
            total = more if total is None else total + more
        dq_ref[2 * y : 2 * y + 2] = (total * (0.5 * SCALE)).astype(BF).reshape(2, 128, HS)


def key_grads(own_ref, blocks, gas, masks, y, dk, dv):
    key = own_ref[y * 256 : (y + 1) * 256, :HS]
    value = own_ref[y * 256 : (y + 1) * 256, HS : 2 * HS]
    for block, ga_block, mask in zip(blocks, gas, masks):
        q = block[256 * y :, 2 * HS :]
        ga = ga_block[256 * y :, :]
        half = dot(key, q, NT).astype(BF)
        probs, ds = slope_times(half, dot(value, ga, NT).astype(BF))
        p_first = probs[:, :256] * mask
        d_first = ds[:, :256] * mask
        if y < 1:
            probs = jnp.concatenate([p_first, probs[:, 256:]], axis=1)
            ds = jnp.concatenate([d_first, ds[:, 256:]], axis=1)
        else:
            probs, ds = p_first, d_first
        more_k = dot(ds, q)
        more_v = dot(probs, ga)
        dk = more_k if dk is None else dk + more_k
        dv = more_v if dv is None else dv + more_v
    return dk, dv


def hist_dkv_begin(info, *refs):
    masks = corner_masks(info, True)[:6]
    for y in range(2):
        dk, dv = key_grads(refs[0], refs[:6], refs[6:12], masks, y, None, None)
        refs[12][y, :, :HS] = dk
        refs[12][y, :, HS:] = dv


def hist_dkv_end(info, dq_ref, normed_ref, own_ref, b0, b1, g0, g1, old_ref, k0, k1, k2, k3, all_ref):
    masks = corner_masks(info, True)[6:]
    for y in range(2):
        dk, dv = key_grads(own_ref, (b0, b1), (g0, g1), masks, y, old_ref[y, :, :HS], old_ref[y, :, HS:])
        all_ref[2 * y : 2 * y + 2, :, HS : 2 * HS] = dk.astype(BF).reshape(2, 128, HS)
        all_ref[2 * y : 2 * y + 2, :, 2 * HS : 3 * HS] = dv.astype(BF).reshape(2, 128, HS)
    for y in range(4):
        all_ref[y, :, :HS] = dq_ref[y]
        all_ref[y, :, 3 * HS :] = normed_ref[y * 128 : (y + 1) * 128, :]
    for k, out in enumerate((k0, k1, k2, k3)):
        out[...] = all_ref[(info[2] + k) & 3]


def hist_close(
    info, x_ref, cot_ref, slope_ref, wo_ref, buf, gate_ref, gm_ref, b0, b1, b2, b3, out_far, grad_far,
    mixed_ref, hid_ref, out_ref, grad_ref, few,
):
    length = jnp.full((128, 1), info[0], jnp.int32).astype(F32)
    for k, b in enumerate((b0, b1, b2, b3)):
        lanes = pl.ds(pl.multiple_of(((info[2] - k) & 3) * HS, HS), HS)

        def put(part, grads, which):
            hid_ref[part, :, lanes] = (grads * slope_ref[which, :, lanes].astype(F32)).astype(BF)

        normed = b[:, 3 * HS :].astype(F32)
        put(0, normed * gm_ref[:, lanes].astype(F32), 3)
        put(1, b[:, 2 * HS : 3 * HS].astype(F32) / length, 1)
        put(2, b[:, :HS].astype(F32), 2)
        put(3, b[:, HS : 2 * HS].astype(F32), 0)
        mixed_ref[:, lanes] = (normed * gate_ref[:, lanes].astype(F32)).astype(BF)
    x = x_ref[...].astype(F32)
    out_ref[...] = (x + dot(mixed_ref[...], wo_ref[...])).astype(BF)
    done = fetched([(out_ref, out_far.at[0])], few)
    e = None
    for part in range(4):
        more = dot(hid_ref[part], buf[part], NT)
        e = more if e is None else e + more
    normed, spread = normalize(x)
    back = spread * (
        e - jnp.mean(e, axis=-1, keepdims=True) - normed * jnp.mean(e * normed, axis=-1, keepdims=True)
    )
    grad_ref[...] = (cot_ref[...].astype(F32) + back).astype(BF)
    done += fetched([(grad_ref, grad_far.at[0])], few.at[pl.ds(1, 1)])
    for copy in done:
        copy.wait()


def cand_close(
    ids_ref, gate_far, ret_ref, x_far, wo_far, w_far, hx_far, cot_far, out_ref, wo_ref, buf, hx_ref, cot_ref,
    gate_ref, x_ref, few, sems,
):
    copies = fetched([(gate_far, gate_ref), (wo_far, wo_ref), (x_far, x_ref)], few)
    later = columns(w_far, buf, sems, (0, 1, 2, 3))
    later += fetched([(hx_far, hx_ref), (cot_far, cot_ref)], few.at[pl.ds(3, 2)])
    col, row, first, second = slot_ids(ids_ref)
    rank = jnp.sum(jnp.where((col == row) & (second < first), 1, 0), axis=1, keepdims=True)
    slot = col * CAP + rank
    hits = (lax.broadcasted_iota(jnp.int32, (256, 4 * CAP), 1) == slot).astype(F32).astype(BF)
    heads = []
    for h in range(HEADS):
        rows = jnp.concatenate([ret_ref[u * HEADS + h] for u in range(4)], axis=0)
        heads.append(dot(hits, rows))
    normed, _ = normalize(jnp.concatenate(heads, axis=1))
    copies[0].wait()
    mixed = (normed * gate_ref[...].astype(F32)).astype(BF)
    copies[1].wait()
    more = dot(mixed, wo_ref[...])
    copies[2].wait()
    out_ref[...] = (x_ref[...].astype(F32) + more).astype(BF)
    for copy in later:
        copy.wait()


def turned(value, axis, size, steps):
    return lax.ppermute(value, axis, [(i, (i + steps) % size) for i in range(size)])


def crossed(value, steps):
    pairs = []
    for c in range(2):
        for y in range(4):
            for xh in range(2):
                pairs.append(((c * 4 + y) * 2 + xh, (xh * 4 + (y + steps) % 4) * 2 + c))
    return lax.ppermute(value, ("c", "y", "xh"), pairs)


def across(value):
    return lax.ppermute(value, "c", [(0, 1), (1, 0)])


def along(value, way, cross):
    pairs = []
    for c in range(2):
        step = way if c == 0 else -way
        for z in range(4):
            pairs.append((4 * c + z, 4 * (c ^ cross) + (z + step) % 4))
    return lax.ppermute(value, ("c", "z"), pairs)


def per_device(hist_x, hist_cot, cand_x, cand_loop, hist_len, w_proj, w_out):
    y, xh, z, c = (lax.axis_index(n) for n in ("y", "xh", "z", "c"))
    x_rows = hist_x.reshape(128, 1024)
    cot = hist_cot.reshape(128, 1024)
    info = jnp.stack([hist_len[0], (y * 8 + xh * 4 + z) * 128, y, c, z]).astype(jnp.int32)
    held = pl.BlockSpec(memory_space=pltpu.VMEM)
    far = pl.BlockSpec(memory_space=pltpu.HBM)

    def weights(count):
        return [pltpu.VMEM((count, 1024, 512), BF), pltpu.SemaphoreType.DMA((count,))]

    def relayed(values, after):
        return call(nothing, "relay", (1,), [], [], [], [], 1_000, after, carry=values)()

    *sent, slope, gate, gm = call(
        project_all, "project_all", (1,), [SMEM, far, far, far, far],
        [shaped((128, 512))] * 4 + [shaped((4, 128, 512))] + [pltpu.HBM((128, 512), BF)] * 2,
        [held] * 5 + [pl.BlockSpec((128, 512), lambda i: (0, 0))] * 2,
        [
            pltpu.VMEM((128, 1024), BF), pltpu.VMEM((128, 512), BF), pltpu.VMEM((128, 1024), BF),
            pltpu.VMEM((128, 1024), BF), pltpu.VMEM((512, 1024), BF), pltpu.SemaphoreType.DMA((3,)),
        ] + weights(4), 700_000_000, (), 16,
    )(info, x_rows, cot, w_out, w_proj)
    parts = [crossed(v, k) for k, v in enumerate(sent)]

    sent_cand, cand_gate = call(
        project_cand, "project_cand", (1,), [held, held, far],
        [shaped((16, 128, 128)), shaped((256, 512))], [held] * 2,
        [pltpu.VMEM((256, 1024), BF)] + weights(2), 700_000_000, (slope,),
    )(cand_loop, cand_x, w_proj)

    own, sent_cand = call(
        arrange, "arrange", (1,), [SMEM] + [held] * 4, shaped((4, 128, 384)), held, [], 1_000_000,
        (cand_gate,), carry=(sent_cand,),
    )(info, *parts)
    own = own.reshape(512, 384)
    own_pair = across(own)
    plus, minus = along(own, 1, 0), along(own, -1, 0)
    arrived = lax.all_to_all(sent_cand, ("xl", "xh", "y"), 0, 0, tiled=True)
    last = [along(plus, 1, 0), along(plus, 1, 1)]
    kvq = [own, own_pair, plus, across(plus), minus, across(minus)]

    q_spec = held
    acc_spec = held

    def cand_part(kvs, total, end, after):
        begin = total is None
        return call(
            functools.partial(cand_attend, len(kvs), begin, end), "cand_attend", (1,),
            [q_spec] + [held] * len(kvs) + ([] if begin else [acc_spec]),
            shaped((16, 128, 128)) if end else shaped((2048, 128), F32),
            q_spec if end else acc_spec, [], 600_000_000 * len(kvs), after, 20,
        )(arrived, *kvs, *([] if begin else [total]))

    att = call(
        hist_begin, "hist_begin", (1,), [SMEM] + [held] * 6,
        shaped((512, 128), F32), held, [], 1_000,
    )(info, *kvq)
    total = cand_part(kvq, None, False, (att,))
    att, stats = call(
        hist_end, "hist_end", (1,), [SMEM] + [held] * 8,
        [shaped((512, 128), F32), shaped((8, 512), F32)], [held] * 2,
        [pltpu.VMEM((512, 128), F32)], 400_000_000, (total,),
    )(info, *parts, own, *last, att)
    all_stats = [stats] + [turned(stats, "y", 4, k) for k in (1, 2, 3)]
    weighed = cand_part(last, total, True, (stats,))
    ga, normed = call(
        normed_grads, "normed_grads", (1,), [SMEM] + [held] * 9,
        [shaped((512, 128))] * 2, [held] * 2,
        [pltpu.VMEM((512, 128), F32)], 1_000_000, (weighed,),
    )(info, *parts, att, *all_stats)

    ga_plus, ga_minus = along(ga, 1, 0), along(ga, -1, 0)
    dq = call(
        hist_dq, "hist_dq", (1,), [SMEM] + [held] * 9,
        shaped((4, 128, 128)), held, [], 2_000_000_000,
    )(info, ga, *kvq, *last)
    ga_plus, ga_minus = relayed([ga_plus, ga_minus], (dq,))
    ga_last = [along(ga_plus, 1, 0), along(ga_plus, 1, 1)]
    gas = [ga, across(ga), ga_plus, across(ga_plus), ga_minus, across(ga_minus)]
    key_sums = call(
        hist_dkv_begin, "hist_dkv_begin", (1,), [SMEM] + [held] * 12,
        shaped((2, 256, 256), F32), held, [], 2_000_000_000,
    )(info, *kvq, *gas)
    (leaving,) = relayed([weighed], (key_sums, *ga_last))
    returned = lax.all_to_all(leaving, ("xl", "xh", "y"), 0, 0, tiled=True)
    grads = call(
        hist_dkv_end, "hist_dkv_end", (1,), [SMEM] + [held] * 8,
        [shaped((128, 512))] * 4, [held] * 4, [pltpu.VMEM((4, 128, 512), BF)], 800_000_000,
    )(info, dq, normed, own, *last, *ga_last, key_sums)
    back = [crossed(v, k) for k, v in enumerate(grads)]

    cand_out, wo_near, w_near, x_near, cot_near = call(
        cand_close, "cand_close", (1,), [held, far, held] + [far] * 5,
        [pltpu.HBM((256, 1024), BF), shaped((512, 1024)), shaped((4, 1024, 512))] + [shaped((128, 1024))] * 2,
        [pl.BlockSpec((256, 1024), lambda i: (0, 0))] + [held] * 4,
        [
            pltpu.VMEM((256, 512), BF), pltpu.VMEM((256, 1024), BF),
            pltpu.SemaphoreType.DMA((5,)), pltpu.SemaphoreType.DMA((4,)),
        ], 400_000_000, (grads[0],),
    )(cand_loop, cand_gate, returned, cand_x, w_out, w_proj, x_rows, cot)
    final = pltpu.HBM((1, 128, 1024), BF)
    hist_out, hist_grad = call(
        hist_close, "hist_close", (1,), [SMEM] + [held] * 11,
        [final] * 2, [far] * 2,
        [
            pltpu.VMEM((128, 512), BF), pltpu.VMEM((4, 128, 512), BF), pltpu.VMEM((128, 1024), BF),
            pltpu.VMEM((128, 1024), BF), pltpu.SemaphoreType.DMA((2,)),
        ], 700_000_000,
    )(info, x_near, cot_near, slope, wo_near, w_near, gate, gm, *back)
    return hist_out, hist_grad, cand_out


def solution(mesh):
    split = Mesh(mesh.devices.reshape(2, 2, 4, 2, 4), ("xl", "c", "y", "xh", "z"))
    users, rows = ("xl", "c"), ("y", "xh", "z")
    hist = P(users, rows, None)
    cand = P(users + rows, None)
    return jax.shard_map(
        per_device,
        mesh=split,
        in_specs=(hist, hist, cand, cand, P(users), P(), P()),
        out_specs=(hist, hist, cand),
        check_vma=False,
    )
```

```python
import functools

import jax
import jax.numpy as jnp
from jax import lax
from jax.experimental import pallas as pl
from jax.experimental.pallas import tpu as pltpu
from jax.sharding import Mesh, PartitionSpec as P

HS = 128
CAP = 128
HEADS = 4
EPS = 1e-05
SCALE = HS ** (-0.5)
BF = jnp.bfloat16
F32 = jnp.float32

NN = (((1,), (0,)), ((), ()))
NT = (((1,), (1,)), ((), ()))
SMEM = pl.BlockSpec(memory_space=pltpu.SMEM)


def dot(a, b, dims=NN):
    return lax.dot_general(a, b, dims, preferred_element_type=F32)


def whole(shape):
    return pl.BlockSpec(memory_space=pltpu.VMEM)


def call(body, name, grid, in_specs, outs, out_specs, scratch, flops, after=(), limit=12, carry=()):
    count, extra = len(in_specs), len(after) + len(carry)
    single = not isinstance(outs, (list, tuple))
    outs = [outs] if single else list(outs)
    out_specs = [out_specs] if single else list(out_specs)
    kept = len(outs)
    anywhere = pl.BlockSpec(memory_space=pl.ANY)

    def without(*refs):
        first = count + extra
        return body(*refs[:count], *refs[first : first + kept], *refs[first + kept + len(carry) :])

    made = pl.pallas_call(
        without,
        out_shape=outs + [jax.ShapeDtypeStruct(v.shape, v.dtype) for v in carry],
        grid=grid,
        in_specs=list(in_specs) + [anywhere] * extra,
        out_specs=out_specs + [anywhere] * len(carry),
        input_output_aliases={count + len(after) + n: kept + n for n in range(len(carry))},
        scratch_shapes=scratch,
        compiler_params=pltpu.CompilerParams(vmem_limit_bytes=limit * 1024 * 1024),
        cost_estimate=pl.CostEstimate(flops=flops, transcendentals=0, bytes_accessed=(1 << 20) if flops > 1000 else 1000),
        name=name,
    )

    def run(*args):
        pinned = []
        for arg, spec in zip(args, in_specs):
            if spec is not SMEM:
                space = spec.memory_space or pltpu.VMEM
                arg = pltpu.with_memory_space_constraint(arg, space)
            pinned.append(arg)
        got = made(*pinned, *after, *carry)
        return got[0] if len(got) == 1 and single else got

    return run


def shaped(shape, dtype=BF):
    return pltpu.VMEM(shape, dtype)


def normalize(values):
    center = values - jnp.mean(values, axis=-1, keepdims=True)
    spread = lax.rsqrt(jnp.mean(center * center, axis=-1, keepdims=True) + EPS)
    return center * spread, spread


def silu_parts(pre):
    half = 0.5 * pre
    sig = 0.5 + 0.5 * jnp.tanh(half)
    act = pre * sig
    return act, sig + act * (1.0 - sig)


def columns(w_ref, buf, sems, picks):
    copies = []
    for slot, pick in enumerate(picks):
        copy = pltpu.make_async_copy(w_ref.at[:, pl.ds(512 * pick, 512)], buf.at[slot], sems.at[slot])
        copy.start()
        copies.append(copy)
    return copies


def slot_ids(ids_ref):
    col = ids_ref[...]
    first = lax.broadcasted_iota(jnp.int32, (256, 256), 0)
    second = lax.broadcasted_iota(jnp.int32, (256, 256), 1)
    row = jnp.sum(jnp.where(first == second, col, 0), axis=0, keepdims=True)
    return col, row, first, second


def fetched(pairs, sems):
    copies = []
    for slot, (source, target) in enumerate(pairs):
        copy = pltpu.make_async_copy(source, target, sems.at[slot])
        copy.start()
        copies.append(copy)
    return copies


def project_all(
    info, x_far, cot_far, wo_far, w_ref, k0, k1, k2, k3, slope_ref, gate_far, gm_far,
    gate_ref, gm_ref, xn_ref, act_ref, x_ref, cot_ref, wo_ref, few, buf, sems,
):
    (got_x,) = fetched([(x_far, x_ref)], few)
    copies = columns(w_ref, buf, sems, (3, 1, 0))
    rest = fetched([(cot_far, cot_ref), (wo_far, wo_ref)], few.at[pl.ds(1, 2)])
    copies += columns(w_ref, buf.at[pl.ds(3, 1)], sems.at[pl.ds(3, 1)], (2,))
    got_x.wait()
    normed, _ = normalize(x_ref[...].astype(F32))
    xn_ref[...] = normed.astype(BF)
    rows = info[1] + lax.broadcasted_iota(jnp.int32, (128, 1), 0)
    inside = jnp.where(rows < info[0], 1.0, 0.0)
    length = jnp.full((128, 1), info[0], jnp.int32).astype(F32)

    def put(values, part):
        act_ref[...] = values.astype(BF)
        for k, out in enumerate((k0, k1, k2, k3)):
            lane = pl.multiple_of(((info[2] + k) & 3) * HS, HS)
            out[:, part * HS : (part + 1) * HS] = act_ref[:, pl.ds(lane, HS)]

    def project(slot, which):
        copies[slot].wait()
        act, slope = silu_parts(dot(xn_ref[...], buf[slot]))
        slope_ref[which] = slope.astype(BF)
        return act

    put(project(0, 0) * inside, 0)
    put(project(1, 1) * (inside / length), 1)
    gate_ref[...] = project(2, 3).astype(BF)
    leaving = fetched([(gate_ref, gate_far)], few.at[pl.ds(3, 1)])
    for copy in rest:
        copy.wait()
    gm = dot(cot_ref[...], wo_ref[...], NT)
    gm_ref[...] = gm.astype(BF)
    leaving += fetched([(gm_ref, gm_far)], few.at[pl.ds(4, 1)])
    put(gm * gate_ref[...].astype(F32), 3)
    put(project(3, 2) * (0.5 * SCALE), 2)
    for copy in leaving:
        copy.wait()


def arrange(info, a0, a1, a2, a3, out_ref):
    for k, a in enumerate((a0, a1, a2, a3)):
        out_ref[(info[2] - k) & 3] = a[:, : 3 * HS]


def project_cand(ids_ref, x_ref, w_ref, sent_ref, gate_ref, xn_ref, buf, sems):
    copies = columns(w_ref, buf, sems, (2, 0))
    xn_ref[...] = normalize(x_ref[...].astype(F32))[0].astype(BF)
    col, row, first, second = slot_ids(ids_ref)
    rank = jnp.sum(jnp.where((col == row) & (first < second), 1, 0), axis=0, keepdims=True)
    slot = row * CAP + rank
    hits = (lax.broadcasted_iota(jnp.int32, (4 * CAP, 256), 0) == slot).astype(F32).astype(BF)
    copies[0].wait()
    act, _ = silu_parts(dot(xn_ref[...], buf[0]))
    placed = dot(hits, (act * (0.5 * SCALE)).astype(BF)).astype(BF)
    for u in range(4):
        for h in range(HEADS):
            sent_ref[u * HEADS + h] = placed[u * CAP : (u + 1) * CAP, h * HS : (h + 1) * HS]
    copies[1].wait()
    act, _ = silu_parts(dot(xn_ref[...], buf[1]))
    gate_ref[...] = act.astype(BF)


def nothing(*refs):
    del refs


def order_of(info):
    c, z = info[3], info[4]
    o = 1 - c
    side = 1 - 2 * c
    near, far = (z - side) & 3, (z + side) & 3
    across = (z + 2) & 3
    spots = [(c, z), (o, z), (c, near), (o, far), (c, far), (o, near), (c, across), (o, across)]
    return [4 * core + spot for core, spot in spots]


def corner_masks(info, backward):
    order = order_of(info)
    first = lax.broadcasted_iota(jnp.int32, (256, 256), 0)
    second = lax.broadcasted_iota(jnp.int32, (256, 256), 1)
    early, late = (first, second) if backward else (second, first)
    below = (early >> 7) < (late >> 7)
    gap = jnp.where((early >> 7) == (late >> 7), early - late, 512)
    gap = jnp.where(below, -512, gap)
    masks = []
    for o in order:
        ahead = o > order[0] if backward else o < order[0]
        lead = jnp.where(ahead, 128, jnp.where(o == order[0], 0, -128))
        masks.append((gap <= lead).astype(F32).astype(BF))
    return masks


def cand_attend(count, begin, end, *refs):
    q_ref, kvs, rest = refs[0], refs[1 : 1 + count], refs[1 + count :]
    q = q_ref[...].reshape(16 * CAP, HS)
    total = None if begin else rest[0][...]
    for block in kvs:
        half = dot(q, block[:, :HS], NT).astype(BF)
        probs = half + half * jnp.tanh(half)
        more = dot(probs, block[:, HS : 2 * HS])
        total = more if total is None else total + more
    if end:
        rest[-1][...] = total.astype(BF).reshape(16, CAP, HS)
    else:
        rest[-1][...] = total


def attend_rows(q_ref, blocks, masks, old_ref, att_ref):
    for y in range(2):
        rows = slice(y * 256, (y + 1) * 256)
        q = q_ref[rows, 2 * HS :]
        total = None if old_ref is None else old_ref[rows, :]
        for block, mask in zip(blocks, masks):
            half = dot(q, block[: 256 * (y + 1), :HS], NT).astype(BF)
            probs = half + half * jnp.tanh(half)
            last = probs[:, 256 * y :] * mask
            probs = last if y == 0 else jnp.concatenate([probs[:, : 256 * y], last], axis=1)
            more = dot(probs, block[: 256 * (y + 1), HS : 2 * HS])
            total = more if total is None else total + more
        att_ref[rows, :] = total


def hist_begin(info, *refs):
    attend_rows(refs[0], refs[:6], corner_masks(info, False)[:6], None, refs[6])


def hist_end(info, p0, p1, p2, p3, own_ref, b0, b1, old_ref, att_ref, stat_ref, g_ref):
    for k, part in enumerate((p0, p1, p2, p3)):
        rows = pl.ds(pl.multiple_of(((info[2] - k) & 3) * 128, 128), 128)
        g_ref[rows, :] = part[:, 3 * HS :].astype(F32)
    attend_rows(own_ref, (b0, b1), corner_masks(info, False)[6:], old_ref, att_ref)
    att = att_ref[...]
    g = g_ref[...]
    mean = jnp.mean(att, axis=1, keepdims=True)
    center = att - mean
    lane = lax.broadcasted_iota(jnp.int32, (512, 128), 1)
    stats = jnp.where(lane == 0, mean, 0.0)
    stats = jnp.where(lane == 1, jnp.sum(center * center, axis=1, keepdims=True), stats)
    stats = jnp.where(lane == 2, jnp.sum(g, axis=1, keepdims=True), stats)
    stats = jnp.where(lane == 3, jnp.sum(g * center, axis=1, keepdims=True), stats)
    stat_ref[...] = jnp.transpose(stats)[:8]


def normed_grads(info, p0, p1, p2, p3, att_ref, s0, s1, s2, s3, ga_ref, normed_ref, g_ref):
    for k, part in enumerate((p0, p1, p2, p3)):
        y = (info[2] - k) & 3
        rows = pl.ds(pl.multiple_of(y * 128, 128), 128)
        g_ref[rows, :] = part[:, 3 * HS :].astype(F32)
    stats = [s[...] for s in (s0, s1, s2, s3)]
    mean = sum(s[0:1] for s in stats) * 0.25
    squares = sum(s[1:2] + HS * (s[0:1] - mean) * (s[0:1] - mean) for s in stats)
    spread = lax.rsqrt(squares * (1.0 / (HEADS * HS)) + EPS)
    g_mean = sum(s[2:3] for s in stats) * (1.0 / (HEADS * HS))
    ga_sum = sum(s[3:4] + s[2:3] * (s[0:1] - mean) for s in stats)
    ga_mean = ga_sum * spread * (1.0 / (HEADS * HS))
    line = lax.broadcasted_iota(jnp.int32, (128, 512), 0)
    packed = jnp.where(line == 0, mean, 0.0)
    packed = jnp.where(line == 1, spread, packed)
    packed = jnp.where(line == 2, g_mean, packed)
    packed = jnp.where(line == 3, ga_mean, packed)
    cols = jnp.transpose(packed)
    spread_c = cols[:, 1:2]
    normed = (att_ref[...] - cols[:, 0:1]) * spread_c
    ga_ref[...] = (spread_c * (g_ref[...] - cols[:, 2:3] - normed * cols[:, 3:4])).astype(BF)
    normed_ref[...] = normed.astype(BF)


def slope_times(half, grads):
    t = jnp.tanh(half)
    probs = half + half * t
    slope = (1.0 + t + probs * (1.0 - t)).astype(BF)
    return probs, grads * slope


def hist_dq(info, ga_ref, *refs):
    blocks, dq_ref = refs[:8], refs[8]
    masks = corner_masks(info, False)
    for y in range(2):
        q = blocks[0][y * 256 : (y + 1) * 256, 2 * HS :]
        ga = ga_ref[y * 256 : (y + 1) * 256, :]
        total = None
        for block, mask in zip(blocks, masks):
            key = block[: 256 * (y + 1), :HS]
            half = dot(q, key, NT).astype(BF)
            _, ds = slope_times(half, dot(ga, block[: 256 * (y + 1), HS : 2 * HS], NT).astype(BF))
            last = ds[:, 256 * y :] * mask
            ds = last if y == 0 else jnp.concatenate([ds[:, : 256 * y], last], axis=1)
            more = dot(ds, key)
            total = more if total is None else total + more
        dq_ref[2 * y : 2 * y + 2] = (total * (0.5 * SCALE)).astype(BF).reshape(2, 128, HS)


def key_grads(own_ref, blocks, gas, masks, y, dk, dv):
    key = own_ref[y * 256 : (y + 1) * 256, :HS]
    value = own_ref[y * 256 : (y + 1) * 256, HS : 2 * HS]
    for block, ga_block, mask in zip(blocks, gas, masks):
        q = block[256 * y :, 2 * HS :]
        ga = ga_block[256 * y :, :]
        half = dot(key, q, NT).astype(BF)
        probs, ds = slope_times(half, dot(value, ga, NT).astype(BF))
        p_first = probs[:, :256] * mask
        d_first = ds[:, :256] * mask
        if y < 1:
            probs = jnp.concatenate([p_first, probs[:, 256:]], axis=1)
            ds = jnp.concatenate([d_first, ds[:, 256:]], axis=1)
        else:
            probs, ds = p_first, d_first
        more_k = dot(ds, q)
        more_v = dot(probs, ga)
        dk = more_k if dk is None else dk + more_k
        dv = more_v if dv is None else dv + more_v
    return dk, dv


def hist_dkv_begin(info, *refs):
    masks = corner_masks(info, True)[:6]
    for y in range(2):
        dk, dv = key_grads(refs[0], refs[:6], refs[6:12], masks, y, None, None)
        refs[12][y, :, :HS] = dk
        refs[12][y, :, HS:] = dv


def hist_dkv_end(info, dq_ref, normed_ref, own_ref, b0, b1, g0, g1, old_ref, k0, k1, k2, k3, all_ref):
    masks = corner_masks(info, True)[6:]
    for y in range(2):
        dk, dv = key_grads(own_ref, (b0, b1), (g0, g1), masks, y, old_ref[y, :, :HS], old_ref[y, :, HS:])
        all_ref[2 * y : 2 * y + 2, :, HS : 2 * HS] = dk.astype(BF).reshape(2, 128, HS)
        all_ref[2 * y : 2 * y + 2, :, 2 * HS : 3 * HS] = dv.astype(BF).reshape(2, 128, HS)
    for y in range(4):
        all_ref[y, :, :HS] = dq_ref[y]
        all_ref[y, :, 3 * HS :] = normed_ref[y * 128 : (y + 1) * 128, :]
    for k, out in enumerate((k0, k1, k2, k3)):
        out[...] = all_ref[(info[2] + k) & 3]


def hist_close(
    info, x_ref, cot_ref, slope_ref, wo_ref, buf, gate_ref, gm_ref, b0, b1, b2, b3, out_far, grad_far,
    mixed_ref, hid_ref, out_ref, grad_ref, few,
):
    length = jnp.full((128, 1), info[0], jnp.int32).astype(F32)
    for k, b in enumerate((b0, b1, b2, b3)):
        lanes = pl.ds(pl.multiple_of(((info[2] - k) & 3) * HS, HS), HS)

        def put(part, grads, which):
            hid_ref[part, :, lanes] = (grads * slope_ref[which, :, lanes].astype(F32)).astype(BF)

        normed = b[:, 3 * HS :].astype(F32)
        put(0, normed * gm_ref[:, lanes].astype(F32), 3)
        put(1, b[:, 2 * HS : 3 * HS].astype(F32) / length, 1)
        put(2, b[:, :HS].astype(F32), 2)
        put(3, b[:, HS : 2 * HS].astype(F32), 0)
        mixed_ref[:, lanes] = (normed * gate_ref[:, lanes].astype(F32)).astype(BF)
    x = x_ref[...].astype(F32)
    out_ref[...] = (x + dot(mixed_ref[...], wo_ref[...])).astype(BF)
    done = fetched([(out_ref, out_far.at[0])], few)
    e = None
    for part in range(4):
        more = dot(hid_ref[part], buf[part], NT)
        e = more if e is None else e + more
    normed, spread = normalize(x)
    back = spread * (
        e - jnp.mean(e, axis=-1, keepdims=True) - normed * jnp.mean(e * normed, axis=-1, keepdims=True)
    )
    grad_ref[...] = (cot_ref[...].astype(F32) + back).astype(BF)
    done += fetched([(grad_ref, grad_far.at[0])], few.at[pl.ds(1, 1)])
    for copy in done:
        copy.wait()


def cand_close(
    ids_ref, gate_far, ret_ref, x_far, wo_far, w_far, hx_far, cot_far, out_ref, wo_ref, buf, hx_ref, cot_ref,
    gate_ref, x_ref, few, sems,
):
    copies = fetched([(gate_far, gate_ref), (wo_far, wo_ref), (x_far, x_ref)], few)
    later = columns(w_far, buf, sems, (0, 1, 2, 3))
    later += fetched([(hx_far, hx_ref), (cot_far, cot_ref)], few.at[pl.ds(3, 2)])
    col, row, first, second = slot_ids(ids_ref)
    rank = jnp.sum(jnp.where((col == row) & (second < first), 1, 0), axis=1, keepdims=True)
    slot = col * CAP + rank
    hits = (lax.broadcasted_iota(jnp.int32, (256, 4 * CAP), 1) == slot).astype(F32).astype(BF)
    heads = []
    for h in range(HEADS):
        rows = jnp.concatenate([ret_ref[u * HEADS + h] for u in range(4)], axis=0)
        heads.append(dot(hits, rows))
    normed, _ = normalize(jnp.concatenate(heads, axis=1))
    copies[0].wait()
    mixed = (normed * gate_ref[...].astype(F32)).astype(BF)
    copies[1].wait()
    more = dot(mixed, wo_ref[...])
    copies[2].wait()
    out_ref[...] = (x_ref[...].astype(F32) + more).astype(BF)
    for copy in later:
        copy.wait()


def turned(value, axis, size, steps):
    return lax.ppermute(value, axis, [(i, (i + steps) % size) for i in range(size)])


def crossed(value, steps):
    pairs = []
    for c in range(2):
        for y in range(4):
            for xh in range(2):
                pairs.append(((c * 4 + y) * 2 + xh, (xh * 4 + (y + steps) % 4) * 2 + c))
    return lax.ppermute(value, ("c", "y", "xh"), pairs)


def across(value):
    return lax.ppermute(value, "c", [(0, 1), (1, 0)])


def along(value, way, cross):
    pairs = []
    for c in range(2):
        step = way if c == 0 else -way
        for z in range(4):
            pairs.append((4 * c + z, 4 * (c ^ cross) + (z + step) % 4))
    return lax.ppermute(value, ("c", "z"), pairs)


def per_device(hist_x, hist_cot, cand_x, cand_loop, hist_len, w_proj, w_out):
    y, xh, z, c = (lax.axis_index(n) for n in ("y", "xh", "z", "c"))
    x_rows = hist_x.reshape(128, 1024)
    cot = hist_cot.reshape(128, 1024)
    info = jnp.stack([hist_len[0], (y * 8 + xh * 4 + z) * 128, y, c, z]).astype(jnp.int32)
    held = pl.BlockSpec(memory_space=pltpu.VMEM)
    far = pl.BlockSpec(memory_space=pltpu.HBM)

    def weights(count):
        return [pltpu.VMEM((count, 1024, 512), BF), pltpu.SemaphoreType.DMA((count,))]

    def relayed(values, after):
        return call(nothing, "relay", (1,), [], [], [], [], 1_000, after, carry=values)()

    *sent, slope, gate, gm = call(
        project_all, "project_all", (1,), [SMEM, far, far, far, far],
        [shaped((128, 512))] * 4 + [shaped((4, 128, 512))] + [pltpu.HBM((128, 512), BF)] * 2,
        [held] * 5 + [far] * 2,
        [
            pltpu.VMEM((128, 512), BF), pltpu.VMEM((128, 512), BF),
            pltpu.VMEM((128, 1024), BF), pltpu.VMEM((128, 512), BF), pltpu.VMEM((128, 1024), BF),
            pltpu.VMEM((128, 1024), BF), pltpu.VMEM((512, 1024), BF), pltpu.SemaphoreType.DMA((5,)),
        ] + weights(4), 700_000_000, (), 16,
    )(info, x_rows, cot, w_out, w_proj)
    parts = [crossed(v, k) for k, v in enumerate(sent)]

    sent_cand, cand_gate = call(
        project_cand, "project_cand", (1,), [held, held, far],
        [shaped((16, 128, 128)), shaped((256, 512))], [held] * 2,
        [pltpu.VMEM((256, 1024), BF)] + weights(2), 700_000_000, (slope,),
    )(cand_loop, cand_x, w_proj)

    own, sent_cand = call(
        arrange, "arrange", (1,), [SMEM] + [held] * 4, shaped((4, 128, 384)), held, [], 1_000_000,
        (cand_gate,), carry=(sent_cand,),
    )(info, *parts)
    own = own.reshape(512, 384)
    own_pair = across(own)
    plus, minus = along(own, 1, 0), along(own, -1, 0)
    arrived = lax.all_to_all(sent_cand, ("xl", "xh", "y"), 0, 0, tiled=True)
    last = [along(plus, 1, 0), along(plus, 1, 1)]
    kvq = [own, own_pair, plus, across(plus), minus, across(minus)]

    q_spec = held
    acc_spec = held

    def cand_part(kvs, total, end, after):
        begin = total is None
        return call(
            functools.partial(cand_attend, len(kvs), begin, end), "cand_attend", (1,),
            [q_spec] + [held] * len(kvs) + ([] if begin else [acc_spec]),
            shaped((16, 128, 128)) if end else shaped((2048, 128), F32),
            q_spec if end else acc_spec, [], 600_000_000 * len(kvs), after, 20,
        )(arrived, *kvs, *([] if begin else [total]))

    att = call(
        hist_begin, "hist_begin", (1,), [SMEM] + [held] * 6,
        shaped((512, 128), F32), held, [], 1_000,
    )(info, *kvq)
    total = cand_part(kvq, None, False, (att,))
    att, stats = call(
        hist_end, "hist_end", (1,), [SMEM] + [held] * 8,
        [shaped((512, 128), F32), shaped((8, 512), F32)], [held] * 2,
        [pltpu.VMEM((512, 128), F32)], 400_000_000, (total,),
    )(info, *parts, own, *last, att)
    all_stats = [stats] + [turned(stats, "y", 4, k) for k in (1, 2, 3)]
    weighed = cand_part(last, total, True, (stats,))
    ga, normed = call(
        normed_grads, "normed_grads", (1,), [SMEM] + [held] * 9,
        [shaped((512, 128))] * 2, [held] * 2,
        [pltpu.VMEM((512, 128), F32)], 1_000_000, (weighed,),
    )(info, *parts, att, *all_stats)

    ga_plus, ga_minus = along(ga, 1, 0), along(ga, -1, 0)
    dq = call(
        hist_dq, "hist_dq", (1,), [SMEM] + [held] * 9,
        shaped((4, 128, 128)), held, [], 2_000_000_000,
    )(info, ga, *kvq, *last)
    ga_plus, ga_minus = relayed([ga_plus, ga_minus], (dq,))
    ga_last = [along(ga_plus, 1, 0), along(ga_plus, 1, 1)]
    gas = [ga, across(ga), ga_plus, across(ga_plus), ga_minus, across(ga_minus)]
    key_sums = call(
        hist_dkv_begin, "hist_dkv_begin", (1,), [SMEM] + [held] * 12,
        shaped((2, 256, 256), F32), held, [], 2_000_000_000,
    )(info, *kvq, *gas)
    (leaving,) = relayed([weighed], (key_sums, *ga_last))
    returned = lax.all_to_all(leaving, ("xl", "xh", "y"), 0, 0, tiled=True)
    grads = call(
        hist_dkv_end, "hist_dkv_end", (1,), [SMEM] + [held] * 8,
        [shaped((128, 512))] * 4, [held] * 4, [pltpu.VMEM((4, 128, 512), BF)], 800_000_000,
    )(info, dq, normed, own, *last, *ga_last, key_sums)
    back = [crossed(v, k) for k, v in enumerate(grads)]

    cand_out, wo_near, w_near, x_near, cot_near = call(
        cand_close, "cand_close", (1,), [held, far, held] + [far] * 5,
        [pltpu.HBM((256, 1024), BF), shaped((512, 1024)), shaped((4, 1024, 512))] + [shaped((128, 1024))] * 2,
        [pl.BlockSpec((256, 1024), lambda i: (0, 0))] + [held] * 4,
        [
            pltpu.VMEM((256, 512), BF), pltpu.VMEM((256, 1024), BF),
            pltpu.SemaphoreType.DMA((5,)), pltpu.SemaphoreType.DMA((4,)),
        ], 400_000_000, (grads[0],),
    )(cand_loop, cand_gate, returned, cand_x, w_out, w_proj, x_rows, cot)
    final = pltpu.HBM((1, 128, 1024), BF)
    hist_out, hist_grad = call(
        hist_close, "hist_close", (1,), [SMEM] + [held] * 11,
        [final] * 2, [far] * 2,
        [
            pltpu.VMEM((128, 512), BF), pltpu.VMEM((4, 128, 512), BF), pltpu.VMEM((128, 1024), BF),
            pltpu.VMEM((128, 1024), BF), pltpu.SemaphoreType.DMA((2,)),
        ], 700_000_000,
    )(info, x_near, cot_near, slope, wo_near, w_near, gate, gm, *back)
    return hist_out, hist_grad, cand_out


def solution(mesh):
    split = Mesh(mesh.devices.reshape(2, 2, 4, 2, 4), ("xl", "c", "y", "xh", "z"))
    users, rows = ("xl", "c"), ("y", "xh", "z")
    hist = P(users, rows, None)
    cand = P(users + rows, None)
    return jax.shard_map(
        per_device,
        mesh=split,
        in_specs=(hist, hist, cand, cand, P(users), P(), P()),
        out_specs=(hist, hist, cand),
        check_vma=False,
    )
```

```python
import functools

import jax
import jax.numpy as jnp
from jax import lax
from jax.experimental import pallas as pl
from jax.experimental.pallas import tpu as pltpu
from jax.sharding import Mesh, PartitionSpec as P

HS = 128
CAP = 128
HEADS = 4
EPS = 1e-05
SCALE = HS ** (-0.5)
BF = jnp.bfloat16
F32 = jnp.float32

NN = (((1,), (0,)), ((), ()))
NT = (((1,), (1,)), ((), ()))
SMEM = pl.BlockSpec(memory_space=pltpu.SMEM)


def dot(a, b, dims=NN):
    return lax.dot_general(a, b, dims, preferred_element_type=F32)


def whole(shape):
    return pl.BlockSpec(memory_space=pltpu.VMEM)


def call(body, name, grid, in_specs, outs, out_specs, scratch, flops, after=(), limit=12, carry=()):
    count, extra = len(in_specs), len(after) + len(carry)
    single = not isinstance(outs, (list, tuple))
    outs = [outs] if single else list(outs)
    out_specs = [out_specs] if single else list(out_specs)
    kept = len(outs)
    anywhere = pl.BlockSpec(memory_space=pl.ANY)

    def without(*refs):
        first = count + extra
        return body(*refs[:count], *refs[first : first + kept], *refs[first + kept + len(carry) :])

    made = pl.pallas_call(
        without,
        out_shape=outs + [jax.ShapeDtypeStruct(v.shape, v.dtype) for v in carry],
        grid=grid,
        in_specs=list(in_specs) + [anywhere] * extra,
        out_specs=out_specs + [anywhere] * len(carry),
        input_output_aliases={count + len(after) + n: kept + n for n in range(len(carry))},
        scratch_shapes=scratch,
        compiler_params=pltpu.CompilerParams(vmem_limit_bytes=limit * 1024 * 1024),
        cost_estimate=pl.CostEstimate(flops=flops, transcendentals=0, bytes_accessed=(1 << 20) if flops > 1000 else 1000),
        name=name,
    )

    def run(*args):
        pinned = []
        for arg, spec in zip(args, in_specs):
            if spec is not SMEM:
                space = spec.memory_space or pltpu.VMEM
                arg = pltpu.with_memory_space_constraint(arg, space)
            pinned.append(arg)
        got = made(*pinned, *after, *carry)
        return got[0] if len(got) == 1 and single else got

    return run


def shaped(shape, dtype=BF):
    return pltpu.VMEM(shape, dtype)


def normalize(values):
    center = values - jnp.mean(values, axis=-1, keepdims=True)
    spread = lax.rsqrt(jnp.mean(center * center, axis=-1, keepdims=True) + EPS)
    return center * spread, spread


def silu_parts(pre):
    half = 0.5 * pre
    sig = 0.5 + 0.5 * jnp.tanh(half)
    act = pre * sig
    return act, sig + act * (1.0 - sig)


def columns(w_ref, buf, sems, picks):
    copies = []
    for slot, pick in enumerate(picks):
        copy = pltpu.make_async_copy(w_ref.at[:, pl.ds(512 * pick, 512)], buf.at[slot], sems.at[slot])
        copy.start()
        copies.append(copy)
    return copies


def slot_ids(ids_ref):
    col = ids_ref[...]
    first = lax.broadcasted_iota(jnp.int32, (256, 256), 0)
    second = lax.broadcasted_iota(jnp.int32, (256, 256), 1)
    row = jnp.sum(jnp.where(first == second, col, 0), axis=0, keepdims=True)
    return col, row, first, second


def fetched(pairs, sems):
    copies = []
    for slot, (source, target) in enumerate(pairs):
        copy = pltpu.make_async_copy(source, target, sems.at[slot])
        copy.start()
        copies.append(copy)
    return copies


def project_all(
    info, x_far, cot_far, wo_far, w_ref, k0, k1, k2, k3, slope_ref, gate_far, gm_far,
    gate_ref, gm_ref, xn_ref, act_ref, x_ref, cot_ref, wo_ref, few, buf, sems,
):
    (got_x,) = fetched([(x_far, x_ref)], few)
    copies = columns(w_ref, buf, sems, (3, 1, 0))
    rest = fetched([(cot_far, cot_ref), (wo_far, wo_ref)], few.at[pl.ds(1, 2)])
    copies += columns(w_ref, buf.at[pl.ds(3, 1)], sems.at[pl.ds(3, 1)], (2,))
    got_x.wait()
    normed, _ = normalize(x_ref[...].astype(F32))
    xn_ref[...] = normed.astype(BF)
    rows = info[1] + lax.broadcasted_iota(jnp.int32, (128, 1), 0)
    inside = jnp.where(rows < info[0], 1.0, 0.0)
    length = jnp.full((128, 1), info[0], jnp.int32).astype(F32)

    def put(values, part):
        act_ref[...] = values.astype(BF)
        for k, out in enumerate((k0, k1, k2, k3)):
            lane = pl.multiple_of(((info[2] + k) & 3) * HS, HS)
            out[:, part * HS : (part + 1) * HS] = act_ref[:, pl.ds(lane, HS)]

    def project(slot, which):
        copies[slot].wait()
        act, slope = silu_parts(dot(xn_ref[...], buf[slot]))
        slope_ref[which] = slope.astype(BF)
        return act

    put(project(0, 0) * inside, 0)
    put(project(1, 1) * (inside / length), 1)
    gate_ref[...] = project(2, 3).astype(BF)
    leaving = fetched([(gate_ref, gate_far)], few.at[pl.ds(3, 1)])
    for copy in rest:
        copy.wait()
    gm = dot(cot_ref[...], wo_ref[...], NT)
    gm_ref[...] = gm.astype(BF)
    leaving += fetched([(gm_ref, gm_far)], few.at[pl.ds(4, 1)])
    put(gm * gate_ref[...].astype(F32), 3)
    put(project(3, 2) * (0.5 * SCALE), 2)
    for copy in leaving:
        copy.wait()


def arrange(info, a0, a1, a2, a3, out_ref):
    for k, a in enumerate((a0, a1, a2, a3)):
        out_ref[(info[2] - k) & 3] = a[:, : 3 * HS]


def project_cand(ids_ref, x_ref, w_ref, sent_ref, gate_ref, xn_ref, buf, sems):
    copies = columns(w_ref, buf, sems, (2, 0))
    xn_ref[...] = normalize(x_ref[...].astype(F32))[0].astype(BF)
    col, row, first, second = slot_ids(ids_ref)
    rank = jnp.sum(jnp.where((col == row) & (first < second), 1, 0), axis=0, keepdims=True)
    slot = row * CAP + rank
    hits = (lax.broadcasted_iota(jnp.int32, (4 * CAP, 256), 0) == slot).astype(F32).astype(BF)
    copies[0].wait()
    act, _ = silu_parts(dot(xn_ref[...], buf[0]))
    placed = dot(hits, (act * (0.5 * SCALE)).astype(BF)).astype(BF)
    for u in range(4):
        for h in range(HEADS):
            sent_ref[u * HEADS + h] = placed[u * CAP : (u + 1) * CAP, h * HS : (h + 1) * HS]
    copies[1].wait()
    act, _ = silu_parts(dot(xn_ref[...], buf[1]))
    gate_ref[...] = act.astype(BF)


def nothing(*refs):
    del refs


def order_of(info):
    c, z = info[3], info[4]
    o = 1 - c
    side = 1 - 2 * c
    near, far = (z - side) & 3, (z + side) & 3
    across = (z + 2) & 3
    spots = [(c, z), (o, z), (c, near), (o, far), (c, far), (o, near), (c, across), (o, across)]
    return [4 * core + spot for core, spot in spots]


def corner_masks(info, backward):
    order = order_of(info)
    first = lax.broadcasted_iota(jnp.int32, (256, 256), 0)
    second = lax.broadcasted_iota(jnp.int32, (256, 256), 1)
    early, late = (first, second) if backward else (second, first)
    below = (early >> 7) < (late >> 7)
    gap = jnp.where((early >> 7) == (late >> 7), early - late, 512)
    gap = jnp.where(below, -512, gap)
    masks = []
    for o in order:
        ahead = o > order[0] if backward else o < order[0]
        lead = jnp.where(ahead, 128, jnp.where(o == order[0], 0, -128))
        masks.append((gap <= lead).astype(F32).astype(BF))
    return masks


def cand_attend(count, begin, end, *refs):
    q_ref, kvs, rest = refs[0], refs[1 : 1 + count], refs[1 + count :]
    q = q_ref[...].reshape(16 * CAP, HS)
    total = None if begin else rest[0][...]
    for block in kvs:
        half = dot(q, block[:, :HS], NT).astype(BF)
        probs = half + half * jnp.tanh(half)
        more = dot(probs, block[:, HS : 2 * HS])
        total = more if total is None else total + more
    if end:
        rest[-1][...] = total.astype(BF).reshape(16, CAP, HS)
    else:
        rest[-1][...] = total


def attend_rows(q_ref, blocks, masks, old_ref, att_ref):
    for y in range(2):
        rows = slice(y * 256, (y + 1) * 256)
        q = q_ref[rows, 2 * HS :]
        total = None if old_ref is None else old_ref[rows, :]
        for block, mask in zip(blocks, masks):
            half = dot(q, block[: 256 * (y + 1), :HS], NT).astype(BF)
            probs = half + half * jnp.tanh(half)
            last = probs[:, 256 * y :] * mask
            probs = last if y == 0 else jnp.concatenate([probs[:, : 256 * y], last], axis=1)
            more = dot(probs, block[: 256 * (y + 1), HS : 2 * HS])
            total = more if total is None else total + more
        att_ref[rows, :] = total


def hist_begin(info, *refs):
    attend_rows(refs[0], refs[:6], corner_masks(info, False)[:6], None, refs[6])


def hist_end(info, p0, p1, p2, p3, own_ref, b0, b1, old_ref, att_ref, stat_ref, g_ref):
    for k, part in enumerate((p0, p1, p2, p3)):
        rows = pl.ds(pl.multiple_of(((info[2] - k) & 3) * 128, 128), 128)
        g_ref[rows, :] = part[:, 3 * HS :].astype(F32)
    attend_rows(own_ref, (b0, b1), corner_masks(info, False)[6:], old_ref, att_ref)
    att = att_ref[...]
    g = g_ref[...]
    mean = jnp.mean(att, axis=1, keepdims=True)
    center = att - mean
    lane = lax.broadcasted_iota(jnp.int32, (512, 128), 1)
    stats = jnp.where(lane == 0, mean, 0.0)
    stats = jnp.where(lane == 1, jnp.sum(center * center, axis=1, keepdims=True), stats)
    stats = jnp.where(lane == 2, jnp.sum(g, axis=1, keepdims=True), stats)
    stats = jnp.where(lane == 3, jnp.sum(g * center, axis=1, keepdims=True), stats)
    stat_ref[...] = jnp.transpose(stats)[:8]


def normed_grads(info, p0, p1, p2, p3, att_ref, s0, s1, s2, s3, ga_ref, normed_ref, g_ref):
    for k, part in enumerate((p0, p1, p2, p3)):
        y = (info[2] - k) & 3
        rows = pl.ds(pl.multiple_of(y * 128, 128), 128)
        g_ref[rows, :] = part[:, 3 * HS :].astype(F32)
    stats = [s[...] for s in (s0, s1, s2, s3)]
    mean = sum(s[0:1] for s in stats) * 0.25
    squares = sum(s[1:2] + HS * (s[0:1] - mean) * (s[0:1] - mean) for s in stats)
    spread = lax.rsqrt(squares * (1.0 / (HEADS * HS)) + EPS)
    g_mean = sum(s[2:3] for s in stats) * (1.0 / (HEADS * HS))
    ga_sum = sum(s[3:4] + s[2:3] * (s[0:1] - mean) for s in stats)
    ga_mean = ga_sum * spread * (1.0 / (HEADS * HS))
    line = lax.broadcasted_iota(jnp.int32, (128, 512), 0)
    packed = jnp.where(line == 0, mean, 0.0)
    packed = jnp.where(line == 1, spread, packed)
    packed = jnp.where(line == 2, g_mean, packed)
    packed = jnp.where(line == 3, ga_mean, packed)
    cols = jnp.transpose(packed)
    spread_c = cols[:, 1:2]
    normed = (att_ref[...] - cols[:, 0:1]) * spread_c
    ga_ref[...] = (spread_c * (g_ref[...] - cols[:, 2:3] - normed * cols[:, 3:4])).astype(BF)
    normed_ref[...] = normed.astype(BF)


def slope_times(half, grads):
    t = jnp.tanh(half)
    up = 1.0 + t
    probs = half * up
    return probs, grads * (up + probs * (1.0 - t))


def hist_dq(info, ga_ref, *refs):
    blocks, dq_ref = refs[:8], refs[8]
    masks = corner_masks(info, False)
    for y in range(2):
        q = blocks[0][y * 256 : (y + 1) * 256, 2 * HS :]
        ga = ga_ref[y * 256 : (y + 1) * 256, :]
        total = None
        for block, mask in zip(blocks, masks):
            key = block[: 256 * (y + 1), :HS]
            half = dot(q, key, NT).astype(BF)
            _, ds = slope_times(half, dot(ga, block[: 256 * (y + 1), HS : 2 * HS], NT).astype(BF))
            last = ds[:, 256 * y :] * mask
            ds = last if y == 0 else jnp.concatenate([ds[:, : 256 * y], last], axis=1)
            more = dot(ds, key)
            total = more if total is None else total + more
        dq_ref[2 * y : 2 * y + 2] = (total * (0.5 * SCALE)).astype(BF).reshape(2, 128, HS)


def key_grads(own_ref, blocks, gas, masks, y, dk, dv):
    key = own_ref[y * 256 : (y + 1) * 256, :HS]
    value = own_ref[y * 256 : (y + 1) * 256, HS : 2 * HS]
    for block, ga_block, mask in zip(blocks, gas, masks):
        q = block[256 * y :, 2 * HS :]
        ga = ga_block[256 * y :, :]
        half = dot(key, q, NT).astype(BF)
        probs, ds = slope_times(half, dot(value, ga, NT).astype(BF))
        p_first = probs[:, :256] * mask
        d_first = ds[:, :256] * mask
        if y < 1:
            probs = jnp.concatenate([p_first, probs[:, 256:]], axis=1)
            ds = jnp.concatenate([d_first, ds[:, 256:]], axis=1)
        else:
            probs, ds = p_first, d_first
        more_k = dot(ds, q)
        more_v = dot(probs, ga)
        dk = more_k if dk is None else dk + more_k
        dv = more_v if dv is None else dv + more_v
    return dk, dv


def hist_dkv_begin(info, *refs):
    masks = corner_masks(info, True)[:6]
    for y in range(2):
        dk, dv = key_grads(refs[0], refs[:6], refs[6:12], masks, y, None, None)
        refs[12][y, :, :HS] = dk
        refs[12][y, :, HS:] = dv


def hist_dkv_end(info, dq_ref, normed_ref, own_ref, b0, b1, g0, g1, old_ref, k0, k1, k2, k3, all_ref):
    masks = corner_masks(info, True)[6:]
    for y in range(2):
        dk, dv = key_grads(own_ref, (b0, b1), (g0, g1), masks, y, old_ref[y, :, :HS], old_ref[y, :, HS:])
        all_ref[2 * y : 2 * y + 2, :, HS : 2 * HS] = dk.astype(BF).reshape(2, 128, HS)
        all_ref[2 * y : 2 * y + 2, :, 2 * HS : 3 * HS] = dv.astype(BF).reshape(2, 128, HS)
    for y in range(4):
        all_ref[y, :, :HS] = dq_ref[y]
        all_ref[y, :, 3 * HS :] = normed_ref[y * 128 : (y + 1) * 128, :]
    for k, out in enumerate((k0, k1, k2, k3)):
        out[...] = all_ref[(info[2] + k) & 3]


def hist_close(
    info, x_ref, cot_ref, slope_ref, wo_ref, buf, gate_ref, gm_ref, b0, b1, b2, b3, out_far, grad_far,
    mixed_ref, hid_ref, out_ref, grad_ref, few,
):
    length = jnp.full((128, 1), info[0], jnp.int32).astype(F32)
    for k, b in enumerate((b0, b1, b2, b3)):
        lanes = pl.ds(pl.multiple_of(((info[2] - k) & 3) * HS, HS), HS)

        def put(part, grads, which):
            hid_ref[part, :, lanes] = (grads * slope_ref[which, :, lanes].astype(F32)).astype(BF)

        normed = b[:, 3 * HS :].astype(F32)
        put(0, normed * gm_ref[:, lanes].astype(F32), 3)
        put(1, b[:, 2 * HS : 3 * HS].astype(F32) / length, 1)
        put(2, b[:, :HS].astype(F32), 2)
        put(3, b[:, HS : 2 * HS].astype(F32), 0)
        mixed_ref[:, lanes] = (normed * gate_ref[:, lanes].astype(F32)).astype(BF)
    x = x_ref[...].astype(F32)
    out_ref[...] = (x + dot(mixed_ref[...], wo_ref[...])).astype(BF)
    done = fetched([(out_ref, out_far.at[0])], few)
    e = None
    for part in range(4):
        more = dot(hid_ref[part], buf[part], NT)
        e = more if e is None else e + more
    normed, spread = normalize(x)
    back = spread * (
        e - jnp.mean(e, axis=-1, keepdims=True) - normed * jnp.mean(e * normed, axis=-1, keepdims=True)
    )
    grad_ref[...] = (cot_ref[...].astype(F32) + back).astype(BF)
    done += fetched([(grad_ref, grad_far.at[0])], few.at[pl.ds(1, 1)])
    for copy in done:
        copy.wait()


def cand_close(
    ids_ref, gate_far, ret_ref, x_far, wo_far, w_far, hx_far, cot_far, out_ref, wo_ref, buf, hx_ref, cot_ref,
    gate_ref, x_ref, few, sems,
):
    copies = fetched([(gate_far, gate_ref), (wo_far, wo_ref), (x_far, x_ref)], few)
    later = columns(w_far, buf, sems, (0, 1, 2, 3))
    later += fetched([(hx_far, hx_ref), (cot_far, cot_ref)], few.at[pl.ds(3, 2)])
    col, row, first, second = slot_ids(ids_ref)
    rank = jnp.sum(jnp.where((col == row) & (second < first), 1, 0), axis=1, keepdims=True)
    slot = col * CAP + rank
    hits = (lax.broadcasted_iota(jnp.int32, (256, 4 * CAP), 1) == slot).astype(F32).astype(BF)
    heads = []
    for h in range(HEADS):
        rows = jnp.concatenate([ret_ref[u * HEADS + h] for u in range(4)], axis=0)
        heads.append(dot(hits, rows))
    normed, _ = normalize(jnp.concatenate(heads, axis=1))
    copies[0].wait()
    mixed = (normed * gate_ref[...].astype(F32)).astype(BF)
    copies[1].wait()
    more = dot(mixed, wo_ref[...])
    copies[2].wait()
    out_ref[...] = (x_ref[...].astype(F32) + more).astype(BF)
    for copy in later:
        copy.wait()


def turned(value, axis, size, steps):
    return lax.ppermute(value, axis, [(i, (i + steps) % size) for i in range(size)])


def crossed(value, steps):
    pairs = []
    for c in range(2):
        for y in range(4):
            for xh in range(2):
                pairs.append(((c * 4 + y) * 2 + xh, (xh * 4 + (y + steps) % 4) * 2 + c))
    return lax.ppermute(value, ("c", "y", "xh"), pairs)


def across(value):
    return lax.ppermute(value, "c", [(0, 1), (1, 0)])


def along(value, way, cross):
    pairs = []
    for c in range(2):
        step = way if c == 0 else -way
        for z in range(4):
            pairs.append((4 * c + z, 4 * (c ^ cross) + (z + step) % 4))
    return lax.ppermute(value, ("c", "z"), pairs)


def per_device(hist_x, hist_cot, cand_x, cand_loop, hist_len, w_proj, w_out):
    y, xh, z, c = (lax.axis_index(n) for n in ("y", "xh", "z", "c"))
    x_rows = hist_x.reshape(128, 1024)
    cot = hist_cot.reshape(128, 1024)
    info = jnp.stack([hist_len[0], (y * 8 + xh * 4 + z) * 128, y, c, z]).astype(jnp.int32)
    held = pl.BlockSpec(memory_space=pltpu.VMEM)
    far = pl.BlockSpec(memory_space=pltpu.HBM)

    def weights(count):
        return [pltpu.VMEM((count, 1024, 512), BF), pltpu.SemaphoreType.DMA((count,))]

    def relayed(values, after):
        return call(nothing, "relay", (1,), [], [], [], [], 1_000, after, carry=values)()

    *sent, slope, gate, gm = call(
        project_all, "project_all", (1,), [SMEM, far, far, far, far],
        [shaped((128, 512))] * 4 + [shaped((4, 128, 512))] + [pltpu.HBM((128, 512), BF)] * 2,
        [held] * 5 + [far] * 2,
        [
            pltpu.VMEM((128, 512), BF), pltpu.VMEM((128, 512), BF),
            pltpu.VMEM((128, 1024), BF), pltpu.VMEM((128, 512), BF), pltpu.VMEM((128, 1024), BF),
            pltpu.VMEM((128, 1024), BF), pltpu.VMEM((512, 1024), BF), pltpu.SemaphoreType.DMA((5,)),
        ] + weights(4), 700_000_000, (), 16,
    )(info, x_rows, cot, w_out, w_proj)
    parts = [crossed(v, k) for k, v in enumerate(sent)]

    sent_cand, cand_gate = call(
        project_cand, "project_cand", (1,), [held, held, far],
        [shaped((16, 128, 128)), shaped((256, 512))], [held] * 2,
        [pltpu.VMEM((256, 1024), BF)] + weights(2), 700_000_000, (slope,),
    )(cand_loop, cand_x, w_proj)

    own, sent_cand = call(
        arrange, "arrange", (1,), [SMEM] + [held] * 4, shaped((4, 128, 384)), held, [], 1_000_000,
        (cand_gate,), carry=(sent_cand,),
    )(info, *parts)
    own = own.reshape(512, 384)
    own_pair = across(own)
    plus, minus = along(own, 1, 0), along(own, -1, 0)
    arrived = lax.all_to_all(sent_cand, ("xl", "xh", "y"), 0, 0, tiled=True)
    last = [along(plus, 1, 0), along(plus, 1, 1)]
    kvq = [own, own_pair, plus, across(plus), minus, across(minus)]

    q_spec = held
    acc_spec = held

    def cand_part(kvs, total, end, after):
        begin = total is None
        return call(
            functools.partial(cand_attend, len(kvs), begin, end), "cand_attend", (1,),
            [q_spec] + [held] * len(kvs) + ([] if begin else [acc_spec]),
            shaped((16, 128, 128)) if end else shaped((2048, 128), F32),
            q_spec if end else acc_spec, [], 600_000_000 * len(kvs), after, 20,
        )(arrived, *kvs, *([] if begin else [total]))

    att = call(
        hist_begin, "hist_begin", (1,), [SMEM] + [held] * 6,
        shaped((512, 128), F32), held, [], 1_000,
    )(info, *kvq)
    total = cand_part(kvq, None, False, (att,))
    att, stats = call(
        hist_end, "hist_end", (1,), [SMEM] + [held] * 8,
        [shaped((512, 128), F32), shaped((8, 512), F32)], [held] * 2,
        [pltpu.VMEM((512, 128), F32)], 400_000_000, (total,),
    )(info, *parts, own, *last, att)
    all_stats = [stats] + [turned(stats, "y", 4, k) for k in (1, 2, 3)]
    weighed = cand_part(last, total, True, (stats,))
    ga, normed = call(
        normed_grads, "normed_grads", (1,), [SMEM] + [held] * 9,
        [shaped((512, 128))] * 2, [held] * 2,
        [pltpu.VMEM((512, 128), F32)], 1_000_000, (weighed,),
    )(info, *parts, att, *all_stats)

    ga_plus, ga_minus = along(ga, 1, 0), along(ga, -1, 0)
    dq = call(
        hist_dq, "hist_dq", (1,), [SMEM] + [held] * 9,
        shaped((4, 128, 128)), held, [], 2_000_000_000,
    )(info, ga, *kvq, *last)
    ga_plus, ga_minus = relayed([ga_plus, ga_minus], (dq,))
    ga_last = [along(ga_plus, 1, 0), along(ga_plus, 1, 1)]
    gas = [ga, across(ga), ga_plus, across(ga_plus), ga_minus, across(ga_minus)]
    key_sums = call(
        hist_dkv_begin, "hist_dkv_begin", (1,), [SMEM] + [held] * 12,
        shaped((2, 256, 256), F32), held, [], 2_000_000_000,
    )(info, *kvq, *gas)
    (leaving,) = relayed([weighed], (key_sums, *ga_last))
    returned = lax.all_to_all(leaving, ("xl", "xh", "y"), 0, 0, tiled=True)
    grads = call(
        hist_dkv_end, "hist_dkv_end", (1,), [SMEM] + [held] * 8,
        [shaped((128, 512))] * 4, [held] * 4, [pltpu.VMEM((4, 128, 512), BF)], 800_000_000,
    )(info, dq, normed, own, *last, *ga_last, key_sums)
    back = [crossed(v, k) for k, v in enumerate(grads)]

    cand_out, wo_near, w_near, x_near, cot_near = call(
        cand_close, "cand_close", (1,), [held, far, held] + [far] * 5,
        [pltpu.HBM((256, 1024), BF), shaped((512, 1024)), shaped((4, 1024, 512))] + [shaped((128, 1024))] * 2,
        [pl.BlockSpec((256, 1024), lambda i: (0, 0))] + [held] * 4,
        [
            pltpu.VMEM((256, 512), BF), pltpu.VMEM((256, 1024), BF),
            pltpu.SemaphoreType.DMA((5,)), pltpu.SemaphoreType.DMA((4,)),
        ], 400_000_000, (grads[0],),
    )(cand_loop, cand_gate, returned, cand_x, w_out, w_proj, x_rows, cot)
    final = pltpu.HBM((1, 128, 1024), BF)
    hist_out, hist_grad = call(
        hist_close, "hist_close", (1,), [SMEM] + [held] * 11,
        [final] * 2, [far] * 2,
        [
            pltpu.VMEM((128, 512), BF), pltpu.VMEM((4, 128, 512), BF), pltpu.VMEM((128, 1024), BF),
            pltpu.VMEM((128, 1024), BF), pltpu.SemaphoreType.DMA((2,)),
        ], 700_000_000,
    )(info, x_near, cot_near, slope, wo_near, w_near, gate, gm, *back)
    return hist_out, hist_grad, cand_out


def solution(mesh):
    split = Mesh(mesh.devices.reshape(2, 2, 4, 2, 4), ("xl", "c", "y", "xh", "z"))
    users, rows = ("xl", "c"), ("y", "xh", "z")
    hist = P(users, rows, None)
    cand = P(users + rows, None)
    return jax.shard_map(
        per_device,
        mesh=split,
        in_specs=(hist, hist, cand, cand, P(users), P(), P()),
        out_specs=(hist, hist, cand),
        check_vma=False,
    )
```
